32 devices in a mesh: dp: 8 (over z, x), tensor: 4 (over y, core).
Axes of the slice: x: 2, y: 2, z: 4, core: 2. Of those that a mesh axis runs over, the one named last changes fastest.
Arguments:
- tokens: bfloat16 [32768, 1024], P(('dp', 'tensor')), may hold values from -6 to 6
- doc_starts: int32 [16, 4], P('dp'), may hold values from 0 to 2047, as said below
- norm_gains: bfloat16 [2, 2, 1024], replicated, may hold values from 0.5 to 1.5
- norm_shifts: bfloat16 [2, 2, 1024], replicated, may hold values from -1.1953125 to 1.1953125
- qkv_weight: bfloat16 [2, 1024, 3072], P(None, None, 'tensor'), may hold values from -0.1875 to 0.1875
- qkv_bias: bfloat16 [2, 3072], P(None, 'tensor'), may hold values from -1.796875 to 1.796875
- dense_weight: bfloat16 [2, 1024, 1024], P(None, 'tensor'), may hold values from -1.5 to 1.5
- dense_bias: bfloat16 [2, 1024], replicated, may hold values from -1.796875 to 1.796875
- up_weight: bfloat16 [2, 1024, 4096], P(None, None, 'tensor'), may hold values from -0.1875 to 0.1875
- up_bias: bfloat16 [2, 4096], P(None, 'tensor'), may hold values from -3 to 3
- down_weight: bfloat16 [2, 4096, 1024], P(None, 'tensor'), may hold values from -0.09375 to 0.09375
- down_bias: bfloat16 [2, 1024], replicated, may hold values from -1.796875 to 1.796875
- out_grad: bfloat16 [32768, 1024], P(('dp', 'tensor')), may hold values from -6 to 6
Outputs:
- out: bfloat16 [32768, 1024], P(('dp', 'tensor'))
- tokens_grad: float32 [32768, 1024], P(('dp', 'tensor'))
- norm_gains_grad: float32 [2, 2, 1024], replicated
- norm_shifts_grad: float32 [2, 2, 1024], replicated
- qkv_weight_grad: float32 [2, 1024, 3072], P(None, None, 'tensor')
- qkv_bias_grad: float32 [2, 3072], P(None, 'tensor')
- dense_weight_grad: float32 [2, 1024, 1024], P(None, 'tensor')
- dense_bias_grad: float32 [2, 1024], replicated
- up_weight_grad: float32 [2, 1024, 4096], P(None, None, 'tensor')
- up_bias_grad: float32 [2, 4096], P(None, 'tensor')
- down_weight_grad: float32 [2, 4096, 1024], P(None, 'tensor')
- down_bias_grad: float32 [2, 1024], replicated
The draws below stay inside these ranges and needn't reach their ends.
Inputs may be any that keep to these rules, and one draw needn't show every extreme that they name: `doc_starts`: each row holds the document starts of one packed sequence: the first is 0 and they never fall (equal starts leave empty documents). In each aligned block of 2 rows one row has its second start below 128, its last start at 2047 and the others from 1920 on; the other row's last start is 2047.
All inputs are finite; a program needn't handle non-finite values.
Results may differ from the reference program's by a relative error of at most 0.019.
Values may be sent and summed in bfloat16 or wider, within the bound.
No kernel may reach another device: no remote copies, remote signals or barrier semaphores. Data moves between devices by JAX's collectives and lax.ppermute only.
A program may use at most 448 MiB of HBM per device.

```python
import math
from functools import partial
import jax
import jax.numpy as jnp
from jax import lax

D = 1024
HS = 64
FF = 4096
FEATS = 64
ROT = 16
BLOCK = 64
LEN = 2048
NDOC = 4
LAYERS = 2
SEQS = 2
SEQ_ALL = 16
TOKENS = 32768


def draw_doc_starts(key, part):
    key = jax.random.fold_in(key, 7)
    groups = SEQ_ALL // SEQS
    cut_points = jax.random.randint(jax.random.fold_in(key, 1), (SEQ_ALL, NDOC - 1), 1, LEN)
    cut_points = jnp.sort(cut_points, axis=1)
    starts = jnp.concatenate([jnp.zeros((SEQ_ALL, 1), jnp.int32), cut_points.astype(jnp.int32)], axis=1)
    early_cut = jax.random.randint(jax.random.fold_in(key, 3), (SEQ_ALL, 1), 1, max(2, LEN // 16))
    late_cuts = jax.random.randint(jax.random.fold_in(key, 4), (SEQ_ALL, NDOC), LEN - LEN // 16, LEN - 1)
    late_cuts = jnp.sort(late_cuts, axis=1)
    columns = jnp.arange(NDOC)[None, :]
    spanning = jnp.where(columns == 0, 0, jnp.where(columns == 1, early_cut, jnp.where(columns == NDOC - 1, LEN - 1, late_cuts)))
    chosen = jax.random.randint(jax.random.fold_in(key, 2), (groups, 1), 0, SEQS)
    seq_index = jnp.arange(SEQS)[None, :]
    single = (seq_index == chosen).reshape(SEQ_ALL, 1)
    ending = ((seq_index == (chosen + 1) % SEQS) & (seq_index != chosen)).reshape(SEQ_ALL, 1)
    last_col = columns == NDOC - 1
    starts = jnp.where(ending & last_col, LEN - 1, starts)
    return jnp.where(single, spanning, starts).astype(jnp.int32)


def steps_of(own_key, extent, shards, low, top_value):
    loudness, own = 1.0, jax.random.fold_in(own_key, 6)
    for position, parts in shards:
        steps = jnp.exp(jax.random.uniform(jax.random.fold_in(own, position), (parts,), jnp.float32, low / len(shards), top_value / len(shards)))
        loudness = loudness * jnp.repeat(steps, extent[position] // parts).reshape([-1 if axis == position else 1 for axis in range(len(extent))])
    return loudness


def normal_values(stream_key, extent, deviation, most, split=(), held_as=jnp.bfloat16):
    loudness = steps_of(stream_key, extent, split, -0.22, 0.18) if split else 1.0
    array = jax.random.normal(stream_key, extent, jnp.float32) * deviation * loudness
    return jnp.minimum(jnp.maximum(array, -most), most).astype(held_as)


def setup_inputs(seed: int = 0) -> dict:
    seeds = jax.random.split(jax.random.key(seed), 14)
    return {
        "tokens": normal_values(seeds[0], (TOKENS, D), 1.0, 6.0, ((0, 32),)),
        "doc_starts": draw_doc_starts(jax.random.fold_in(seeds[13], 71), 0),
        "norm_gains": jnp.clip(1.0 + 0.1 * jax.random.normal(seeds[2], (LAYERS, 2, D), jnp.float32), 0.5, 1.5).astype(jnp.bfloat16),
        "norm_shifts": normal_values(seeds[3], (LAYERS, 2, D), 0.2, 1.1953125),
        "qkv_weight": normal_values(seeds[4], (LAYERS, D, 3 * D), D ** -0.5, 0.1875, ((2, 4),)),
        "qkv_bias": normal_values(seeds[5], (LAYERS, 3 * D), 0.3, 1.796875, ((1, 4),)),
        "dense_weight": normal_values(seeds[6], (LAYERS, D, D), (D // 64) ** -0.5, 1.5, ((1, 4),)),
        "dense_bias": normal_values(seeds[7], (LAYERS, D), 0.3, 1.796875),
        "up_weight": normal_values(seeds[8], (LAYERS, D, FF), D ** -0.5, 0.1875, ((2, 4),)),
        "up_bias": normal_values(seeds[9], (LAYERS, FF), 0.5, 3.0, ((1, 4),)),
        "down_weight": normal_values(seeds[10], (LAYERS, FF, D), FF ** -0.5, 0.09375, ((1, 4),)),
        "down_bias": normal_values(seeds[11], (LAYERS, D), 0.3, 1.796875),
        "out_grad": normal_values(seeds[12], (TOKENS, D), 1.0, 6.0, ((0, 32),)),
    }


norm_eps = 1e-05
feature_scale = 0.75
rotary_base = 10000.0
highest = lax.Precision.HIGHEST

@jax.custom_vjp
def low(v):
    return lax.optimization_barrier(v.astype(jnp.bfloat16)).astype(jnp.float32)

@jax.custom_vjp
def low_back(v):
    return v

def low_keep(v):
    return (low(v), None)

def low_pass(kept, grad):
    return (grad,)

def back_keep(v):
    return (v, None)

def back_low(kept, grad):
    return (low(grad),)
low.defvjp(low_keep, low_pass)
low_back.defvjp(back_keep, back_low)

def both_low(operand):
    return low_back(low(operand))

def normalize(matrix, scaling, offset):
    center = lax.optimization_barrier(jnp.mean(matrix, axis=-1, keepdims=True))
    shifted = matrix - center
    spread = lax.optimization_barrier(jnp.mean(shifted * shifted, axis=-1, keepdims=True))
    return shifted * lax.rsqrt(spread + norm_eps) * scaling + offset

def dct_rows(feature_count, head_width):
    row_index = jnp.arange(feature_count, dtype=jnp.float32)[:, None]
    col_index = jnp.arange(head_width, dtype=jnp.float32)[None, :]
    table = jnp.cos(math.pi * (col_index + 0.5) * row_index / head_width) * math.sqrt(2.0 / head_width)
    return table * jnp.where(row_index == 0, math.sqrt(0.5), 1.0)

def doc_layout(starts, length):
    places = jnp.arange(length, dtype=jnp.int32)
    started = starts[:, None, :] <= places[None, :, None]
    doc_ids = lax.optimization_barrier(jnp.sum(started.astype(jnp.int32), axis=-1))
    latest = lax.optimization_barrier(jnp.max(jnp.where(started, starts[:, None, :], 0), axis=-1))
    return (doc_ids, places[None, :] - latest)

def rotary_tables(offsets, rotary_dims):
    halfway = rotary_dims // 2
    inverse = rotary_base ** (-(jnp.arange(halfway, dtype=jnp.float32) * 2.0 / rotary_dims))
    angles = offsets.astype(jnp.float32)[..., None] * inverse
    return (jnp.cos(angles), jnp.sin(angles))

def rotate(vectors, cosine, sine_table, rotary_dims):
    halfway = rotary_dims // 2
    leading = vectors[..., :halfway]
    trailing = vectors[..., halfway:rotary_dims]
    return jnp.concatenate([leading * cosine - trailing * sine_table, trailing * cosine + leading * sine_table, vectors[..., rotary_dims:]], axis=-1)

def attend_head(queries, keys_in, values_in, cosine, sine_table, doc_ids, dct_table, block_size, rotary_dims):
    length = queries.shape[0]
    blocks = length // block_size
    turned_q = rotate(queries, cosine, sine_table, rotary_dims)
    turned_k = rotate(keys_in, cosine, sine_table, rotary_dims)
    query_feat = low(jnp.exp(feature_scale * jnp.dot(turned_q, dct_table.T, precision=highest)))
    key_feat = low(jnp.exp(feature_scale * jnp.dot(turned_k, dct_table.T, precision=highest)))
    value_low = low(values_in)
    query_blocks = query_feat.reshape(blocks, block_size, -1)
    key_blocks = key_feat.reshape(blocks, block_size, -1)
    value_blocks = value_low.reshape(blocks, block_size, -1)
    doc_blocks = doc_ids.reshape(blocks, block_size)
    lead_doc = doc_blocks[:, 0]
    next_doc = jnp.concatenate([lead_doc[1:], jnp.full((1,), -1, jnp.int32)])
    carried = (doc_blocks == lead_doc[:, None]).astype(jnp.float32)
    feeding = (doc_blocks == next_doc[:, None]).astype(jnp.float32)
    keeping = (next_doc == lead_doc).astype(jnp.float32)
    places = jnp.arange(block_size)
    causal = places[:, None] >= places[None, :]
    allowed = (causal[None] & (doc_blocks[:, :, None] == doc_blocks[:, None, :])).astype(jnp.float32)
    scores = jnp.einsum('bcm,bdm->bcd', query_blocks, key_blocks, precision=highest) * allowed
    inner_den = lax.optimization_barrier(jnp.sum(scores, axis=-1))
    inner_num = jnp.einsum('bcd,bde->bce', both_low(scores), value_blocks, precision=highest)
    fed_keys = key_blocks * feeding[..., None]
    state_add = jnp.einsum('bcm,bce->bme', fed_keys, value_blocks, precision=highest)
    total_add = lax.optimization_barrier(jnp.sum(fed_keys, axis=1))

    def advance(carried_in, pieces):
        state_now, total_now = carried_in
        state_more, total_more, kept_share = pieces
        return ((kept_share * state_now + state_more, kept_share * total_now + total_more), (state_now, total_now))
    start_state = (jnp.zeros(state_add.shape[1:], jnp.float32), jnp.zeros(total_add.shape[1:], jnp.float32))
    _, (states, totals) = lax.scan(advance, start_state, (state_add, total_add, keeping))
    outer_num = jnp.einsum('bcm,bme->bce', query_blocks, both_low(states), precision=highest) * carried[..., None]
    outer_den = jnp.einsum('bcm,bm->bc', query_blocks, totals, precision=highest) * carried
    numerator = (inner_num + outer_num).reshape(length, -1)
    denominator = (inner_den + outer_den).reshape(length, 1)
    return low_back(numerator) / denominator

def attend_all(mixed, cosine, sine_table, doc_ids, dct_table, seq_count, head_size, block_size, rotary_dims):
    length = mixed.shape[0] // seq_count
    packed = mixed.reshape(seq_count, length, -1, 3, head_size)
    per_head = partial(attend_head, dct_table=dct_table, block_size=block_size, rotary_dims=rotary_dims)
    over_heads = jax.vmap(per_head, in_axes=(1, 1, 1, None, None, None), out_axes=1)
    over_seqs = jax.vmap(over_heads)
    context = over_seqs(packed[:, :, :, 0], packed[:, :, :, 1], packed[:, :, :, 2], cosine, sine_table, doc_ids)
    return context.reshape(seq_count * length, -1)

def forward(residual, weights, cosine, sine_table, doc_ids, dct_table):
    gains, shifts, qkv_weight, qkv_bias, dense_weight, dense_bias, up_weight, up_bias, down_weight, down_bias = weights
    for layer_index in range(LAYERS):
        normed_one = low(normalize(residual, gains[layer_index, 0], shifts[layer_index, 0]))
        normed_two = low(normalize(residual, gains[layer_index, 1], shifts[layer_index, 1]))
        mixed = low_back(jnp.dot(normed_one, qkv_weight[layer_index], precision=highest, preferred_element_type=jnp.float32) + qkv_bias[layer_index])
        context = low(attend_all(mixed, cosine, sine_table, doc_ids, dct_table, SEQS, HS, BLOCK, ROT))
        hidden = low_back(jnp.dot(normed_two, up_weight[layer_index], precision=highest, preferred_element_type=jnp.float32) + up_bias[layer_index])
        active = low(jax.nn.gelu(hidden, approximate=False))
        branch = low_back(jnp.dot(context, dense_weight[layer_index], precision=highest, preferred_element_type=jnp.float32) + jnp.dot(active, down_weight[layer_index], precision=highest, preferred_element_type=jnp.float32) + dense_bias[layer_index] + down_bias[layer_index])
        residual = residual + branch
        if layer_index + 1 < LAYERS:
            residual = low(residual)
    return residual

def reference(tokens, doc_starts, norm_gains, norm_shifts, qkv_weight, qkv_bias, dense_weight, dense_bias, up_weight, up_bias, down_weight, down_bias, out_grad):
    params = (norm_gains.astype(jnp.float32), norm_shifts.astype(jnp.float32), qkv_weight.astype(jnp.float32), qkv_bias.astype(jnp.float32), dense_weight.astype(jnp.float32), dense_bias.astype(jnp.float32), up_weight.astype(jnp.float32), up_bias.astype(jnp.float32), down_weight.astype(jnp.float32), down_bias.astype(jnp.float32))
    groups = SEQ_ALL // SEQS
    dct_table = dct_rows(FEATS, HS)
    rows_in = tokens.astype(jnp.float32).reshape(groups, SEQS * LEN, D)
    starts_in = doc_starts.reshape(groups, SEQS, NDOC)
    grads_in = out_grad.astype(jnp.float32).reshape(groups, SEQS * LEN, D)

    def one_group(totals, pieces):
        rows_now, starts_now, grad_now = pieces
        doc_ids, offsets = doc_layout(starts_now, LEN)
        cosine, sine_table = rotary_tables(offsets, ROT)

        def forward_rows(matrix, weights):
            return forward(matrix, weights, cosine, sine_table, doc_ids, dct_table)
        result, pull_back = jax.vjp(forward_rows, rows_now, params)
        rows_grad, weight_grads = pull_back(grad_now)
        totals = jax.tree.map(jnp.add, totals, weight_grads)
        return (totals, (result.astype(jnp.bfloat16), rows_grad))
    zero_grads = jax.tree.map(jnp.zeros_like, params)
    totals, (outputs, input_grads) = lax.scan(one_group, zero_grads, (rows_in, starts_in, grads_in))
    gains_grad, shifts_grad, qkv_weight_grad, qkv_bias_grad, dense_weight_grad, dense_bias_grad, up_weight_grad, up_bias_grad, down_weight_grad, down_bias_grad = totals
    return (outputs.reshape(SEQ_ALL * LEN, D), input_grads.reshape(SEQ_ALL * LEN, D), gains_grad, shifts_grad, qkv_weight_grad, qkv_bias_grad, dense_weight_grad, dense_bias_grad, up_weight_grad, up_bias_grad, down_weight_grad, down_bias_grad)
```

```python
from functools import partial
import math

import numpy as np
import jax
import jax.numpy as jnp
from jax import lax
from jax.experimental import pallas as pl
from jax.experimental.pallas import tpu as pltpu
from jax.sharding import PartitionSpec as P

HS = 64
FEATS = 64
ROT = 16
PAIR = 2 * HS
SUB = 128

norm_eps = 1e-05
feature_scale = 0.75
rotary_base = 10000.0

f32 = jnp.float32
bf16 = jnp.bfloat16
NT = (((1,), (1,)), ((), ()))
TN = (((0,), (0,)), ((), ()))


def pair_order():
    half = ROT // 2
    rest = (HS - ROT) // 2
    order = []
    for side in range(2):
        for head in range(2):
            order += [(head, side * half + i) for i in range(half)]
        for head in range(2):
            order += [(head, ROT + side * rest + i) for i in range(rest)]
    return order


def column_order(heads):
    padded = heads + heads % 2
    width = padded * HS
    matrix = np.zeros((heads * 3 * HS, 3 * width), np.float32)
    order = pair_order()
    for pair in range(padded // 2):
        for lane, (side, entry) in enumerate(order):
            head = 2 * pair + side
            if head < heads:
                for part in range(2):
                    matrix[head * 3 * HS + part * HS + entry, part * width + pair * PAIR + lane] = 1
    for head in range(heads):
        for entry in range(HS):
            matrix[head * 3 * HS + 2 * HS + entry, 2 * width + head * HS + entry] = 1
    return matrix


def feature_matrix(group):
    rows = np.arange(FEATS)[:, None]
    cols = np.arange(HS)[None, :]
    table = np.cos(np.pi * (cols + 0.5) * rows / HS) * np.sqrt(2.0 / HS)
    table = table * np.where(rows == 0, np.sqrt(0.5), 1.0) * feature_scale
    matrix = np.zeros((group, group), np.float32)
    for pair in range(group // PAIR):
        for lane, (side, entry) in enumerate(pair_order()):
            start = pair * PAIR + side * FEATS
            matrix[pair * PAIR + lane, start : start + FEATS] = table[:, entry]
    return matrix


def lane_rates():
    half = ROT // 2
    rates = np.zeros((1, PAIR), np.float32)
    signs = np.zeros((1, PAIR), np.float32)
    for lane, (_, entry) in enumerate(pair_order()):
        if entry < ROT:
            rates[0, lane] = 1.0
            signs[0, lane] = -1.0 if entry < half else 1.0
    return rates, signs


def rotary_tables(starts, length):
    places = jnp.arange(length, dtype=jnp.int32)
    started = starts[:, None, :] <= places[None, :, None]
    latest = jnp.max(jnp.where(started, starts[:, None, :], 0), axis=-1)
    offsets = (places[None, :] - latest).reshape(-1, 1).astype(f32)
    half = ROT // 2
    rates, signs = lane_rates()
    powers = np.array([entry % half if entry < ROT else 0 for _, entry in pair_order()], np.float32)
    inverse = rotary_base ** (-(jnp.asarray(powers) * 2.0 / ROT)) * jnp.asarray(rates)
    angles = offsets * inverse.reshape(1, PAIR)
    return jnp.cos(angles), jnp.sin(angles) * jnp.asarray(signs)


def dot(a, b):
    return jnp.dot(a, b, preferred_element_type=f32)


def dot_nt(a, b):
    return lax.dot_general(a, b, NT, preferred_element_type=f32)


def latest_start(starts_ref, seq, count, places):
    latest = jnp.zeros_like(places)
    for j in range(count):
        start = starts_ref[seq, j]
        latest = jnp.maximum(latest, jnp.where(start <= places, start, 0))
    return latest


def latest_scalar(starts_ref, seq, count, place):
    latest = jnp.int32(0)
    for j in range(count):
        start = starts_ref[seq, j]
        latest = jnp.maximum(latest, jnp.where(start <= place, start, 0))
    return latest


def block_masks(starts_ref, seq, count, place):
    rows = place + lax.broadcasted_iota(jnp.int32, (SUB, SUB), 0)
    cols = place + lax.broadcasted_iota(jnp.int32, (SUB, SUB), 1)
    latest_rows = latest_start(starts_ref, seq, count, rows)
    allowed = (cols <= rows) & (cols >= latest_rows)
    carried = (latest_rows <= place).astype(f32)
    following = latest_scalar(starts_ref, seq, count, place + SUB)
    feeding = (rows >= following).astype(f32)
    keeping = jnp.where(following <= place, 1.0, 0.0).astype(f32)
    return rows, cols, allowed, carried, feeding, keeping


def halves(tile, low_lanes):
    zero = jnp.zeros_like(tile)
    return jnp.where(low_lanes, tile, zero), jnp.where(low_lanes, zero, tile)


def gelu_parts(hidden):
    size = jnp.abs(hidden)
    bell = jnp.exp(hidden * hidden * -0.5)
    t = 1.0 / (1.0 + (0.3275911 * math.sqrt(0.5)) * size)
    series = t * (
        0.5 * 0.254829592
        + t
        * (
            0.5 * -0.284496736
            + t * (0.5 * 1.421413741 + t * (0.5 * -1.453152027 + t * (0.5 * 1.061405429)))
        )
    )
    tail = series * bell
    share = jnp.where(hidden >= 0, 1.0 - tail, tail)
    return hidden * share, share + hidden * bell * (1.0 / math.sqrt(2.0 * math.pi))


def forward_kernel(
    width,
    count,
    blocks_per_seq,
    first_place,
    starts_ref,
    x_ref,
    wf_ref,
    bf_ref,
    wo_ref,
    dct_ref,
    cos_ref,
    sin_ref,
    state_in_ref,
    xh_ref,
    qkv_ref,
    ca_ref,
    rden_ref,
    gp_ref,
    states_ref,
    out_ref,
    state_ref,
):
    step = pl.program_id(0)
    seq = step // blocks_per_seq
    within = lax.rem(step, blocks_per_seq)
    rows = x_ref.shape[0]
    pairs = width // PAIR
    group = dct_ref.shape[0]

    @pl.when(within == 0)
    def _():
        state_ref[...] = state_in_ref[0]

    x = x_ref[...].astype(f32)
    center = jnp.mean(x, axis=-1, keepdims=True)
    shifted = x - center
    spread = jnp.mean(shifted * shifted, axis=-1, keepdims=True)
    xh = (shifted * lax.rsqrt(spread + norm_eps)).astype(bf16)
    xh_ref[...] = xh

    mixed = dot(xh, wf_ref[:, : 3 * width]) + bf_ref[:, : 3 * width]
    cosine = cos_ref[...]
    sine = sin_ref[...]
    dct = dct_ref[...]
    for part in range(2):
        for start in range(0, width, group):
            turned = []
            for lane in range(start, start + group, PAIR):
                tile = mixed[:, part * width + lane : part * width + lane + PAIR]
                turned.append(tile * cosine + pltpu.roll(tile, HS, 1) * sine)
            turned = turned[0] if len(turned) == 1 else jnp.concatenate(turned, axis=1)
            feats = jnp.exp(dot(turned.astype(bf16), dct)).astype(bf16)
            qkv_ref[:, part * width + start : part * width + start + group] = feats
    qkv_ref[:, 2 * width :] = mixed[:, 2 * width :].astype(bf16)

    hidden = dot(xh, wf_ref[:, 3 * width :]) + bf_ref[:, 3 * width :]
    active, slope = gelu_parts(hidden)
    ca_ref[:, width:] = active.astype(bf16)
    gp_ref[...] = slope.astype(bf16)

    low_lanes = lax.broadcasted_iota(jnp.int32, (SUB, PAIR), 1) < HS
    ones = jnp.ones((SUB, PAIR), bf16)
    for sub in range(rows // SUB):
        place = first_place + within * rows + sub * SUB
        _, _, allowed, carried, feeding, keeping = block_masks(starts_ref, seq, count, place)
        allowed2 = jnp.concatenate([allowed, allowed], axis=0)
        carried = carried.astype(bf16)
        feeding = feeding.astype(bf16)
        at = slice(sub * SUB, (sub + 1) * SUB)
        for pair in range(pairs):
            lanes = slice(pair * PAIR, (pair + 1) * PAIR)
            q = qkv_ref[at, pair * PAIR : (pair + 1) * PAIR]
            k = qkv_ref[at, width + pair * PAIR : width + (pair + 1) * PAIR]
            v = qkv_ref[at, 2 * width + pair * PAIR : 2 * width + (pair + 1) * PAIR]
            q0, q1 = halves(q, low_lanes)
            qs = jnp.concatenate([q0, q1], axis=0)
            weights = jnp.where(allowed2, dot_nt(qs, k), 0.0).astype(bf16)
            state = state_ref[pair * PAIR : (pair + 1) * PAIR, :]
            state_low = state.astype(bf16)
            first = (sub * pairs + pair) * PAIR
            states_ref[first : first + PAIR, :] = state_low
            qc = jnp.concatenate([q0 * carried, q1 * carried], axis=0)
            left = jnp.concatenate([weights, qc], axis=1)
            valued = jnp.concatenate([v, ones], axis=1)
            right = jnp.concatenate([valued, state_low], axis=0)
            both = dot(left, right)
            numerator = jnp.where(low_lanes, both[:SUB, :PAIR], both[SUB:, :PAIR])
            denominator = jnp.where(low_lanes, both[:SUB, PAIR:], both[SUB:, PAIR:])
            inverse = 1.0 / denominator
            ca_ref[at, lanes] = (numerator * inverse).astype(bf16)
            rden_ref[at, lanes] = inverse.astype(bf16)
            added = lax.dot_general(k * feeding, valued, TN, preferred_element_type=f32)
            state_ref[pair * PAIR : (pair + 1) * PAIR, :] = keeping * state + added

    out_ref[...] = dot(ca_ref[...], wo_ref[...]).astype(bf16)


def backward_kernel(
    width,
    count,
    blocks_per_seq,
    first_place,
    starts_ref,
    bg_ref,
    wot_ref,
    wft_ref,
    dctt_ref,
    cos_ref,
    sin_ref,
    state_in_ref,
    qkv_ref,
    ca_ref,
    rden_ref,
    gp_ref,
    states_ref,
    dz_ref,
    dx_ref,
    db_ref,
    state_ref,
    dqk_ref,
):
    step = pl.program_id(0)
    blocks = pl.num_programs(0)
    seq = (blocks - 1 - step) // blocks_per_seq
    within = lax.rem(blocks - 1 - step, blocks_per_seq)
    rows = bg_ref.shape[0]
    pairs = width // PAIR
    group = dctt_ref.shape[0]

    @pl.when(within == blocks_per_seq - 1)
    def _():
        state_ref[...] = state_in_ref[0]

    @pl.when(step == 0)
    def _():
        db_ref[...] = jnp.zeros_like(db_ref)

    bg = bg_ref[...]
    active_grad = dot(bg, wot_ref[:, width:])
    dz_ref[:, 3 * width :] = (active_grad * gp_ref[...].astype(f32)).astype(bf16)
    context_grad = dot(bg, wot_ref[:, :width])

    low_lanes = lax.broadcasted_iota(jnp.int32, (SUB, PAIR), 1) < HS
    ones = jnp.ones((SUB, PAIR), bf16)
    zeros = jnp.zeros((SUB, PAIR), bf16)
    scale = 1.0 / HS
    sum_rows = lax.broadcasted_iota(jnp.int32, (2 * PAIR, 2 * PAIR), 0)
    sum_cols = lax.broadcasted_iota(jnp.int32, (2 * PAIR, 2 * PAIR), 1)
    same_head = (lax.rem(sum_rows, PAIR) // HS) == (sum_cols // PAIR)
    summing = jnp.where(same_head, -scale, 0.0).astype(bf16)
    for sub in reversed(range(rows // SUB)):
        place = first_place + within * rows + sub * SUB
        rows_at, cols_at, allowed, carried, feeding, keeping = block_masks(
            starts_ref, seq, count, place
        )
        latest_cols = latest_start(starts_ref, seq, count, cols_at)
        flipped = (rows_at <= cols_at) & (rows_at >= latest_cols)
        allowed2 = jnp.concatenate([allowed, allowed], axis=0)
        flipped2 = jnp.concatenate([flipped, flipped], axis=0)
        carried2 = jnp.concatenate([carried, carried], axis=0)
        feeding2 = jnp.concatenate([feeding, feeding], axis=0)
        carried_low = carried.astype(bf16)
        at = slice(sub * SUB, (sub + 1) * SUB)
        for pair in range(pairs):
            lanes = slice(pair * PAIR, (pair + 1) * PAIR)
            q = qkv_ref[at, pair * PAIR : (pair + 1) * PAIR]
            k = qkv_ref[at, width + pair * PAIR : width + (pair + 1) * PAIR]
            v = qkv_ref[at, 2 * width + pair * PAIR : 2 * width + (pair + 1) * PAIR]
            first = (sub * pairs + pair) * PAIR
            state = states_ref[first : first + PAIR, :]
            later = state_ref[pair * PAIR : (pair + 1) * PAIR, :]
            later_low = later.astype(bf16)
            scaled = context_grad[at, lanes] * rden_ref[at, lanes].astype(f32)
            dnum = scaled.astype(bf16)
            product = scaled * ca_ref[at, lanes].astype(f32)
            product_high = product.astype(bf16)
            product_low = (product - product_high.astype(f32)).astype(bf16)
            dden = dot(jnp.concatenate([product_high, product_low], axis=1), summing)
            dden0, dden1 = dden[:, :PAIR], dden[:, PAIR:]
            high0, high1 = dden0.astype(bf16), dden1.astype(bf16)
            split0 = jnp.where(low_lanes, dden0, dden0 - high0.astype(f32)).astype(bf16)
            split1 = jnp.where(low_lanes, dden1, dden1 - high1.astype(f32)).astype(bf16)
            dnum0, dnum1 = halves(dnum, low_lanes)
            xs = jnp.concatenate(
                [
                    jnp.concatenate([dnum0, split0], axis=1),
                    jnp.concatenate([dnum1, split1], axis=1),
                ],
                axis=0,
            )
            valued = jnp.concatenate([v, ones], axis=1)
            first_two = dot_nt(xs, jnp.concatenate([valued, state], axis=0))
            dscores = jnp.where(allowed2, first_two[:, :SUB], 0.0).astype(bf16)
            dq = dot(dscores, k) + first_two[:, SUB:] * carried2
            dq = jnp.where(low_lanes, dq[:SUB], dq[SUB:])
            v0, v1 = halves(v, low_lanes)
            k0, k1 = halves(k, low_lanes)
            q0, q1 = halves(q, low_lanes)
            back0 = dot_nt(
                jnp.concatenate([v0, ones], axis=1),
                jnp.concatenate([jnp.concatenate([dnum, split0], axis=1), later_low], axis=0),
            )
            back1 = dot_nt(
                jnp.concatenate([v1, ones], axis=1),
                jnp.concatenate([jnp.concatenate([dnum, split1], axis=1), later_low], axis=0),
            )
            back = jnp.concatenate([back0, back1], axis=0)
            ks = jnp.concatenate([k0, k1], axis=0)
            q_turned = jnp.transpose(q)
            over = dot(ks, jnp.concatenate([q_turned, later_low[:, :PAIR]], axis=1))
            left = jnp.concatenate(
                [
                    jnp.where(flipped2, back[:, :SUB], 0.0).astype(bf16),
                    jnp.where(flipped2, over[:, :SUB], 0.0).astype(bf16),
                ],
                axis=1,
            )
            right = jnp.concatenate(
                [
                    jnp.concatenate([q, zeros], axis=1),
                    jnp.concatenate([zeros, dnum], axis=1),
                ],
                axis=0,
            )
            both = dot(left, right)
            dk = both[:, :PAIR] + back[:, SUB:] * feeding2
            dv = both[:, PAIR:] + over[:, SUB:] * feeding2
            dk = jnp.where(low_lanes, dk[:SUB], dk[SUB:])
            dv = jnp.where(low_lanes, dv[:SUB], dv[SUB:])
            dqk_ref[at, lanes] = (dq * q.astype(f32)).astype(bf16)
            dqk_ref[at, width + pair * PAIR : width + (pair + 1) * PAIR] = (
                dk * k.astype(f32)
            ).astype(bf16)
            dz_ref[at, 2 * width + pair * PAIR : 2 * width + (pair + 1) * PAIR] = dv.astype(bf16)
            qs = jnp.concatenate([q0 * carried_low, q1 * carried_low], axis=0)
            added = lax.dot_general(qs, xs, TN, preferred_element_type=f32)
            state_ref[pair * PAIR : (pair + 1) * PAIR, :] = keeping * later + added

    cosine = cos_ref[...]
    sine = sin_ref[...]
    dctt = dctt_ref[...]
    for part in range(2):
        for start in range(0, width, group):
            begin = part * width + start
            turned = dot(dqk_ref[:, begin : begin + group], dctt)
            for lane in range(0, group, PAIR):
                tile = turned[:, lane : lane + PAIR]
                back = tile * cosine - pltpu.roll(tile, HS, 1) * sine
                dz_ref[:, begin + lane : begin + lane + PAIR] = back.astype(bf16)

    dz = dz_ref[...]
    dx_ref[...] = dot(dz, wft_ref[...]).astype(bf16)
    db_ref[...] += jnp.sum(dz.astype(f32), axis=0, keepdims=True)


def whole_spec(array):
    return pl.BlockSpec(array.shape, lambda i, *_: (0,) * array.ndim)


def forward_layer(x, starts, wf, bf, wo, dct, cosine, sine, state_in, first_place, block):
    rows, model = x.shape
    seqs, count = starts.shape
    span = wf.shape[1]
    inner = wo.shape[0]
    width = (span - inner) // 2
    hidden = inner - width
    pairs = width // PAIR
    blocks = rows // block
    per_seq = blocks // seqs
    by_rows = lambda cols: pl.BlockSpec((block, cols), lambda i, *_: (i, 0))
    state_rows = block // SUB * pairs * PAIR
    return pl.pallas_call(
        partial(forward_kernel, width, count, per_seq, first_place),
        grid_spec=pltpu.PrefetchScalarGridSpec(
            num_scalar_prefetch=1,
            grid=(blocks,),
            in_specs=[
                by_rows(model),
                whole_spec(wf),
                whole_spec(bf),
                whole_spec(wo),
                whole_spec(dct),
                by_rows(PAIR),
                by_rows(PAIR),
                pl.BlockSpec((1, pairs * PAIR, 2 * PAIR), lambda i, *_: (i // per_seq, 0, 0)),
            ],
            out_specs=[
                by_rows(model),
                by_rows(3 * width),
                by_rows(inner),
                by_rows(width),
                by_rows(hidden),
                pl.BlockSpec((state_rows, 2 * PAIR), lambda i, *_: (i, 0)),
                by_rows(model),
            ],
            scratch_shapes=[pltpu.VMEM((pairs * PAIR, 2 * PAIR), f32)],
        ),
        out_shape=[
            jax.ShapeDtypeStruct((rows, model), bf16),
            jax.ShapeDtypeStruct((rows, 3 * width), bf16),
            jax.ShapeDtypeStruct((rows, inner), bf16),
            jax.ShapeDtypeStruct((rows, width), bf16),
            jax.ShapeDtypeStruct((rows, hidden), bf16),
            jax.ShapeDtypeStruct((blocks * state_rows, 2 * PAIR), bf16),
            jax.ShapeDtypeStruct((rows, model), bf16),
        ],
        compiler_params=pltpu.CompilerParams(vmem_limit_bytes=56 * 1024 * 1024),
        cost_estimate=pl.CostEstimate(
            flops=2 * rows * model * (span + inner),
            bytes_accessed=2 * rows * (3 * model + 3 * width + inner + width + hidden),
            transcendentals=0,
        ),
        name="layer_forward",
    )(starts, x, wf, bf, wo, dct, cosine, sine, state_in)


def backward_layer(bg, starts, wot, wft, dctt, cosine, sine, state_in, saved, first_place, block):
    qkv, ca, rden, gp, states = saved
    rows, model = bg.shape
    seqs, count = starts.shape
    span = wft.shape[0]
    inner = wot.shape[1]
    width = (span - inner) // 2
    hidden = inner - width
    pairs = width // PAIR
    blocks = rows // block
    per_seq = blocks // seqs
    by_rows = lambda cols: pl.BlockSpec((block, cols), lambda i, *_: (blocks - 1 - i, 0))
    state_rows = block // SUB * pairs * PAIR
    return pl.pallas_call(
        partial(backward_kernel, width, count, per_seq, first_place),
        grid_spec=pltpu.PrefetchScalarGridSpec(
            num_scalar_prefetch=1,
            grid=(blocks,),
            in_specs=[
                by_rows(model),
                whole_spec(wot),
                whole_spec(wft),
                whole_spec(dctt),
                by_rows(PAIR),
                by_rows(PAIR),
                pl.BlockSpec(
                    (1, pairs * PAIR, 2 * PAIR), lambda i, *_: ((blocks - 1 - i) // per_seq, 0, 0)
                ),
                by_rows(3 * width),
                by_rows(inner),
                by_rows(width),
                by_rows(hidden),
                pl.BlockSpec((state_rows, 2 * PAIR), lambda i, *_: (blocks - 1 - i, 0)),
            ],
            out_specs=[
                by_rows(span),
                by_rows(model),
                pl.BlockSpec((1, span), lambda i, *_: (0, 0)),
            ],
            scratch_shapes=[
                pltpu.VMEM((pairs * PAIR, 2 * PAIR), f32),
                pltpu.VMEM((block, 2 * width), bf16),
            ],
        ),
        out_shape=[
            jax.ShapeDtypeStruct((rows, span), bf16),
            jax.ShapeDtypeStruct((rows, model), bf16),
            jax.ShapeDtypeStruct((1, span), f32),
        ],
        compiler_params=pltpu.CompilerParams(vmem_limit_bytes=56 * 1024 * 1024),
        cost_estimate=pl.CostEstimate(
            flops=2 * rows * model * (span + inner),
            bytes_accessed=2 * rows * (2 * model + span + 3 * width + inner + width + hidden),
            transcendentals=0,
        ),
        name="layer_backward",
    )(starts, bg, wot, wft, dctt, cosine, sine, state_in, qkv, ca, rden, gp, states)


def swapped(array, axis, distance):
    size = lax.axis_size(axis)
    return lax.ppermute(array, axis, [(i, i ^ distance) for i in range(size)])


def bits_of(axis):
    return [1 << b for b in range(lax.axis_size(axis).bit_length() - 1)]


def gather_rows(block, axis):
    own = lax.axis_index(axis)
    held = {0: block}
    for distance in reversed(bits_of(axis)):
        held.update({m | distance: swapped(b, axis, distance) for m, b in list(held.items())})
    rows = block.shape[0]
    whole = jnp.zeros((rows * len(held),) + block.shape[1:], block.dtype)
    for m, b in held.items():
        whole = lax.dynamic_update_slice_in_dim(whole, b, (own ^ m) * rows, 0)
    return whole


def scatter_rows(partial_sum, axis):
    own = lax.axis_index(axis)
    size = lax.axis_size(axis)
    rows = partial_sum.shape[0] // size
    rest = partial_sum.shape[1:]
    now = partial_sum.reshape((size, rows) + rest)
    distances = bits_of(axis)
    for distance in distances:
        now = now.reshape((now.shape[0] // 2, 2, rows) + rest)
        bit = (own // distance) % 2
        keep = lax.dynamic_index_in_dim(now, bit, 1, keepdims=False)
        send = lax.dynamic_index_in_dim(now, 1 - bit, 1, keepdims=False)
        now = keep.astype(f32) + swapped(send, axis, distance).astype(f32)
        if distance != distances[-1]:
            now = now.astype(bf16)
    return now.reshape((rows,) + rest)


def on_device(
    tokens,
    doc_starts,
    norm_gains,
    norm_shifts,
    qkv_weight,
    qkv_bias,
    dense_weight,
    dense_bias,
    up_weight,
    up_bias,
    down_weight,
    down_bias,
    out_grad,
):
    layers = qkv_weight.shape[0]
    seqs = doc_starts.shape[0]
    model = tokens.shape[1]
    total_rows = tokens.shape[0] * lax.axis_size("tensor")
    length = total_rows // seqs
    heads = qkv_weight.shape[2] // (3 * HS)
    padded = heads + heads % 2
    width = padded * HS
    group = 2 * PAIR if padded % 4 == 0 else PAIR
    block = min(512, length)

    order = jnp.asarray(column_order(heads), bf16)
    feature = feature_matrix(group)
    dct = jnp.asarray(feature, bf16)
    dctt = jnp.asarray(feature.T, bf16)
    cosine, sine = rotary_tables(doc_starts, length)
    zero_state = jnp.zeros((seqs, padded // 2 * PAIR, 2 * PAIR), f32)
    gains = norm_gains.astype(f32)
    shifts = norm_shifts.astype(f32)

    folded = []
    for l in range(layers):
        ordered = dot(qkv_weight[l], order)
        wf = jnp.concatenate(
            [
                (gains[l, 0][:, None] * ordered).astype(bf16),
                (gains[l, 1][:, None] * up_weight[l].astype(f32)).astype(bf16),
            ],
            axis=1,
        )
        bias_one = dot(norm_shifts[l, 0:1], qkv_weight[l]) + qkv_bias[l].astype(f32)[None]
        bias_one = jnp.dot(bias_one, order.astype(f32), precision=lax.Precision.HIGHEST)
        bias_two = dot(norm_shifts[l, 1:2], up_weight[l]) + up_bias[l].astype(f32)[None]
        bf = jnp.concatenate([bias_one, bias_two], axis=1)
        dense = dense_weight[l]
        if padded != heads:
            dense = jnp.concatenate([dense, jnp.zeros((width - heads * HS, model), bf16)], axis=0)
        wo = jnp.concatenate([dense, down_weight[l]], axis=0)
        folded.append((wf, bf, wo, ordered.astype(bf16)))

    gathered_out_grad = gather_rows(out_grad, "tensor")
    own = tokens
    inputs = []
    saved = []
    for l in range(layers):
        wf, bf, wo, _ = folded[l]
        x = gather_rows(own, "tensor")
        xh, qkv, ca, rden, gp, states, out = forward_layer(
            x, doc_starts, wf, bf, wo, dct, cosine, sine, zero_state, 0, block
        )
        summed = scatter_rows(out, "tensor")
        inputs.append(own)
        saved.append((xh, qkv, ca, rden, gp, states))
        biases = dense_bias[l].astype(f32) + down_bias[l].astype(f32)
        own = (own.astype(f32) + (summed + biases)).astype(bf16)
    result = own

    incoming = out_grad.astype(f32)
    sums = [None] * layers
    weight_grads = [None] * layers
    for l in reversed(range(layers)):
        wf, bf, wo, ordered = folded[l]
        xh, qkv, ca, rden, gp, states = saved[l]
        own_grad = incoming.astype(bf16)
        bias_grad = jnp.sum(own_grad.astype(f32), axis=0)
        bg = gathered_out_grad if l == layers - 1 else gather_rows(own_grad, "tensor")
        dz, dx, db = backward_layer(
            bg,
            doc_starts,
            wo.T,
            wf.T,
            dctt,
            cosine,
            sine,
            zero_state,
            (qkv, ca, rden, gp, states),
            0,
            block,
        )
        out_weight_grad = lax.dot_general(ca, bg, TN, preferred_element_type=f32)
        in_weight_grad = lax.dot_general(xh, dz, TN, preferred_element_type=f32)
        db_one, db_two = db[:, : 3 * width], db[:, 3 * width :]
        grad_one = in_weight_grad[:, : 3 * width]
        grad_two = in_weight_grad[:, 3 * width :]
        weights_one = ordered.astype(f32)
        weights_two = up_weight[l].astype(f32)
        gain_grad = jnp.stack(
            [jnp.sum(weights_one * grad_one, axis=1), jnp.sum(weights_two * grad_two, axis=1)]
        )
        shift_grad = jnp.stack(
            [jnp.sum(weights_one * db_one, axis=1), jnp.sum(weights_two * db_two, axis=1)]
        )
        qkv_grad = (gains[l, 0][:, None] * grad_one + shifts[l, 0][:, None] * db_one).astype(bf16)
        up_grad = (gains[l, 1][:, None] * grad_two + shifts[l, 1][:, None] * db_two).astype(bf16)
        dense_grad = out_weight_grad[: heads * HS].astype(bf16)
        down_grad = out_weight_grad[width:].astype(bf16)
        qkv_bias_grad = jnp.dot(
            db_one, order.astype(f32).T, precision=lax.Precision.HIGHEST
        ).astype(bf16)[0]
        up_bias_grad = db_two.astype(bf16)[0]
        weight_grads[l] = lax.psum(
            (qkv_grad, dense_grad, up_grad, down_grad, qkv_bias_grad, up_bias_grad), "dp"
        )
        sums[l] = (gain_grad, shift_grad, bias_grad)

        normed_grad = scatter_rows(dx, "tensor")
        rows_in = inputs[l].astype(f32)
        center = jnp.mean(rows_in, axis=-1, keepdims=True)
        shifted = rows_in - center
        spread = jnp.mean(shifted * shifted, axis=-1, keepdims=True)
        inverse = lax.rsqrt(spread + norm_eps)
        normal = shifted * inverse
        along = jnp.mean(normed_grad * normal, axis=-1, keepdims=True)
        level = jnp.mean(normed_grad, axis=-1, keepdims=True)
        incoming = incoming + inverse * (normed_grad - level - normal * along)

    stack = lambda j: jnp.stack([weight_grads[l][j] for l in range(layers)])
    qkv_total = lax.dot_general(
        stack(0), order, (((2,), (1,)), ((), ())), preferred_element_type=f32
    )
    gains_total, shifts_total, bias_total = lax.psum(
        tuple(jnp.stack([sums[l][j] for l in range(layers)]) for j in range(3)), ("dp", "tensor")
    )
    return (
        result,
        incoming,
        gains_total,
        shifts_total,
        qkv_total,
        stack(4).astype(f32),
        stack(1).astype(f32),
        bias_total,
        stack(2).astype(f32),
        stack(5).astype(f32),
        stack(3).astype(f32),
        bias_total,
    )


def solution(mesh):
    return jax.shard_map(
        on_device,
        mesh=mesh,
        in_specs=(
            P(("dp", "tensor"), None),
            P("dp", None),
            P(),
            P(),
            P(None, None, "tensor"),
            P(None, "tensor"),
            P(None, "tensor", None),
            P(),
            P(None, None, "tensor"),
            P(None, "tensor"),
            P(None, "tensor", None),
            P(),
            P(("dp", "tensor"), None),
        ),
        out_specs=(
            P(("dp", "tensor"), None),
            P(("dp", "tensor"), None),
            P(),
            P(),
            P(None, None, "tensor"),
            P(None, "tensor"),
            P(None, "tensor", None),
            P(),
            P(None, None, "tensor"),
            P(None, "tensor"),
            P(None, "tensor", None),
            P(),
        ),
        check_vma=False,
    )
```

```python
from functools import partial
import math

import numpy as np
import jax
import jax.numpy as jnp
from jax import lax
from jax.experimental import pallas as pl
from jax.experimental.pallas import tpu as pltpu
from jax.sharding import PartitionSpec as P

HS = 64
FEATS = 64
ROT = 16
PAIR = 2 * HS
SUB = 128
HIDDEN_CHUNK = 256
PARTS = 2

norm_eps = 1e-05
feature_scale = 0.75
rotary_base = 10000.0

f32 = jnp.float32
bf16 = jnp.bfloat16
NT = (((1,), (1,)), ((), ()))
TN = (((0,), (0,)), ((), ()))


def pair_order():
    half = ROT // 2
    rest = (HS - ROT) // 2
    order = []
    for side in range(2):
        for head in range(2):
            order += [(head, side * half + i) for i in range(half)]
        for head in range(2):
            order += [(head, ROT + side * rest + i) for i in range(rest)]
    return order


def column_order(heads):
    padded = heads + heads % 2
    width = padded * HS
    matrix = np.zeros((heads * 3 * HS, 3 * width), np.float32)
    order = pair_order()
    for pair in range(padded // 2):
        for lane, (side, entry) in enumerate(order):
            head = 2 * pair + side
            if head < heads:
                for part in range(2):
                    matrix[head * 3 * HS + part * HS + entry, part * width + pair * PAIR + lane] = 1
    for head in range(heads):
        for entry in range(HS):
            matrix[head * 3 * HS + 2 * HS + entry, 2 * width + head * HS + entry] = 1
    return matrix


def feature_matrix(group):
    rows = np.arange(FEATS)[:, None]
    cols = np.arange(HS)[None, :]
    table = np.cos(np.pi * (cols + 0.5) * rows / HS) * np.sqrt(2.0 / HS)
    table = table * np.where(rows == 0, np.sqrt(0.5), 1.0) * feature_scale
    matrix = np.zeros((group, group), np.float32)
    for pair in range(group // PAIR):
        for lane, (side, entry) in enumerate(pair_order()):
            start = pair * PAIR + side * FEATS
            matrix[pair * PAIR + lane, start : start + FEATS] = table[:, entry]
    return matrix


def rotary_tables(starts, length):
    places = jnp.arange(length, dtype=jnp.int32)
    started = starts[:, :, None] <= places[None, None, :]
    latest = jnp.max(jnp.where(started, starts[:, :, None], 0), axis=1)
    offsets = (places[None, :] - latest).reshape(1, -1).astype(f32)
    half = ROT // 2
    inverse = rotary_base ** (-(jnp.arange(half, dtype=f32) * 2.0 / ROT))
    angles = inverse[:, None] * offsets
    cos_lanes = np.zeros((half, PAIR), np.float32)
    sin_lanes = np.zeros((half, PAIR), np.float32)
    plain = np.zeros((1, PAIR), np.float32)
    for lane, (_, entry) in enumerate(pair_order()):
        if entry < ROT:
            cos_lanes[entry % half, lane] = 1.0
            sin_lanes[entry % half, lane] = -1.0 if entry < half else 1.0
        else:
            plain[0, lane] = 1.0

    def spread(table, lanes):
        return lax.dot_general(
            table, jnp.asarray(lanes), TN, precision=lax.Precision.HIGHEST
        )

    cosine = spread(jnp.cos(angles), cos_lanes) + jnp.asarray(plain)
    return cosine, spread(jnp.sin(angles), sin_lanes)


def dot(a, b):
    return jnp.dot(a, b, preferred_element_type=f32)


def dot_nt(a, b):
    return lax.dot_general(a, b, NT, preferred_element_type=f32)


def latest_start(starts_ref, seq, count, places):
    latest = jnp.zeros_like(places)
    for j in range(count):
        start = starts_ref[seq, j]
        latest = jnp.maximum(latest, jnp.where(start <= places, start, 0))
    return latest


def latest_scalar(starts_ref, seq, count, place):
    latest = jnp.int32(0)
    for j in range(count):
        start = starts_ref[seq, j]
        latest = jnp.maximum(latest, jnp.where(start <= place, start, 0))
    return latest


def block_masks(starts_ref, seq, count, place):
    rows = place + lax.broadcasted_iota(jnp.int32, (SUB, SUB), 0)
    cols = place + lax.broadcasted_iota(jnp.int32, (SUB, SUB), 1)
    latest_rows = latest_start(starts_ref, seq, count, rows)
    allowed = (cols <= rows) & (cols >= latest_rows)
    carried = (latest_rows <= place).astype(f32)
    following = latest_scalar(starts_ref, seq, count, place + SUB)
    feeding = (rows >= following).astype(f32)
    keeping = jnp.where(following <= place, 1.0, 0.0).astype(f32)
    return rows, cols, allowed, carried, feeding, keeping


def gelu_parts(hidden):
    share = 0.5 + 0.5 * lax.erf(hidden * math.sqrt(0.5))
    bell = jnp.exp(hidden * hidden * -0.5)
    return hidden * share, share + hidden * (bell * (1.0 / math.sqrt(2.0 * math.pi)))


def lane_halves():
    lane = lax.broadcasted_iota(jnp.int32, (SUB, PAIR), 1)
    low = (lane < HS).astype(f32).astype(bf16)
    return low, 1 - low


def pick_rows(seq, within, index, refs):
    values = []
    for one in refs:
        if len(one) == 1:
            values.append(one[0][...])
        else:
            values.append(jnp.where(within == index, one[0][...], one[1][...]))
    return jnp.where(seq == 0, values[0], values[1])


def place_rows(seq, within, index, rows, refs):
    if len(refs) == 1:
        refs[0][...] = rows
        return
    for side in range(2):
        for sent in range(2):

            @pl.when((seq == side) & ((within == index) == (sent == 0)))
            def _():
                refs[2 * side + sent][...] = rows


def forward_kernel(
    count,
    blocks_per_seq,
    first_place,
    shapes,
    starts_ref,
    index_ref,
    *refs,
):
    ways, rest = shapes
    sources = (refs[: ways[0]], refs[ways[0] : sum(ways)])
    outs = refs[sum(ways) + 16 : sum(ways) + 16 + rest]
    forward_body(
        count,
        blocks_per_seq,
        first_place,
        starts_ref,
        index_ref[0],
        sources,
        outs,
        *refs[sum(ways) : sum(ways) + 16],
        *refs[sum(ways) + 16 + rest :],
    )


def forward_body(
    count,
    blocks_per_seq,
    first_place,
    starts_ref,
    index,
    sources,
    outs,
    wq_ref,
    bq_ref,
    wu_ref,
    bu_ref,
    wo_ref,
    dct_ref,
    cos_ref,
    sin_ref,
    state_in_ref,
    xh_ref,
    qkv_ref,
    ca_ref,
    rden_ref,
    gp_ref,
    states_ref,
    state_out_ref,
    state_ref,
):
    step = pl.program_id(0)
    seq = step // blocks_per_seq
    within = lax.rem(step, blocks_per_seq)
    rows = sources[0][0].shape[0]
    inner = wu_ref.shape[1]
    width = wo_ref.shape[0] - inner
    pairs = width // PAIR
    group = dct_ref.shape[0]

    @pl.when(within == 0)
    def _():
        state_ref[...] = state_in_ref[0]

    x = pick_rows(seq, within, index, sources).astype(f32)
    center = jnp.mean(x, axis=-1, keepdims=True)
    shifted = x - center
    spread = jnp.mean(shifted * shifted, axis=-1, keepdims=True)
    xh = (shifted * lax.rsqrt(spread + norm_eps)).astype(bf16)
    xh_ref[...] = xh

    cosine = cos_ref[...]
    sine = sin_ref[...]
    dct = dct_ref[...]
    mixed = dot(xh, wq_ref[...]) + bq_ref[...]
    for start in range(0, 2 * width, group):
        turned = []
        for lane in range(start, start + group, PAIR):
            tile = mixed[:, lane : lane + PAIR]
            turned.append((tile * cosine + pltpu.roll(tile, HS, 1) * sine).astype(bf16))
        turned = turned[0] if len(turned) == 1 else jnp.concatenate(turned, axis=1)
        qkv_ref[:, start : start + group] = jnp.exp(dot(turned, dct)).astype(bf16)
    qkv_ref[:, 2 * width :] = mixed[:, 2 * width :].astype(bf16)

    low_lanes = lax.broadcasted_iota(jnp.int32, (SUB, PAIR), 1) < HS
    low, high = lane_halves()
    ones = jnp.ones((SUB, PAIR), bf16)
    active, slope = gelu_parts(dot(xh, wu_ref[...]) + bu_ref[...])
    ca_ref[:, width:] = active.astype(bf16)
    gp_ref[...] = slope.astype(bf16)

    for sub in range(rows // SUB):
        place = first_place + within * rows + sub * SUB
        _, _, allowed, carried, feeding, keeping = block_masks(starts_ref, seq, count, place)
        carried = carried.astype(bf16)
        feeding = feeding.astype(bf16)
        at = slice(sub * SUB, (sub + 1) * SUB)
        for pair in range(pairs):
            lanes = slice(pair * PAIR, (pair + 1) * PAIR)
            q = qkv_ref[at, pair * PAIR : (pair + 1) * PAIR]
            k = qkv_ref[at, width + pair * PAIR : width + (pair + 1) * PAIR]
            v = qkv_ref[at, 2 * width + pair * PAIR : 2 * width + (pair + 1) * PAIR]
            q0, q1 = q * low, q * high
            qs = jnp.concatenate([q0, q1], axis=0)
            scores = dot_nt(qs, k)
            weights = [
                jnp.where(allowed, scores[:SUB], 0.0).astype(bf16),
                jnp.where(allowed, scores[SUB:], 0.0).astype(bf16),
            ]
            state = state_ref[pair * PAIR : (pair + 1) * PAIR, :]
            state_low = state.astype(bf16)
            first = (sub * pairs + pair) * PAIR
            states_ref[first : first + PAIR, :] = state_low
            left = jnp.concatenate(
                [
                    jnp.concatenate([weights[0], q0 * carried], axis=1),
                    jnp.concatenate([weights[1], q1 * carried], axis=1),
                ],
                axis=0,
            )
            valued = jnp.concatenate([v, ones], axis=1)
            both = dot(left, jnp.concatenate([valued, state_low], axis=0))
            numerator = jnp.where(low_lanes, both[:SUB, :PAIR], both[SUB:, :PAIR])
            denominator = jnp.where(low_lanes, both[:SUB, PAIR:], both[SUB:, PAIR:])
            inverse = 1.0 / denominator
            ca_ref[at, lanes] = (numerator * inverse).astype(bf16)
            rden_ref[at, lanes] = inverse.astype(bf16)
            added = lax.dot_general(k * feeding, valued, TN, preferred_element_type=f32)
            state_ref[pair * PAIR : (pair + 1) * PAIR, :] = keeping * state + added

    out = dot(ca_ref[...], wo_ref[...]).astype(bf16)
    place_rows(seq, within, index, out, outs)

    @pl.when(within == blocks_per_seq - 1)
    def _():
        state_out_ref[0] = state_ref[...]


def backward_kernel(
    count,
    blocks_per_seq,
    first_place,
    shapes,
    starts_ref,
    index_ref,
    *refs,
):
    ways, rest = shapes
    sources = (refs[: ways[0]], refs[ways[0] : sum(ways)])
    outs = refs[sum(ways) + 15 : sum(ways) + 15 + rest]
    backward_body(
        count,
        blocks_per_seq,
        first_place,
        starts_ref,
        index_ref[0],
        sources,
        outs,
        *refs[sum(ways) : sum(ways) + 15],
        *refs[sum(ways) + 15 + rest :],
    )


def backward_body(
    count,
    blocks_per_seq,
    first_place,
    starts_ref,
    index,
    sources,
    outs,
    wq_ref,
    wu_ref,
    wo_ref,
    dctt_ref,
    cos_ref,
    sin_ref,
    state_in_ref,
    qkv_ref,
    ca_ref,
    rden_ref,
    gp_ref,
    states_ref,
    dz_ref,
    db_ref,
    state_out_ref,
    state_ref,
    dqk_ref,
    split_ref,
    dnum_ref,
):
    step = pl.program_id(0)
    blocks = pl.num_programs(0)
    seq = (blocks - 1 - step) // blocks_per_seq
    within = lax.rem(blocks - 1 - step, blocks_per_seq)
    rows = sources[0][0].shape[0]
    inner = wu_ref.shape[1]
    width = wo_ref.shape[0] - inner
    pairs = width // PAIR
    group = dctt_ref.shape[0]

    @pl.when(within == blocks_per_seq - 1)
    def _():
        state_ref[...] = state_in_ref[0]

    @pl.when(step == 0)
    def _():
        db_ref[...] = jnp.zeros_like(db_ref)

    bg = pick_rows(seq, within, index, sources)
    context_grad = dot_nt(bg, wo_ref[:width, :])

    low_rows = lax.broadcasted_iota(jnp.int32, (rows, PAIR), 1) < HS
    low_lanes = lax.broadcasted_iota(jnp.int32, (SUB, PAIR), 1) < HS
    low, high = lane_halves()
    ones = jnp.ones((SUB, PAIR), bf16)
    zeros = jnp.zeros((SUB, PAIR), bf16)
    sum_rows = lax.broadcasted_iota(jnp.int32, (2 * PAIR, 2 * PAIR), 0)
    sum_cols = lax.broadcasted_iota(jnp.int32, (2 * PAIR, 2 * PAIR), 1)
    same_head = (lax.rem(sum_rows, PAIR) // HS) == (sum_cols // PAIR)
    summing = jnp.where(same_head, -1.0 / HS, 0.0).astype(bf16)

    for pair in range(pairs):
        lanes = slice(pair * PAIR, (pair + 1) * PAIR)
        scaled = context_grad[:, lanes] * rden_ref[:, lanes].astype(f32)
        dnum_ref[:, lanes] = scaled.astype(bf16)
        product = scaled * ca_ref[:, lanes].astype(f32)
        product_high = product.astype(bf16)
        product_low = (product - product_high.astype(f32)).astype(bf16)
        dden = dot(jnp.concatenate([product_high, product_low], axis=1), summing)
        for side in range(2):
            part = dden[:, side * PAIR : (side + 1) * PAIR]
            top = part.astype(bf16).astype(f32)
            split = jnp.where(low_rows, part, part - top).astype(bf16)
            split_ref[:, (2 * pair + side) * PAIR : (2 * pair + side + 1) * PAIR] = split

    subs = rows // SUB
    chunk = min(inner, HIDDEN_CHUNK)
    chunks = inner // chunk
    done = 0

    def hidden_chunk(j):
        at = slice(j * chunk, (j + 1) * chunk)
        active_grad = dot_nt(bg, wo_ref[width + j * chunk : width + (j + 1) * chunk, :])
        grad = (active_grad * gp_ref[:, at].astype(f32)).astype(bf16)
        dz_ref[:, 3 * width + j * chunk : 3 * width + (j + 1) * chunk] = grad

    for sub in reversed(range(subs)):
        while done < (subs - sub) * chunks // subs:
            hidden_chunk(done)
            done += 1
        place = first_place + within * rows + sub * SUB
        rows_at, cols_at, allowed, carried, feeding, keeping = block_masks(
            starts_ref, seq, count, place
        )
        latest_cols = latest_start(starts_ref, seq, count, cols_at)
        flipped = (rows_at <= cols_at) & (rows_at >= latest_cols)
        carried_low = carried.astype(bf16)
        at = slice(sub * SUB, (sub + 1) * SUB)
        items = [dict(pair=pair) for pair in range(pairs)]
        for it in items:
            pair = it["pair"]
            it["q"] = qkv_ref[at, pair * PAIR : (pair + 1) * PAIR]
            it["k"] = qkv_ref[at, width + pair * PAIR : width + (pair + 1) * PAIR]
            it["v"] = qkv_ref[at, 2 * width + pair * PAIR : 2 * width + (pair + 1) * PAIR]
            it["dnum"] = dnum_ref[at, pair * PAIR : (pair + 1) * PAIR]
            it["split"] = [
                split_ref[at, (2 * pair + side) * PAIR : (2 * pair + side + 1) * PAIR]
                for side in range(2)
            ]
            first = (sub * pairs + pair) * PAIR
            it["state"] = states_ref[first : first + PAIR, :]
            it["later"] = state_ref[pair * PAIR : (pair + 1) * PAIR, :]
            it["later_low"] = it["later"].astype(bf16)
        for it in items:
            it["xs"] = jnp.concatenate(
                [
                    jnp.concatenate([it["dnum"] * low, it["split"][0]], axis=1),
                    jnp.concatenate([it["dnum"] * high, it["split"][1]], axis=1),
                ],
                axis=0,
            )
            valued = jnp.concatenate([it["v"], ones], axis=1)
            it["ahead"] = dot_nt(it["xs"], jnp.concatenate([valued, it["state"]], axis=0))
        for it in items:
            back = []
            for side, mask in enumerate((low, high)):
                back.append(
                    dot_nt(
                        jnp.concatenate([it["v"] * mask, ones], axis=1),
                        jnp.concatenate(
                            [
                                jnp.concatenate([it["dnum"], it["split"][side]], axis=1),
                                it["later_low"],
                            ],
                            axis=0,
                        ),
                    )
                )
            it["back"] = back
        for it in items:
            ks = jnp.concatenate([it["k"] * low, it["k"] * high], axis=0)
            it["q_turned"] = jnp.transpose(it["q"])
            it["over"] = dot(
                ks, jnp.concatenate([it["q_turned"], it["later_low"][:, :PAIR]], axis=1)
            )
        for it in items:
            qc = it["q"] * carried_low
            qs = jnp.concatenate([qc * low, qc * high], axis=0)
            added = lax.dot_general(qs, it["xs"], TN, preferred_element_type=f32)
            pair = it["pair"]
            state_ref[pair * PAIR : (pair + 1) * PAIR, :] = keeping * it["later"] + added
        for it in items:
            dscores = jnp.concatenate(
                [
                    jnp.where(allowed, it["ahead"][:SUB, :SUB], 0.0).astype(bf16),
                    jnp.where(allowed, it["ahead"][SUB:, :SUB], 0.0).astype(bf16),
                ],
                axis=0,
            )
            it["dq"] = dot(dscores, it["k"])
        for it in items:
            left = jnp.concatenate(
                [
                    jnp.concatenate(
                        [
                            jnp.where(flipped, it["back"][side][:, :SUB], 0.0).astype(bf16),
                            jnp.where(
                                flipped, it["over"][side * SUB : (side + 1) * SUB, :SUB], 0.0
                            ).astype(bf16),
                        ],
                        axis=1,
                    )
                    for side in range(2)
                ],
                axis=0,
            )
            right = jnp.concatenate(
                [
                    jnp.concatenate([it["q"], zeros], axis=1),
                    jnp.concatenate([zeros, it["dnum"]], axis=1),
                ],
                axis=0,
            )
            it["both"] = dot(left, right)
        for it in items:
            pair = it["pair"]
            dq, ahead, both, back, over = (
                it["dq"],
                it["ahead"],
                it["both"],
                it["back"],
                it["over"],
            )
            dq = (
                jnp.where(low_lanes, dq[:SUB], dq[SUB:])
                + jnp.where(low_lanes, ahead[:SUB, SUB:], ahead[SUB:, SUB:]) * carried
            )
            dk = (
                jnp.where(low_lanes, both[:SUB, :PAIR], both[SUB:, :PAIR])
                + jnp.where(low_lanes, back[0][:, SUB:], back[1][:, SUB:]) * feeding
            )
            dv = (
                jnp.where(low_lanes, both[:SUB, PAIR:], both[SUB:, PAIR:])
                + jnp.where(low_lanes, over[:SUB, SUB:], over[SUB:, SUB:]) * feeding
            )
            dqk_ref[at, pair * PAIR : (pair + 1) * PAIR] = (dq * it["q"].astype(f32)).astype(bf16)
            dqk_ref[at, width + pair * PAIR : width + (pair + 1) * PAIR] = (
                dk * it["k"].astype(f32)
            ).astype(bf16)
            dz_ref[at, 2 * width + pair * PAIR : 2 * width + (pair + 1) * PAIR] = dv.astype(bf16)

    cosine = cos_ref[...]
    sine = sin_ref[...]
    dctt = dctt_ref[...]
    for start in range(0, 2 * width, group):
        turned = dot(dqk_ref[:, start : start + group], dctt)
        for lane in range(0, group, PAIR):
            tile = turned[:, lane : lane + PAIR]
            back = tile * cosine - pltpu.roll(tile, HS, 1) * sine
            dz_ref[:, start + lane : start + lane + PAIR] = back.astype(bf16)

    dx = dot_nt(dz_ref[:, 3 * width :], wu_ref[...]) + dot_nt(dz_ref[:, : 3 * width], wq_ref[...])
    place_rows(seq, within, index, dx.astype(bf16), outs)
    db_ref[...] += jnp.sum(dz_ref[...].astype(f32), axis=0, keepdims=True)

    @pl.when(within == 0)
    def _():
        state_out_ref[0] = state_ref[...]


def out_weight_kernel(parts, steps, ways, index_ref, *refs):
    lefts = refs[:parts]
    rights, at = [], parts
    for count in ways:
        rights.append(refs[at : at + count])
        at += count
    grad_ref, total_ref = refs[at:]
    step = pl.program_id(0)
    per_part = steps // parts
    per_side = per_part // 2
    index = index_ref[0]

    @pl.when(step == 0)
    def _():
        total_ref[...] = jnp.zeros_like(total_ref)

    for part in range(parts):
        for side in range(2):
            first = part * per_part + side * per_side
            blocks = rights[2 * part + side]

            @pl.when((step >= first) & (step < first + per_side))
            def _():
                right = blocks[0][...]
                if len(blocks) == 2:
                    right = jnp.where(step - first == index, right, blocks[1][...])
                total_ref[...] += lax.dot_general(
                    lefts[part][...], right, TN, preferred_element_type=f32
                )

    @pl.when(step == steps - 1)
    def _():
        grad_ref[...] = total_ref[...].astype(bf16)


def in_weight_kernel(parts, steps, pieces, *refs):
    lefts, rights = refs[:parts], refs[parts : 2 * parts]
    db_ref, gains_ref, wq_ref, wu_ref = refs[2 * parts : 2 * parts + 4]
    grad_refs = refs[2 * parts + 4 : 2 * parts + 4 + pieces]
    sums_ref, total_ref = refs[2 * parts + 4 + pieces :]
    step = pl.program_id(0)
    per_part = steps // parts

    @pl.when(step == 0)
    def _():
        total_ref[...] = jnp.zeros_like(total_ref)

    for part in range(parts):

        @pl.when((step >= part * per_part) & (step < (part + 1) * per_part))
        def _():
            total_ref[...] += lax.dot_general(
                lefts[part][...], rights[part][...], TN, preferred_element_type=f32
            )

    @pl.when(step == steps - 1)
    def _():
        split = wq_ref.shape[1]
        rows = 128
        lane = lax.broadcasted_iota(jnp.int32, (rows, 128), 1)
        per_piece = total_ref.shape[0] // pieces
        for piece, grad_ref in enumerate(grad_refs):

            @pl.loop(0, per_piece // rows)
            def _(block):
                inside = pl.ds(pl.multiple_of(block * rows, rows), rows)
                at = pl.ds(pl.multiple_of(piece * per_piece + block * rows, rows), rows)
                columns = gains_ref[at, :]
                sums = jnp.zeros((rows, 128), f32)
                for j, (weight_ref, cols) in enumerate(
                    ((wq_ref, slice(0, split)), (wu_ref, slice(split, None)))
                ):
                    gain, shift = columns[:, j : j + 1], columns[:, 2 + j : 3 + j]
                    total = total_ref[at, cols]
                    bias = db_ref[:, cols]
                    weight = weight_ref[at, :].astype(f32)
                    grad_ref[inside, cols] = (gain * total + shift * bias).astype(bf16)
                    sums = sums + jnp.where(
                        lane == j, jnp.sum(weight * total, axis=1, keepdims=True), 0.0
                    )
                    sums = sums + jnp.where(
                        lane == 2 + j, jnp.sum(weight * bias, axis=1, keepdims=True), 0.0
                    )
                sums_ref[at, :] = sums


def with_token(kernel, inputs, waits):
    def body(*refs):
        outputs = refs[inputs + waits :]
        token_at = kernel.token
        outputs[token_at][...] = jnp.zeros_like(outputs[token_at])
        kernel.run(*refs[:inputs], *outputs[:token_at], *outputs[token_at + 1 :])

    return body


class Timed:
    def __init__(self, run, token):
        self.run = run
        self.token = token


class Order:
    def __init__(self):
        self.before = []
        self.token = None

    def after(self, array):
        if self.token is None:
            return array
        return array + self.token.astype(array.dtype).reshape((1,) * array.ndim)

    def call(self, run, scalars, operands, specs, out_specs, out_shape, **options):
        waits, self.before = self.before, []
        token_spec = pl.BlockSpec((1, 1), lambda i, *_: (0, 0))
        body = with_token(Timed(run, len(out_shape)), len(scalars) + len(operands), len(waits))
        *results, token = pl.pallas_call(
            body,
            grid_spec=pltpu.PrefetchScalarGridSpec(
                num_scalar_prefetch=len(scalars),
                grid=options.pop("grid"),
                in_specs=list(specs) + [pl.BlockSpec(memory_space=pl.ANY)] * len(waits),
                out_specs=list(out_specs) + [token_spec],
                scratch_shapes=options.pop("scratch_shapes", []),
            ),
            out_shape=list(out_shape) + [jax.ShapeDtypeStruct((1, 1), f32)],
            compiler_params=pltpu.CompilerParams(vmem_limit_bytes=56 * 1024 * 1024),
            cost_estimate=pl.CostEstimate(flops=0, bytes_accessed=0, transcendentals=0),
            **options,
        )(*scalars, *operands, *waits)
        self.token = token
        return results

    def mark(self, *arrays):
        self.before += arrays
        self.call(lambda *refs: None, [], [], [], [], [], grid=(1,), name="mark")


def whole_spec(array):
    return pl.BlockSpec(array.shape, lambda i, *_: (0,) * array.ndim)


def row_spec(block, cols, first, last, offset=0):
    return pl.BlockSpec((block, cols), lambda i, *_: (jnp.clip(i, first, last) - first + offset, 0))


def split_rows(source):
    return not isinstance(source[1], int)


def row_sources(sources, block, per_seq, step_of):
    arrays, specs, ways = [], [], []
    for side, source in enumerate(sources):
        first = side * per_seq
        model = source[0].shape[1]
        if split_rows(source):
            arrays += source
            specs += [pl.BlockSpec((block, model), lambda i, *_: (0, 0))] * 2
            ways.append(2)
        else:
            arrays.append(source[0])
            specs.append(
                pl.BlockSpec(
                    (block, model),
                    lambda i, *_, first=first, offset=source[1]: (
                        jnp.clip(step_of(i), first, first + per_seq - 1) - first + offset,
                        0,
                    ),
                )
            )
            ways.append(1)
    return arrays, specs, tuple(ways)


def row_outs(block, model, blocks, split, step_of):
    if split == 1:
        return [pl.BlockSpec((block, model), lambda i, *_: (step_of(i), 0))]
    return [pl.BlockSpec((block, model), lambda i, *_: (0, 0))] * 4


def forward_layer(when, own, other, starts, index, weights, dct, cosine, sine, state_in, part, parts, block):
    wq, bq, wu, bu, wo = weights
    model = wq.shape[0]
    seqs, count = starts.shape
    length = cosine.shape[0] // seqs // parts
    rows = length * seqs
    hidden = wu.shape[1]
    width = wo.shape[0] - hidden
    pairs = width // PAIR
    per_seq = length // block
    blocks = per_seq * seqs
    by_rows = lambda cols: pl.BlockSpec((block, cols), lambda i, *_: (i, 0))
    table = pl.BlockSpec(
        (block, PAIR),
        lambda i, *_: ((i // per_seq) * per_seq * parts + part * per_seq + lax.rem(i, per_seq), 0),
    )
    state_spec = pl.BlockSpec((1, pairs * PAIR, 2 * PAIR), lambda i, *_: (i // per_seq, 0, 0))
    state_rows = block // SUB * pairs * PAIR
    sources, source_specs, ways = row_sources((own, other), block, per_seq, lambda i: i)
    outs = row_outs(block, model, blocks, len(own) if split_rows(own) else 1, lambda i: i)
    return when.call(
        partial(forward_kernel, count, per_seq, part * length, (ways, len(outs))),
        [starts, index],
        [*sources, *weights, dct, cosine, sine, state_in],
        source_specs
            + [whole_spec(w) for w in (*weights, dct)]
            + [table, table, state_spec],
        [
                by_rows(model),
                by_rows(3 * width),
                by_rows(width + hidden),
                by_rows(width),
                by_rows(hidden),
                pl.BlockSpec((state_rows, 2 * PAIR), lambda i, *_: (i, 0)),
                state_spec,
                *outs,
            ],
        [
            jax.ShapeDtypeStruct((rows, model), bf16),
            jax.ShapeDtypeStruct((rows, 3 * width), bf16),
            jax.ShapeDtypeStruct((rows, width + hidden), bf16),
            jax.ShapeDtypeStruct((rows, width), bf16),
            jax.ShapeDtypeStruct((rows, hidden), bf16),
            jax.ShapeDtypeStruct((blocks * state_rows, 2 * PAIR), bf16),
            jax.ShapeDtypeStruct((seqs, pairs * PAIR, 2 * PAIR), f32),
            *[jax.ShapeDtypeStruct((rows // len(outs), model), bf16) for _ in outs],
        ],
        grid=(blocks,),
        scratch_shapes=[pltpu.VMEM((pairs * PAIR, 2 * PAIR), f32)],
        name="forward_layer",
    )


def backward_layer(
    when, own, other, starts, index, weights, dctt, cosine, sine, state_in, saved, part, parts, block
):
    wq, _, wu, _, wo = weights
    weights = (wq, wu, wo)
    model = wq.shape[0]
    seqs, count = starts.shape
    length = cosine.shape[0] // seqs // parts
    rows = length * seqs
    hidden = wu.shape[1]
    width = wo.shape[0] - hidden
    span = 3 * width + hidden
    pairs = width // PAIR
    per_seq = length // block
    blocks = per_seq * seqs
    by_rows = lambda cols: pl.BlockSpec((block, cols), lambda i, *_: (blocks - 1 - i, 0))

    def table_index(i, *_):
        at = blocks - 1 - i
        return (at // per_seq) * per_seq * parts + part * per_seq + lax.rem(at, per_seq), 0

    table = pl.BlockSpec((block, PAIR), table_index)
    state_spec = pl.BlockSpec(
        (1, pairs * PAIR, 2 * PAIR), lambda i, *_: ((blocks - 1 - i) // per_seq, 0, 0)
    )
    state_rows = block // SUB * pairs * PAIR
    back = lambda i: blocks - 1 - i
    sources, source_specs, ways = row_sources((own, other), block, per_seq, back)
    outs = row_outs(block, model, blocks, len(own) if split_rows(own) else 1, back)
    return when.call(
        partial(backward_kernel, count, per_seq, part * length, (ways, len(outs))),
        [starts, index],
        [*sources, *weights, dctt, cosine, sine, state_in, *saved],
        source_specs
            + [whole_spec(w) for w in (*weights, dctt)]
            + [
                table,
                table,
                state_spec,
                by_rows(3 * width),
                by_rows(width + hidden),
                by_rows(width),
                by_rows(hidden),
                pl.BlockSpec((state_rows, 2 * PAIR), lambda i, *_: (blocks - 1 - i, 0)),
            ],
        [
                by_rows(span),
                pl.BlockSpec((1, span), lambda i, *_: (0, 0)),
                state_spec,
                *outs,
            ],
        [
            jax.ShapeDtypeStruct((rows, span), bf16),
            jax.ShapeDtypeStruct((1, span), f32),
            jax.ShapeDtypeStruct((seqs, pairs * PAIR, 2 * PAIR), f32),
            *[jax.ShapeDtypeStruct((rows // len(outs), model), bf16) for _ in outs],
        ],
        grid=(blocks,),
        scratch_shapes=[
                pltpu.VMEM((pairs * PAIR, 2 * PAIR), f32),
                pltpu.VMEM((block, 2 * width), bf16),
                pltpu.VMEM((block, 2 * width), bf16),
                pltpu.VMEM((block, width), bf16),
            ],
        name="backward_layer",
    )


def out_weight_grad(when, cas, grads, index, length, block):
    parts = len(cas)
    per_side = length // block
    per_part = 2 * per_side
    steps = per_part * parts
    inner, model = cas[0].shape[1], grads[0][0][0].shape[1]
    rights, right_specs, ways = [], [], ()
    for p, pair in enumerate(grads):
        arrays, specs, count = row_sources(
            pair, block, per_side, lambda i, p=p: jnp.clip(i - p * per_part, 0, per_part - 1)
        )
        rights += arrays
        right_specs += specs
        ways += count
    return when.call(
        partial(out_weight_kernel, parts, steps, ways),
        [index],
        [*cas, *rights],
        [row_spec(block, inner, p * per_part, (p + 1) * per_part - 1) for p in range(parts)]
        + right_specs,
        [pl.BlockSpec((inner, model), lambda i, *_: (0, 0))],
        [jax.ShapeDtypeStruct((inner, model), bf16)],
        grid=(steps,),
        scratch_shapes=[pltpu.VMEM((inner, model), f32)],
        name="out_weight_grad",
    )


def in_weight_grad(when, xhs, dzs, db, columns, wq, wu, block, pieces):
    parts = len(xhs)
    per_part = xhs[0].shape[0] // block
    steps = per_part * parts
    model, span = xhs[0].shape[1], dzs[0].shape[1]
    rows_of = lambda cols: [
        row_spec(block, cols, p * per_part, (p + 1) * per_part - 1) for p in range(parts)
    ]
    per_piece = model // pieces
    return when.call(
        partial(in_weight_kernel, parts, steps, pieces),
        [],
        [*xhs, *dzs, db, columns, wq, wu],
        rows_of(model) + rows_of(span) + [whole_spec(a) for a in (db, columns, wq, wu)],
        [pl.BlockSpec((per_piece, span), lambda i, *_: (0, 0))] * pieces
        + [pl.BlockSpec((model, 128), lambda i, *_: (0, 0))],
        [jax.ShapeDtypeStruct((per_piece, span), bf16)] * pieces
        + [jax.ShapeDtypeStruct((model, 128), f32)],
        grid=(steps,),
        scratch_shapes=[pltpu.VMEM((model, span), f32)],
        name="in_weight_grad",
    )


def swapped(array, axis, distance):
    size = lax.axis_size(axis)
    return lax.ppermute(array, axis, [(i, i ^ distance) for i in range(size)])


def distances(size):
    return [1 << b for b in range(size.bit_length() - 1)]


def bit_of(axis, distance):
    return (lax.axis_index(axis) // distance) % 2


def joined(array, axis, distance):
    partner = swapped(array, axis, distance)
    upper = bit_of(axis, distance) == 1
    return jnp.concatenate(
        [jnp.where(upper, partner, array), jnp.where(upper, array, partner)], axis=0
    )


def gather_inner(rows, inner):
    for distance in distances(inner):
        rows = joined(rows, "tensor", distance)
    return rows


def inner_source(rows, inner):
    if inner == 2:
        return (rows, swapped(rows, "tensor", 1))
    return (gather_inner(rows, inner), 0)


def reduce_start(partial_sums, inner, when):
    if len(partial_sums) == 4:
        keep0, send0, keep1, send1 = partial_sums
        when.before += [send0, send1]
        return [keep0, keep1], [swapped(send0, "tensor", 1), swapped(send1, "tensor", 1)]
    model = partial_sums[0].shape[1]
    share = partial_sums[0].shape[0] // (2 * inner)
    now = [half.reshape(inner, share, model) for half in jnp.split(partial_sums[0], 2)]
    for distance in reversed(distances(inner)):
        half = now[0].shape[0] // 2
        bit = bit_of("tensor", distance)
        keep = [lax.dynamic_slice_in_dim(one, bit * half, half, 0) for one in now]
        send = [lax.dynamic_slice_in_dim(one, (1 - bit) * half, half, 0) for one in now]
        got = [swapped(one, "tensor", distance) for one in send]
        if distance > 1:
            now = reduce_join((keep, got), when)
    return [one.reshape(share, model) for one in keep], [one.reshape(share, model) for one in got]


def reduce_join(pending, when):
    keep, got = pending
    return [
        when.after(keep[side].astype(f32) + got[side].astype(f32)).astype(bf16)
        for side in range(2)
    ]


def sum_over_dp(array, order, when):
    now = array
    kept = []
    for distance in order[:-1]:
        half = now.shape[0] // 2
        bit = bit_of("dp", distance)
        send = lax.dynamic_slice_in_dim(now, (1 - bit) * half, half, 0)
        when.before.append(send)
        got = swapped(send, "dp", distance)
        yield
        keep = lax.dynamic_slice_in_dim(now, bit * half, half, 0)
        now = when.after(keep.astype(f32) + got.astype(f32)).astype(bf16)
        kept.append(distance)
    when.before.append(now)
    got = swapped(now, "dp", order[-1])
    yield
    now = when.after(now.astype(f32) + got.astype(f32)).astype(bf16)
    for distance in reversed(kept):
        when.before.append(now)
        got = swapped(now, "dp", distance)
        yield
        upper = bit_of("dp", distance) == 1
        now = jnp.concatenate(
            [when.after(jnp.where(upper, got, now)), when.after(jnp.where(upper, now, got))],
            axis=0,
        )
    return now


class Sum:
    def __init__(self, array, order, when):
        self.run = sum_over_dp(array, order, when)
        self.value = None
        self.step()

    def step(self):
        if self.value is None:
            try:
                next(self.run)
            except StopIteration as stop:
                self.value = stop.value

    def finish(self):
        while self.value is None:
            self.step()
        return self.value


def small_sum(array, axes):
    for axis in axes:
        for distance in distances(lax.axis_size(axis)):
            array = array + swapped(array, axis, distance)
    return array


def to_shares(rows, inner, parts):
    half = rows.shape[0] // 2
    if inner == 2 and parts == 2:
        upper = bit_of("tensor", 1)
        send = lax.dynamic_slice_in_dim(rows, (1 - upper) * half, half, 0)
        got = swapped(send, "tensor", 1)
        return [jnp.where(upper == 1, got, rows[:half]), jnp.where(upper == 1, rows[half:], got)]
    whole = gather_inner(rows, inner)
    part_rows = whole.shape[0] // parts
    share = part_rows // inner
    first = lax.rem(lax.axis_index("tensor"), inner) * share
    return [
        lax.dynamic_slice_in_dim(whole, part * part_rows + first, share, 0)
        for part in range(parts)
    ]


def to_placement(shares, inner):
    parts = len(shares)
    if inner == 2 and parts == 2:
        upper = bit_of("tensor", 1) == 1
        mine = jnp.where(upper, shares[1], shares[0])
        theirs = jnp.where(upper, shares[0], shares[1])
        got = swapped(theirs, "tensor", 1)
        return jnp.concatenate([jnp.where(upper, got, mine), jnp.where(upper, mine, got)], axis=0)
    whole = jnp.concatenate([gather_inner(rows, inner) for rows in shares], axis=0)
    rows = whole.shape[0] // inner
    index = lax.rem(lax.axis_index("tensor"), inner)
    return lax.dynamic_slice_in_dim(whole, index * rows, rows, 0)


def on_device(
    tokens,
    doc_starts,
    norm_gains,
    norm_shifts,
    qkv_weight,
    qkv_bias,
    dense_weight,
    dense_bias,
    up_weight,
    up_bias,
    down_weight,
    down_bias,
    out_grad,
):
    layers = qkv_weight.shape[0]
    seqs = doc_starts.shape[0]
    model = tokens.shape[1]
    size = lax.axis_size("tensor")
    inner = size // seqs
    index = lax.axis_index("tensor")
    inner_index = lax.rem(index, inner)
    length = tokens.shape[0] * inner
    heads = qkv_weight.shape[2] // (3 * HS)
    padded = heads + heads % 2
    width = padded * HS
    group = 2 * PAIR if padded % 4 == 0 else PAIR
    parts = PARTS
    part_rows = length // parts
    share = part_rows // inner
    block = share if inner == 2 else min(512, part_rows)
    per_part = part_rows // block
    dp_size = lax.axis_size("dp")
    early_x = distances(dp_size)
    late_x = early_x[1:] + early_x[:1]

    when = Order()
    order = jnp.asarray(column_order(heads), bf16)
    feature = feature_matrix(group)
    dct = jnp.asarray(feature, bf16)
    dctt = jnp.asarray(feature.T, bf16)
    starts = jnp.where(index < inner, doc_starts, doc_starts[::-1])
    cosine, sine = rotary_tables(starts, length)
    zero_state = jnp.zeros((seqs, padded // 2 * PAIR, 2 * PAIR), f32)
    gains = norm_gains.astype(f32)
    shifts = norm_shifts.astype(f32)

    last = layers - 1
    place = jnp.full((1,), inner_index, jnp.int32)

    xs = to_shares(tokens, inner, parts)
    def fold(l):
        qkv, up, dense, down = qkv_weight[l], up_weight[l], dense_weight[l], down_weight[l]
        gain_one, gain_two = gains[l, 0][:, None], gains[l, 1][:, None]
        if l > 0:
            gain_one, gain_two = when.after(gain_one), when.after(gain_two)
        ordered = dot(qkv, order).astype(bf16)
        wq = (gain_one * ordered.astype(f32)).astype(bf16)
        wu = (gain_two * up.astype(f32)).astype(bf16)
        bias_one = dot(norm_shifts[l, 0:1], qkv) + qkv_bias[l].astype(f32)[None]
        bq = jnp.dot(bias_one, order.astype(f32), precision=lax.Precision.HIGHEST)
        bu = dot(norm_shifts[l, 1:2], up) + up_bias[l].astype(f32)[None]
        if padded != heads:
            dense = jnp.concatenate([dense, jnp.zeros((width - heads * HS, model), bf16)], axis=0)
        wo = jnp.concatenate([dense, down], axis=0)
        return (wq, bq, wu, bu, wo), ordered

    folded = [None] * layers
    folded[0] = fold(0)
    crossing_x = [swapped(xs[0], "tensor", inner), None]
    when.mark(cosine, sine, *folded[0][0])
    x_parts = [None] * parts
    x_parts[0] = (
        inner_source(xs[0], inner),
        inner_source(when.after(crossing_x[0]), inner),
    )
    when.mark(crossing_x[0])
    sent = when.after(xs[1])
    crossing_x[1] = swapped(sent, "tensor", inner)
    when.before.append(sent)
    when.token = None
    inputs = [None] * layers
    saved = [[None] * parts for _ in range(layers)]
    sums = [[None] * parts for _ in range(layers)]

    def run_forward(l, part, state):
        own, other = x_parts[part]
        xh, qkv, ca, rden, gp, states, state, *out = forward_layer(
            when, own, other, starts, place, folded[l][0], dct, cosine, sine, state, part, parts, block
        )
        saved[l][part] = (xh, qkv, ca, rden, gp, states)
        sums[l][part] = out
        return state

    def begin_reduce(partial_sum):
        return reduce_start(partial_sum, inner, when)

    def cross_reduce(pending):
        mine, theirs = reduce_join(pending, when)
        when.before += [mine, theirs]
        return mine, swapped(theirs, "tensor", inner)

    def end_forward(l, part, crossing):
        mine, got = crossing
        biases = dense_bias[l].astype(f32) + down_bias[l].astype(f32)
        summed = when.after(mine.astype(f32) + got.astype(f32))
        rows = (inputs[l][part].astype(f32) + (summed + biases)).astype(bf16)
        when.before.append(rows)
        return rows

    def end_backward(l, part, crossing):
        mine, got = crossing
        normed_grad = when.after(mine.astype(f32) + got.astype(f32))
        rows_in = inputs[l][part].astype(f32)
        center = jnp.mean(rows_in, axis=-1, keepdims=True)
        shifted = rows_in - center
        spread = jnp.mean(shifted * shifted, axis=-1, keepdims=True)
        inverse = lax.rsqrt(spread + norm_eps)
        normal = shifted * inverse
        along = jnp.mean(normed_grad * normal, axis=-1, keepdims=True)
        level = jnp.mean(normed_grad, axis=-1, keepdims=True)
        rows = incoming[part] + inverse * (normed_grad - level - normal * along)
        when.before.append(rows)
        return rows

    def whole_part(share_rows, crossing):
        return inner_source(share_rows, inner), inner_source(when.after(crossing), inner)

    def send_across(rows):
        when.before.append(rows)
        return swapped(rows, "tensor", inner)

    out_grad_shares = to_shares(out_grad, inner, parts)
    incoming = [rows.astype(f32) for rows in out_grad_shares]
    grads = [None] * parts
    crossing_grad = [None] * parts

    def send_out_grad(part):
        crossing_grad[part] = send_across(when.after(out_grad_shares[part]))

    for l in range(layers):
        inputs[l] = xs
        state = run_forward(l, 0, zero_state)
        if l < last:
            pending = begin_reduce(sums[l][0])
            if l == 0:
                x_parts[1] = whole_part(xs[1], crossing_x[1])
            crossing0 = cross_reduce(pending)
            state = run_forward(l, 1, state)
            pending = begin_reduce(sums[l][1])
            x0 = end_forward(l, 0, crossing0)
            far0 = send_across(x0)
            when.mark(x0)
            crossing1 = cross_reduce(pending)
            folded[l + 1] = fold(l + 1)
            x1 = end_forward(l, 1, crossing1)
            far1 = send_across(x1)
            xs = [x0, x1]
            x_parts = [whole_part(x0, far0), None]
        else:
            x_parts[1] = whole_part(xs[1], far1)
            send_out_grad(1)
            state = run_forward(l, 1, state)
            grads[1] = whole_part(out_grad_shares[1], crossing_grad[1])
            send_out_grad(0)

    small = [None] * layers
    weight_sums = [None] * layers

    def run_backward(l, part, state):
        own, other = grads[part]
        xh, qkv, ca, rden, gp, states = saved[l][part]
        kept = (qkv, ca, rden, gp, states)
        dz, db, state, *dx = backward_layer(
            when,
            own,
            other,
            starts,
            place,
            folded[l][0],
            dctt,
            cosine,
            sine,
            state,
            kept,
            part,
            parts,
            block,
        )
        return dz, dx, db, state

    def out_weights(l):
        return out_weight_grad(
            when, [kept[2] for kept in saved[l]], grads, place, part_rows, block
        )[0]

    def in_weights(l, dzs, dbs, bias_grad, pieces):
        db = sum(dbs)
        columns = jnp.stack([gains[l, 0], gains[l, 1], shifts[l, 0], shifts[l, 1]], axis=1)
        *made, norm_sums = in_weight_grad(
            when,
            [kept[0] for kept in saved[l]],
            dzs,
            db,
            columns,
            folded[l][1],
            up_weight[l],
            block,
            pieces,
        )
        small[l] = (jnp.concatenate([norm_sums[:, :4].T, bias_grad], axis=0), db)
        return made

    running = []

    def advance():
        for one in running:
            one.step()

    def bias_sum():
        return sum(
            jnp.sum(rows.astype(bf16).astype(f32), axis=0, keepdims=True) for rows in incoming
        )

    for l in reversed(range(layers)):
        bias_grad = bias_sum()
        dz1, dx1, db1, state = run_backward(l, 1, zero_state)
        if l == last:
            grads[0] = whole_part(out_grad_shares[0], crossing_grad[0])
        else:
            grads[0] = whole_part(far0[0], far0[1])
        if l > 0:
            pending1 = begin_reduce(dx1)
            out_sum = out_weights(l)
            turned = list(range(dp_size))[::-1]
            out_sum = lax.psum(out_sum, "dp", axis_index_groups=[turned])
            crossing1 = cross_reduce(pending1)
            dz0, dx0, db0, state = run_backward(l, 0, state)
            g1 = end_backward(l, 1, crossing1)
            low1 = g1.astype(bf16)
            far1 = send_across(low1)
            pending0 = begin_reduce(dx0)
            crossing0 = cross_reduce(pending0)
            (made,) = in_weights(l, [dz0, dz1], [db0, db1], bias_grad, 1)
            when.before.append(made)
            weight_sums[l] = (out_sum, lax.psum(made, "dp"))
            g0 = end_backward(l, 0, crossing0)
            low0 = g0.astype(bf16)
            far0 = (low0, send_across(low0))
            grads = [None, whole_part(low1, far1)]
            incoming = [g0, g1]
        else:
            out_made = out_weights(l)
            if l < last:
                when.before.append(weight_sums[l + 1][0])
            dz0, dx0, db0, state = run_backward(l, 0, state)
            made = in_weights(l, [dz0, dz1], [db0, db1], bias_grad, 2)
            running += [
                Sum(made[0], early_x, when),
                Sum(made[1], late_x, when),
                Sum(out_made, early_x, when),
            ]
            weight_sums[l] = (running[2], running[0], running[1])
            pending = [begin_reduce(dx) for dx in (dx1, dx0)]
            crossing = [cross_reduce(one) for one in pending]
            incoming = [end_backward(l, part, crossing[1 - part]) for part in range(parts)]
            out_pending = [begin_reduce(one) for one in sums[last]]
            out_crossing = [cross_reduce(one) for one in out_pending]

    while any(one.value is None for one in running):
        advance()
    weight_grads = []
    for l in range(layers):
        out_sum, *in_sums = [
            one.finish() if isinstance(one, Sum) else one for one in weight_sums[l]
        ]
        weight_grads.append((out_sum, jnp.concatenate(in_sums, axis=0)))
    tokens_grad = to_placement(incoming, inner)
    result = to_placement(
        [end_forward(last, part, out_crossing[part]) for part in range(parts)], inner
    )
    norm_rows = jnp.concatenate([one[0] for one in small], axis=0)
    bias_rows = jnp.concatenate([one[1] for one in small], axis=0)
    span = bias_rows.shape[1]
    bias_rows = jnp.pad(bias_rows, ((0, 0), (0, -span % model))).reshape(-1, model)
    small_rows = small_sum(jnp.concatenate([norm_rows, bias_rows], axis=0), ("dp",))
    norm_rows = small_sum(small_rows[: 5 * layers], ("tensor",)).reshape(layers, 5, model)
    bias_rows = small_rows[5 * layers :].reshape(layers, -1)[:, :span]

    stack = lambda pick: jnp.stack([pick(l) for l in range(layers)])
    bias_total = norm_rows[:, 4]
    bias_one = bias_rows[:, : 3 * width]
    return (
        result,
        tokens_grad,
        norm_rows[:, 0:2],
        norm_rows[:, 2:4],
        lax.dot_general(
            stack(lambda l: weight_grads[l][1][:, : 3 * width]),
            order,
            (((2,), (1,)), ((), ())),
            preferred_element_type=f32,
        ),
        jnp.dot(bias_one, order.astype(f32).T, precision=lax.Precision.HIGHEST),
        stack(lambda l: weight_grads[l][0][: heads * HS]).astype(f32),
        bias_total,
        stack(lambda l: weight_grads[l][1][:, 3 * width :]).astype(f32),
        bias_rows[:, 3 * width :],
        stack(lambda l: weight_grads[l][0][width:]).astype(f32),
        bias_total,
    )


def solution(mesh):
    return jax.shard_map(
        on_device,
        mesh=mesh,
        in_specs=(
            P(("dp", "tensor"), None),
            P("dp", None),
            P(),
            P(),
            P(None, None, "tensor"),
            P(None, "tensor"),
            P(None, "tensor", None),
            P(),
            P(None, None, "tensor"),
            P(None, "tensor"),
            P(None, "tensor", None),
            P(),
            P(("dp", "tensor"), None),
        ),
        out_specs=(
            P(("dp", "tensor"), None),
            P(("dp", "tensor"), None),
            P(),
            P(),
            P(None, None, "tensor"),
            P(None, "tensor"),
            P(None, "tensor", None),
            P(),
            P(None, None, "tensor"),
            P(None, "tensor"),
            P(None, "tensor", None),
            P(),
        ),
        check_vma=False,
    )
```

```python
from functools import partial
import math

import numpy as np
import jax
import jax.numpy as jnp
from jax import lax
from jax.experimental import pallas as pl
from jax.experimental.pallas import tpu as pltpu
from jax.sharding import PartitionSpec as P

HS = 64
FEATS = 64
ROT = 16
PAIR = 2 * HS
SUB = 128
HIDDEN_CHUNK = 256
PARTS = 2

norm_eps = 1e-05
feature_scale = 0.75
rotary_base = 10000.0

f32 = jnp.float32
bf16 = jnp.bfloat16
NT = (((1,), (1,)), ((), ()))
TN = (((0,), (0,)), ((), ()))


def pair_order():
    half = ROT // 2
    rest = (HS - ROT) // 2
    order = []
    for side in range(2):
        for head in range(2):
            order += [(head, side * half + i) for i in range(half)]
        for head in range(2):
            order += [(head, ROT + side * rest + i) for i in range(rest)]
    return order


def column_order(heads):
    padded = heads + heads % 2
    width = padded * HS
    matrix = np.zeros((heads * 3 * HS, 3 * width), np.float32)
    order = pair_order()
    for pair in range(padded // 2):
        for lane, (side, entry) in enumerate(order):
            head = 2 * pair + side
            if head < heads:
                for part in range(2):
                    matrix[head * 3 * HS + part * HS + entry, part * width + pair * PAIR + lane] = 1
    for head in range(heads):
        for entry in range(HS):
            matrix[head * 3 * HS + 2 * HS + entry, 2 * width + head * HS + entry] = 1
    return matrix


def feature_matrix(group):
    rows = np.arange(FEATS)[:, None]
    cols = np.arange(HS)[None, :]
    table = np.cos(np.pi * (cols + 0.5) * rows / HS) * np.sqrt(2.0 / HS)
    table = table * np.where(rows == 0, np.sqrt(0.5), 1.0) * feature_scale
    matrix = np.zeros((group, group), np.float32)
    for pair in range(group // PAIR):
        for lane, (side, entry) in enumerate(pair_order()):
            start = pair * PAIR + side * FEATS
            matrix[pair * PAIR + lane, start : start + FEATS] = table[:, entry]
    return matrix


def rotary_tables(starts, length):
    places = jnp.arange(length, dtype=jnp.int32)
    started = starts[:, :, None] <= places[None, None, :]
    latest = jnp.max(jnp.where(started, starts[:, :, None], 0), axis=1)
    offsets = (places[None, :] - latest).reshape(1, -1).astype(f32)
    half = ROT // 2
    inverse = rotary_base ** (-(jnp.arange(half, dtype=f32) * 2.0 / ROT))
    angles = inverse[:, None] * offsets
    cos_lanes = np.zeros((half, PAIR), np.float32)
    sin_lanes = np.zeros((half, PAIR), np.float32)
    plain = np.zeros((1, PAIR), np.float32)
    for lane, (_, entry) in enumerate(pair_order()):
        if entry < ROT:
            cos_lanes[entry % half, lane] = 1.0
            sin_lanes[entry % half, lane] = -1.0 if entry < half else 1.0
        else:
            plain[0, lane] = 1.0

    def spread(table, lanes):
        return lax.dot_general(
            table, jnp.asarray(lanes), TN, precision=lax.Precision.HIGHEST
        )

    cosine = spread(jnp.cos(angles), cos_lanes) + jnp.asarray(plain)
    return cosine, spread(jnp.sin(angles), sin_lanes)


def dot(a, b):
    return jnp.dot(a, b, preferred_element_type=f32)


def dot_nt(a, b):
    return lax.dot_general(a, b, NT, preferred_element_type=f32)


def latest_start(starts_ref, seq, count, places):
    latest = jnp.zeros_like(places)
    for j in range(count):
        start = starts_ref[seq, j]
        latest = jnp.maximum(latest, jnp.where(start <= places, start, 0))
    return latest


def latest_scalar(starts_ref, seq, count, place):
    latest = jnp.int32(0)
    for j in range(count):
        start = starts_ref[seq, j]
        latest = jnp.maximum(latest, jnp.where(start <= place, start, 0))
    return latest


def block_masks(starts_ref, seq, count, place):
    rows = place + lax.broadcasted_iota(jnp.int32, (SUB, SUB), 0)
    cols = place + lax.broadcasted_iota(jnp.int32, (SUB, SUB), 1)
    latest_rows = latest_start(starts_ref, seq, count, rows)
    allowed = (cols <= rows) & (cols >= latest_rows)
    carried = (latest_rows <= place).astype(f32)
    following = latest_scalar(starts_ref, seq, count, place + SUB)
    feeding = (rows >= following).astype(f32)
    keeping = jnp.where(following <= place, 1.0, 0.0).astype(f32)
    return rows, cols, allowed, carried, feeding, keeping


def gelu_parts(hidden):
    share = 0.5 + 0.5 * lax.erf(hidden * math.sqrt(0.5))
    bell = jnp.exp(hidden * hidden * -0.5)
    return hidden * share, share + hidden * (bell * (1.0 / math.sqrt(2.0 * math.pi)))


def lane_halves():
    lane = lax.broadcasted_iota(jnp.int32, (SUB, PAIR), 1)
    low = (lane < HS).astype(f32).astype(bf16)
    return low, 1 - low


def pick_rows(seq, within, index, refs):
    values = []
    for one in refs:
        if len(one) == 1:
            values.append(one[0][...])
        else:
            values.append(jnp.where(within == index, one[0][...], one[1][...]))
    return jnp.where(seq == 0, values[0], values[1])


def place_rows(seq, within, index, rows, refs):
    if len(refs) == 1:
        refs[0][...] = rows
        return
    for side in range(2):
        for sent in range(2):

            @pl.when((seq == side) & ((within == index) == (sent == 0)))
            def _():
                refs[2 * side + sent][...] = rows


def forward_kernel(
    count,
    blocks_per_seq,
    first_place,
    shapes,
    starts_ref,
    index_ref,
    *refs,
):
    ways, rest = shapes
    sources = (refs[: ways[0]], refs[ways[0] : sum(ways)])
    outs = refs[sum(ways) + 16 : sum(ways) + 16 + rest]
    forward_body(
        count,
        blocks_per_seq,
        first_place,
        starts_ref,
        index_ref[0],
        sources,
        outs,
        *refs[sum(ways) : sum(ways) + 16],
        *refs[sum(ways) + 16 + rest :],
    )


def forward_body(
    count,
    blocks_per_seq,
    first_place,
    starts_ref,
    index,
    sources,
    outs,
    wq_ref,
    bq_ref,
    wu_ref,
    bu_ref,
    wo_ref,
    dct_ref,
    cos_ref,
    sin_ref,
    state_in_ref,
    xh_ref,
    qkv_ref,
    ca_ref,
    rden_ref,
    gp_ref,
    states_ref,
    state_out_ref,
    state_ref,
):
    step = pl.program_id(0)
    seq = step // blocks_per_seq
    within = lax.rem(step, blocks_per_seq)
    rows = sources[0][0].shape[0]
    inner = wu_ref.shape[1]
    width = wo_ref.shape[0] - inner
    pairs = width // PAIR
    group = dct_ref.shape[0]

    @pl.when(within == 0)
    def _():
        state_ref[...] = state_in_ref[0]

    x = pick_rows(seq, within, index, sources).astype(f32)
    center = jnp.mean(x, axis=-1, keepdims=True)
    shifted = x - center
    spread = jnp.mean(shifted * shifted, axis=-1, keepdims=True)
    xh = (shifted * lax.rsqrt(spread + norm_eps)).astype(bf16)
    xh_ref[...] = xh

    cosine = cos_ref[...]
    sine = sin_ref[...]
    dct = dct_ref[...]
    mixed = dot(xh, wq_ref[...]) + bq_ref[...]
    for start in range(0, 2 * width, group):
        turned = []
        for lane in range(start, start + group, PAIR):
            tile = mixed[:, lane : lane + PAIR]
            turned.append((tile * cosine + pltpu.roll(tile, HS, 1) * sine).astype(bf16))
        turned = turned[0] if len(turned) == 1 else jnp.concatenate(turned, axis=1)
        qkv_ref[:, start : start + group] = jnp.exp(dot(turned, dct)).astype(bf16)
    qkv_ref[:, 2 * width :] = mixed[:, 2 * width :].astype(bf16)

    low_lanes = lax.broadcasted_iota(jnp.int32, (SUB, PAIR), 1) < HS
    low, high = lane_halves()
    ones = jnp.ones((SUB, PAIR), bf16)
    active, slope = gelu_parts(dot(xh, wu_ref[...]) + bu_ref[...])
    ca_ref[:, width:] = active.astype(bf16)
    gp_ref[...] = slope.astype(bf16)

    for sub in range(rows // SUB):
        place = first_place + within * rows + sub * SUB
        _, _, allowed, carried, feeding, keeping = block_masks(starts_ref, seq, count, place)
        carried = carried.astype(bf16)
        feeding = feeding.astype(bf16)
        at = slice(sub * SUB, (sub + 1) * SUB)
        for pair in range(pairs):
            lanes = slice(pair * PAIR, (pair + 1) * PAIR)
            q = qkv_ref[at, pair * PAIR : (pair + 1) * PAIR]
            k = qkv_ref[at, width + pair * PAIR : width + (pair + 1) * PAIR]
            v = qkv_ref[at, 2 * width + pair * PAIR : 2 * width + (pair + 1) * PAIR]
            q0, q1 = q * low, q * high
            qs = jnp.concatenate([q0, q1], axis=0)
            scores = dot_nt(qs, k)
            weights = [
                jnp.where(allowed, scores[:SUB], 0.0).astype(bf16),
                jnp.where(allowed, scores[SUB:], 0.0).astype(bf16),
            ]
            state = state_ref[pair * PAIR : (pair + 1) * PAIR, :]
            state_low = state.astype(bf16)
            first = (sub * pairs + pair) * PAIR
            states_ref[first : first + PAIR, :] = state_low
            left = jnp.concatenate(
                [
                    jnp.concatenate([weights[0], q0 * carried], axis=1),
                    jnp.concatenate([weights[1], q1 * carried], axis=1),
                ],
                axis=0,
            )
            valued = jnp.concatenate([v, ones], axis=1)
            both = dot(left, jnp.concatenate([valued, state_low], axis=0))
            numerator = jnp.where(low_lanes, both[:SUB, :PAIR], both[SUB:, :PAIR])
            denominator = jnp.where(low_lanes, both[:SUB, PAIR:], both[SUB:, PAIR:])
            inverse = 1.0 / denominator
            ca_ref[at, lanes] = (numerator * inverse).astype(bf16)
            rden_ref[at, lanes] = inverse.astype(bf16)
            added = lax.dot_general(k * feeding, valued, TN, preferred_element_type=f32)
            state_ref[pair * PAIR : (pair + 1) * PAIR, :] = keeping * state + added

    out = dot(ca_ref[...], wo_ref[...]).astype(bf16)
    place_rows(seq, within, index, out, outs)

    @pl.when(within == blocks_per_seq - 1)
    def _():
        state_out_ref[0] = state_ref[...]


def backward_kernel(
    count,
    blocks_per_seq,
    first_place,
    shapes,
    starts_ref,
    index_ref,
    *refs,
):
    ways, rest = shapes
    sources = (refs[: ways[0]], refs[ways[0] : sum(ways)])
    outs = refs[sum(ways) + 15 : sum(ways) + 15 + rest]
    backward_body(
        count,
        blocks_per_seq,
        first_place,
        starts_ref,
        index_ref[0],
        sources,
        outs,
        *refs[sum(ways) : sum(ways) + 15],
        *refs[sum(ways) + 15 + rest :],
    )


def backward_body(
    count,
    blocks_per_seq,
    first_place,
    starts_ref,
    index,
    sources,
    outs,
    wq_ref,
    wu_ref,
    wo_ref,
    dctt_ref,
    cos_ref,
    sin_ref,
    state_in_ref,
    qkv_ref,
    ca_ref,
    rden_ref,
    gp_ref,
    states_ref,
    dz_ref,
    db_ref,
    state_out_ref,
    state_ref,
    dqk_ref,
    split_ref,
    dnum_ref,
):
    step = pl.program_id(0)
    blocks = pl.num_programs(0)
    seq = (blocks - 1 - step) // blocks_per_seq
    within = lax.rem(blocks - 1 - step, blocks_per_seq)
    rows = sources[0][0].shape[0]
    inner = wu_ref.shape[1]
    width = wo_ref.shape[0] - inner
    pairs = width // PAIR
    group = dctt_ref.shape[0]

    @pl.when(within == blocks_per_seq - 1)
    def _():
        state_ref[...] = state_in_ref[0]

    @pl.when(step == 0)
    def _():
        db_ref[...] = jnp.zeros_like(db_ref)

    bg = pick_rows(seq, within, index, sources)
    context_grad = dot_nt(bg, wo_ref[:width, :])

    low_rows = lax.broadcasted_iota(jnp.int32, (rows, PAIR), 1) < HS
    low_lanes = lax.broadcasted_iota(jnp.int32, (SUB, PAIR), 1) < HS
    low, high = lane_halves()
    ones = jnp.ones((SUB, PAIR), bf16)
    zeros = jnp.zeros((SUB, PAIR), bf16)
    sum_rows = lax.broadcasted_iota(jnp.int32, (2 * PAIR, 2 * PAIR), 0)
    sum_cols = lax.broadcasted_iota(jnp.int32, (2 * PAIR, 2 * PAIR), 1)
    same_head = (lax.rem(sum_rows, PAIR) // HS) == (sum_cols // PAIR)
    summing = jnp.where(same_head, -1.0 / HS, 0.0).astype(bf16)

    for pair in range(pairs):
        lanes = slice(pair * PAIR, (pair + 1) * PAIR)
        scaled = context_grad[:, lanes] * rden_ref[:, lanes].astype(f32)
        dnum_ref[:, lanes] = scaled.astype(bf16)
        product = scaled * ca_ref[:, lanes].astype(f32)
        product_high = product.astype(bf16)
        product_low = (product - product_high.astype(f32)).astype(bf16)
        dden = dot(jnp.concatenate([product_high, product_low], axis=1), summing)
        for side in range(2):
            part = dden[:, side * PAIR : (side + 1) * PAIR]
            top = part.astype(bf16).astype(f32)
            split = jnp.where(low_rows, part, part - top).astype(bf16)
            split_ref[:, (2 * pair + side) * PAIR : (2 * pair + side + 1) * PAIR] = split

    subs = rows // SUB
    chunk = min(inner, HIDDEN_CHUNK)
    chunks = inner // chunk
    done = 0

    def hidden_chunk(j):
        at = slice(j * chunk, (j + 1) * chunk)
        active_grad = dot_nt(bg, wo_ref[width + j * chunk : width + (j + 1) * chunk, :])
        grad = (active_grad * gp_ref[:, at].astype(f32)).astype(bf16)
        dz_ref[:, 3 * width + j * chunk : 3 * width + (j + 1) * chunk] = grad

    for sub in reversed(range(subs)):
        while done < (subs - sub) * chunks // subs:
            hidden_chunk(done)
            done += 1
        place = first_place + within * rows + sub * SUB
        rows_at, cols_at, allowed, carried, feeding, keeping = block_masks(
            starts_ref, seq, count, place
        )
        latest_cols = latest_start(starts_ref, seq, count, cols_at)
        flipped = (rows_at <= cols_at) & (rows_at >= latest_cols)
        carried_low = carried.astype(bf16)
        at = slice(sub * SUB, (sub + 1) * SUB)
        items = [dict(pair=pair) for pair in range(pairs)]
        for it in items:
            pair = it["pair"]
            it["q"] = qkv_ref[at, pair * PAIR : (pair + 1) * PAIR]
            it["k"] = qkv_ref[at, width + pair * PAIR : width + (pair + 1) * PAIR]
            it["v"] = qkv_ref[at, 2 * width + pair * PAIR : 2 * width + (pair + 1) * PAIR]
            it["dnum"] = dnum_ref[at, pair * PAIR : (pair + 1) * PAIR]
            it["split"] = [
                split_ref[at, (2 * pair + side) * PAIR : (2 * pair + side + 1) * PAIR]
                for side in range(2)
            ]
            first = (sub * pairs + pair) * PAIR
            it["state"] = states_ref[first : first + PAIR, :]
            it["later"] = state_ref[pair * PAIR : (pair + 1) * PAIR, :]
            it["later_low"] = it["later"].astype(bf16)
        for it in items:
            it["xs"] = jnp.concatenate(
                [
                    jnp.concatenate([it["dnum"] * low, it["split"][0]], axis=1),
                    jnp.concatenate([it["dnum"] * high, it["split"][1]], axis=1),
                ],
                axis=0,
            )
            valued = jnp.concatenate([it["v"], ones], axis=1)
            it["ahead"] = dot_nt(it["xs"], jnp.concatenate([valued, it["state"]], axis=0))
        for it in items:
            back = []
            for side, mask in enumerate((low, high)):
                back.append(
                    dot_nt(
                        jnp.concatenate([it["v"] * mask, ones], axis=1),
                        jnp.concatenate(
                            [
                                jnp.concatenate([it["dnum"], it["split"][side]], axis=1),
                                it["later_low"],
                            ],
                            axis=0,
                        ),
                    )
                )
            it["back"] = back
        for it in items:
            ks = jnp.concatenate([it["k"] * low, it["k"] * high], axis=0)
            it["q_turned"] = jnp.transpose(it["q"])
            it["over"] = dot(
                ks, jnp.concatenate([it["q_turned"], it["later_low"][:, :PAIR]], axis=1)
            )
        for it in items:
            qc = it["q"] * carried_low
            qs = jnp.concatenate([qc * low, qc * high], axis=0)
            added = lax.dot_general(qs, it["xs"], TN, preferred_element_type=f32)
            pair = it["pair"]
            state_ref[pair * PAIR : (pair + 1) * PAIR, :] = keeping * it["later"] + added
        for it in items:
            dscores = jnp.concatenate(
                [
                    jnp.where(allowed, it["ahead"][:SUB, :SUB], 0.0).astype(bf16),
                    jnp.where(allowed, it["ahead"][SUB:, :SUB], 0.0).astype(bf16),
                ],
                axis=0,
            )
            it["dq"] = dot(dscores, it["k"])
        for it in items:
            left = jnp.concatenate(
                [
                    jnp.concatenate(
                        [
                            jnp.where(flipped, it["back"][side][:, :SUB], 0.0).astype(bf16),
                            jnp.where(
                                flipped, it["over"][side * SUB : (side + 1) * SUB, :SUB], 0.0
                            ).astype(bf16),
                        ],
                        axis=1,
                    )
                    for side in range(2)
                ],
                axis=0,
            )
            right = jnp.concatenate(
                [
                    jnp.concatenate([it["q"], zeros], axis=1),
                    jnp.concatenate([zeros, it["dnum"]], axis=1),
                ],
                axis=0,
            )
            it["both"] = dot(left, right)
        for it in items:
            pair = it["pair"]
            dq, ahead, both, back, over = (
                it["dq"],
                it["ahead"],
                it["both"],
                it["back"],
                it["over"],
            )
            dq = (
                jnp.where(low_lanes, dq[:SUB], dq[SUB:])
                + jnp.where(low_lanes, ahead[:SUB, SUB:], ahead[SUB:, SUB:]) * carried
            )
            dk = (
                jnp.where(low_lanes, both[:SUB, :PAIR], both[SUB:, :PAIR])
                + jnp.where(low_lanes, back[0][:, SUB:], back[1][:, SUB:]) * feeding
            )
            dv = (
                jnp.where(low_lanes, both[:SUB, PAIR:], both[SUB:, PAIR:])
                + jnp.where(low_lanes, over[:SUB, SUB:], over[SUB:, SUB:]) * feeding
            )
            dqk_ref[at, pair * PAIR : (pair + 1) * PAIR] = (dq * it["q"].astype(f32)).astype(bf16)
            dqk_ref[at, width + pair * PAIR : width + (pair + 1) * PAIR] = (
                dk * it["k"].astype(f32)
            ).astype(bf16)
            dz_ref[at, 2 * width + pair * PAIR : 2 * width + (pair + 1) * PAIR] = dv.astype(bf16)

    cosine = cos_ref[...]
    sine = sin_ref[...]
    dctt = dctt_ref[...]
    for start in range(0, 2 * width, group):
        turned = dot(dqk_ref[:, start : start + group], dctt)
        for lane in range(0, group, PAIR):
            tile = turned[:, lane : lane + PAIR]
            back = tile * cosine - pltpu.roll(tile, HS, 1) * sine
            dz_ref[:, start + lane : start + lane + PAIR] = back.astype(bf16)

    dx = dot_nt(dz_ref[:, 3 * width :], wu_ref[...]) + dot_nt(dz_ref[:, : 3 * width], wq_ref[...])
    place_rows(seq, within, index, dx.astype(bf16), outs)
    db_ref[...] += jnp.sum(dz_ref[...].astype(f32), axis=0, keepdims=True)

    @pl.when(within == 0)
    def _():
        state_out_ref[0] = state_ref[...]


def out_weight_kernel(parts, steps, ways, index_ref, *refs):
    lefts = refs[:parts]
    rights, at = [], parts
    for count in ways:
        rights.append(refs[at : at + count])
        at += count
    grad_ref, total_ref = refs[at:]
    step = pl.program_id(0)
    per_part = steps // parts
    per_side = per_part // 2
    index = index_ref[0]

    @pl.when(step == 0)
    def _():
        total_ref[...] = jnp.zeros_like(total_ref)

    for part in range(parts):
        for side in range(2):
            first = part * per_part + side * per_side
            blocks = rights[2 * part + side]

            @pl.when((step >= first) & (step < first + per_side))
            def _():
                right = blocks[0][...]
                if len(blocks) == 2:
                    right = jnp.where(step - first == index, right, blocks[1][...])
                total_ref[...] += lax.dot_general(
                    lefts[part][...], right, TN, preferred_element_type=f32
                )

    @pl.when(step == steps - 1)
    def _():
        grad_ref[...] = total_ref[...].astype(bf16)


def in_weight_kernel(parts, steps, pieces, *refs):
    lefts, rights = refs[:parts], refs[parts : 2 * parts]
    db_ref, gains_ref, wq_ref, wu_ref = refs[2 * parts : 2 * parts + 4]
    grad_refs = refs[2 * parts + 4 : 2 * parts + 4 + pieces]
    sums_ref, total_ref = refs[2 * parts + 4 + pieces :]
    step = pl.program_id(0)
    per_part = steps // parts

    @pl.when(step == 0)
    def _():
        total_ref[...] = jnp.zeros_like(total_ref)

    for part in range(parts):

        @pl.when((step >= part * per_part) & (step < (part + 1) * per_part))
        def _():
            total_ref[...] += lax.dot_general(
                lefts[part][...], rights[part][...], TN, preferred_element_type=f32
            )

    @pl.when(step == steps - 1)
    def _():
        split = wq_ref.shape[1]
        rows = 128
        lane = lax.broadcasted_iota(jnp.int32, (rows, 128), 1)
        per_piece = total_ref.shape[0] // pieces
        for piece, grad_ref in enumerate(grad_refs):

            @pl.loop(0, per_piece // rows)
            def _(block):
                inside = pl.ds(pl.multiple_of(block * rows, rows), rows)
                at = pl.ds(pl.multiple_of(piece * per_piece + block * rows, rows), rows)
                columns = gains_ref[at, :]
                sums = jnp.zeros((rows, 128), f32)
                for j, (weight_ref, cols) in enumerate(
                    ((wq_ref, slice(0, split)), (wu_ref, slice(split, None)))
                ):
                    gain, shift = columns[:, j : j + 1], columns[:, 2 + j : 3 + j]
                    total = total_ref[at, cols]
                    bias = db_ref[:, cols]
                    weight = weight_ref[at, :].astype(f32)
                    grad_ref[inside, cols] = (gain * total + shift * bias).astype(bf16)
                    sums = sums + jnp.where(
                        lane == j, jnp.sum(weight * total, axis=1, keepdims=True), 0.0
                    )
                    sums = sums + jnp.where(
                        lane == 2 + j, jnp.sum(weight * bias, axis=1, keepdims=True), 0.0
                    )
                sums_ref[at, :] = sums


def with_token(kernel, inputs, waits):
    def body(*refs):
        outputs = refs[inputs + waits :]
        token_at = kernel.token
        outputs[token_at][...] = jnp.zeros_like(outputs[token_at])
        kernel.run(*refs[:inputs], *outputs[:token_at], *outputs[token_at + 1 :])

    return body


class Timed:
    def __init__(self, run, token):
        self.run = run
        self.token = token


class Order:
    def __init__(self):
        self.before = []
        self.token = None

    def after(self, array):
        if self.token is None:
            return array
        return array + self.token.astype(array.dtype).reshape((1,) * array.ndim)

    def call(self, run, scalars, operands, specs, out_specs, out_shape, **options):
        waits, self.before = self.before, []
        if self.token is not None:
            waits = waits + [self.token]
        token_spec = pl.BlockSpec((1, 1), lambda i, *_: (0, 0))
        body = with_token(Timed(run, len(out_shape)), len(scalars) + len(operands), len(waits))
        *results, token = pl.pallas_call(
            body,
            grid_spec=pltpu.PrefetchScalarGridSpec(
                num_scalar_prefetch=len(scalars),
                grid=options.pop("grid"),
                in_specs=list(specs) + [pl.BlockSpec(memory_space=pl.ANY)] * len(waits),
                out_specs=list(out_specs) + [token_spec],
                scratch_shapes=options.pop("scratch_shapes", []),
            ),
            out_shape=list(out_shape) + [jax.ShapeDtypeStruct((1, 1), f32)],
            compiler_params=pltpu.CompilerParams(vmem_limit_bytes=56 * 1024 * 1024),
            cost_estimate=pl.CostEstimate(flops=0, bytes_accessed=0, transcendentals=0),
            **options,
        )(*scalars, *operands, *waits)
        self.token = token
        return results

    def mark(self, *arrays):
        self.before += arrays
        self.call(lambda *refs: None, [], [], [], [], [], grid=(1,), name="mark")


def whole_spec(array):
    return pl.BlockSpec(array.shape, lambda i, *_: (0,) * array.ndim)


def row_spec(block, cols, first, last, offset=0):
    return pl.BlockSpec((block, cols), lambda i, *_: (jnp.clip(i, first, last) - first + offset, 0))


def split_rows(source):
    return not isinstance(source[1], int)


def row_sources(sources, block, per_seq, step_of):
    arrays, specs, ways = [], [], []
    for side, source in enumerate(sources):
        first = side * per_seq
        model = source[0].shape[1]
        if split_rows(source):
            arrays += source
            specs += [pl.BlockSpec((block, model), lambda i, *_: (0, 0))] * 2
            ways.append(2)
        else:
            arrays.append(source[0])
            specs.append(
                pl.BlockSpec(
                    (block, model),
                    lambda i, *_, first=first, offset=source[1]: (
                        jnp.clip(step_of(i), first, first + per_seq - 1) - first + offset,
                        0,
                    ),
                )
            )
            ways.append(1)
    return arrays, specs, tuple(ways)


def row_outs(block, model, blocks, split, step_of):
    if split == 1:
        return [pl.BlockSpec((block, model), lambda i, *_: (step_of(i), 0))]
    return [pl.BlockSpec((block, model), lambda i, *_: (0, 0))] * 4


def forward_layer(when, own, other, starts, index, weights, dct, cosine, sine, state_in, part, parts, block):
    wq, bq, wu, bu, wo = weights
    model = wq.shape[0]
    seqs, count = starts.shape
    length = cosine.shape[0] // seqs // parts
    rows = length * seqs
    hidden = wu.shape[1]
    width = wo.shape[0] - hidden
    pairs = width // PAIR
    per_seq = length // block
    blocks = per_seq * seqs
    by_rows = lambda cols: pl.BlockSpec((block, cols), lambda i, *_: (i, 0))
    table = pl.BlockSpec(
        (block, PAIR),
        lambda i, *_: ((i // per_seq) * per_seq * parts + part * per_seq + lax.rem(i, per_seq), 0),
    )
    state_spec = pl.BlockSpec((1, pairs * PAIR, 2 * PAIR), lambda i, *_: (i // per_seq, 0, 0))
    state_rows = block // SUB * pairs * PAIR
    sources, source_specs, ways = row_sources((own, other), block, per_seq, lambda i: i)
    outs = row_outs(block, model, blocks, len(own) if split_rows(own) else 1, lambda i: i)
    return when.call(
        partial(forward_kernel, count, per_seq, part * length, (ways, len(outs))),
        [starts, index],
        [*sources, *weights, dct, cosine, sine, state_in],
        source_specs
            + [whole_spec(w) for w in (*weights, dct)]
            + [table, table, state_spec],
        [
                by_rows(model),
                by_rows(3 * width),
                by_rows(width + hidden),
                by_rows(width),
                by_rows(hidden),
                pl.BlockSpec((state_rows, 2 * PAIR), lambda i, *_: (i, 0)),
                state_spec,
                *outs,
            ],
        [
            jax.ShapeDtypeStruct((rows, model), bf16),
            jax.ShapeDtypeStruct((rows, 3 * width), bf16),
            jax.ShapeDtypeStruct((rows, width + hidden), bf16),
            jax.ShapeDtypeStruct((rows, width), bf16),
            jax.ShapeDtypeStruct((rows, hidden), bf16),
            jax.ShapeDtypeStruct((blocks * state_rows, 2 * PAIR), bf16),
            jax.ShapeDtypeStruct((seqs, pairs * PAIR, 2 * PAIR), f32),
            *[jax.ShapeDtypeStruct((rows // len(outs), model), bf16) for _ in outs],
        ],
        grid=(blocks,),
        scratch_shapes=[pltpu.VMEM((pairs * PAIR, 2 * PAIR), f32)],
        name="forward_layer",
    )


def backward_layer(
    when, own, other, starts, index, weights, dctt, cosine, sine, state_in, saved, part, parts, block
):
    wq, _, wu, _, wo = weights
    weights = (wq, wu, wo)
    model = wq.shape[0]
    seqs, count = starts.shape
    length = cosine.shape[0] // seqs // parts
    rows = length * seqs
    hidden = wu.shape[1]
    width = wo.shape[0] - hidden
    span = 3 * width + hidden
    pairs = width // PAIR
    per_seq = length // block
    blocks = per_seq * seqs
    by_rows = lambda cols: pl.BlockSpec((block, cols), lambda i, *_: (blocks - 1 - i, 0))

    def table_index(i, *_):
        at = blocks - 1 - i
        return (at // per_seq) * per_seq * parts + part * per_seq + lax.rem(at, per_seq), 0

    table = pl.BlockSpec((block, PAIR), table_index)
    state_spec = pl.BlockSpec(
        (1, pairs * PAIR, 2 * PAIR), lambda i, *_: ((blocks - 1 - i) // per_seq, 0, 0)
    )
    state_rows = block // SUB * pairs * PAIR
    back = lambda i: blocks - 1 - i
    sources, source_specs, ways = row_sources((own, other), block, per_seq, back)
    outs = row_outs(block, model, blocks, len(own) if split_rows(own) else 1, back)
    return when.call(
        partial(backward_kernel, count, per_seq, part * length, (ways, len(outs))),
        [starts, index],
        [*sources, *weights, dctt, cosine, sine, state_in, *saved],
        source_specs
            + [whole_spec(w) for w in (*weights, dctt)]
            + [
                table,
                table,
                state_spec,
                by_rows(3 * width),
                by_rows(width + hidden),
                by_rows(width),
                by_rows(hidden),
                pl.BlockSpec((state_rows, 2 * PAIR), lambda i, *_: (blocks - 1 - i, 0)),
            ],
        [
                by_rows(span),
                pl.BlockSpec((1, span), lambda i, *_: (0, 0)),
                state_spec,
                *outs,
            ],
        [
            jax.ShapeDtypeStruct((rows, span), bf16),
            jax.ShapeDtypeStruct((1, span), f32),
            jax.ShapeDtypeStruct((seqs, pairs * PAIR, 2 * PAIR), f32),
            *[jax.ShapeDtypeStruct((rows // len(outs), model), bf16) for _ in outs],
        ],
        grid=(blocks,),
        scratch_shapes=[
                pltpu.VMEM((pairs * PAIR, 2 * PAIR), f32),
                pltpu.VMEM((block, 2 * width), bf16),
                pltpu.VMEM((block, 2 * width), bf16),
                pltpu.VMEM((block, width), bf16),
            ],
        name="backward_layer",
    )


def out_weight_grad(when, cas, grads, index, length, block):
    parts = len(cas)
    per_side = length // block
    per_part = 2 * per_side
    steps = per_part * parts
    inner, model = cas[0].shape[1], grads[0][0][0].shape[1]
    rights, right_specs, ways = [], [], ()
    for p, pair in enumerate(grads):
        arrays, specs, count = row_sources(
            pair, block, per_side, lambda i, p=p: jnp.clip(i - p * per_part, 0, per_part - 1)
        )
        rights += arrays
        right_specs += specs
        ways += count
    return when.call(
        partial(out_weight_kernel, parts, steps, ways),
        [index],
        [*cas, *rights],
        [row_spec(block, inner, p * per_part, (p + 1) * per_part - 1) for p in range(parts)]
        + right_specs,
        [pl.BlockSpec((inner, model), lambda i, *_: (0, 0))],
        [jax.ShapeDtypeStruct((inner, model), bf16)],
        grid=(steps,),
        scratch_shapes=[pltpu.VMEM((inner, model), f32)],
        name="out_weight_grad",
    )


def in_weight_grad(when, xhs, dzs, db, columns, wq, wu, block, pieces):
    parts = len(xhs)
    per_part = xhs[0].shape[0] // block
    steps = per_part * parts
    model, span = xhs[0].shape[1], dzs[0].shape[1]
    rows_of = lambda cols: [
        row_spec(block, cols, p * per_part, (p + 1) * per_part - 1) for p in range(parts)
    ]
    per_piece = model // pieces
    return when.call(
        partial(in_weight_kernel, parts, steps, pieces),
        [],
        [*xhs, *dzs, db, columns, wq, wu],
        rows_of(model) + rows_of(span) + [whole_spec(a) for a in (db, columns, wq, wu)],
        [pl.BlockSpec((per_piece, span), lambda i, *_: (0, 0))] * pieces
        + [pl.BlockSpec((model, 128), lambda i, *_: (0, 0))],
        [jax.ShapeDtypeStruct((per_piece, span), bf16)] * pieces
        + [jax.ShapeDtypeStruct((model, 128), f32)],
        grid=(steps,),
        scratch_shapes=[pltpu.VMEM((model, span), f32)],
        name="in_weight_grad",
    )


def join_pair_kernel(keep0, got0, keep1, got1, mine, theirs):
    mine[...] = (keep0[...].astype(f32) + got0[...].astype(f32)).astype(bf16)
    theirs[...] = (keep1[...].astype(f32) + got1[...].astype(f32)).astype(bf16)


def end_forward_kernel(mine, got, base, dense_bias, down_bias, rows):
    biases = dense_bias[...].astype(f32) + down_bias[...].astype(f32)
    summed = mine[...].astype(f32) + got[...].astype(f32)
    rows[...] = (base[...].astype(f32) + (summed + biases)).astype(bf16)


def end_backward_kernel(mine, got, base, before, rows, low):
    normed_grad = mine[...].astype(f32) + got[...].astype(f32)
    rows_in = base[...].astype(f32)
    center = jnp.mean(rows_in, axis=-1, keepdims=True)
    shifted = rows_in - center
    spread = jnp.mean(shifted * shifted, axis=-1, keepdims=True)
    inverse = lax.rsqrt(spread + norm_eps)
    normal = shifted * inverse
    along = jnp.mean(normed_grad * normal, axis=-1, keepdims=True)
    level = jnp.mean(normed_grad, axis=-1, keepdims=True)
    total = before[...].astype(f32) + inverse * (normed_grad - level - normal * along)
    rows[...] = total
    low[...] = total.astype(bf16)


def fold_kernel(qkv_ref, up_ref, order_ref, columns_ref, ordered_ref, wq_ref, wu_ref):
    columns = columns_ref[...]
    ordered = dot(qkv_ref[...], order_ref[...])
    ordered_ref[...] = ordered.astype(bf16)
    wq_ref[...] = (columns[:, 0:1] * ordered).astype(bf16)
    wu_ref[...] = (columns[:, 1:2] * up_ref[...].astype(f32)).astype(bf16)


def fold_gains(when, qkv, up, order, columns):
    model, hidden = up.shape
    span = order.shape[1]
    rows = min(256, model)
    by_rows = lambda cols: pl.BlockSpec((rows, cols), lambda i, *_: (i, 0))
    return when.call(
        fold_kernel,
        [],
        [qkv, up, order, columns],
        [by_rows(qkv.shape[1]), by_rows(hidden), whole_spec(order), by_rows(columns.shape[1])],
        [by_rows(span), by_rows(span), by_rows(hidden)],
        [
            jax.ShapeDtypeStruct((model, span), bf16),
            jax.ShapeDtypeStruct((model, span), bf16),
            jax.ShapeDtypeStruct((model, hidden), bf16),
        ],
        grid=(model // rows,),
        name="fold_gains",
    )


def by_blocks(when, kernel, sets, small, types, name):
    rows, cols = sets[0][0].shape
    block = min(256, rows)
    spec = pl.BlockSpec((block, cols), lambda i, *_: (i, 0))
    each, made = len(sets[0]), len(types)

    def body(*refs):
        ins, outs = refs[: len(sets) * each + len(small)], refs[len(sets) * each + len(small) :]
        for j in range(len(sets)):
            kernel(
                *ins[j * each : (j + 1) * each],
                *ins[len(sets) * each :],
                *outs[j * made : (j + 1) * made],
            )

    results = when.call(
        body,
        [],
        [a for one in sets for a in one] + list(small),
        [spec] * (len(sets) * each) + [whole_spec(a) for a in small],
        [spec] * (len(sets) * made),
        [jax.ShapeDtypeStruct((rows, cols), t) for _ in sets for t in types],
        grid=(rows // block,),
        name=name,
    )
    return [results[j * made : (j + 1) * made] for j in range(len(sets))]


def join_halves(when, items):
    scalars, operands, specs, outs, shapes, count = [], [], [], [], [], []
    for j, (now, bit, got, after_bit) in enumerate(items):
        half, cols = got.shape
        block = half // 2
        scalars += [jnp.int32(0) if bit is None else bit, jnp.int32(0) if after_bit is None else after_bit]

        def chosen(g, table, j=j, split=after_bit is not None):
            return jnp.where(g == 0, table[2 * j + 1], 1 - table[2 * j + 1]) if split else g

        def now_index(g, table, j=j, chosen=chosen, whole=bit is not None):
            at = chosen(g, table)
            return (table[2 * j] * 2 + at if whole else at), 0

        def got_index(g, table, chosen=chosen):
            return chosen(g, table), 0

        operands += [now, got]
        specs += [pl.BlockSpec((block, cols), now_index), pl.BlockSpec((block, cols), got_index)]
        if after_bit is None:
            outs.append(pl.BlockSpec((block, cols), lambda g, table: (g, 0)))
            shapes.append(jax.ShapeDtypeStruct((half, cols), bf16))
            count.append(1)
        else:
            outs += [pl.BlockSpec((block, cols), lambda g, table: (0, 0))] * 2
            shapes += [jax.ShapeDtypeStruct((block, cols), bf16)] * 2
            count.append(2)

    def kernel(table_ref, *refs):
        ins, made = refs[: 2 * len(items)], refs[2 * len(items) :]
        step = pl.program_id(0)
        at = 0
        for j, outputs in enumerate(count):
            total = (ins[2 * j][...].astype(f32) + ins[2 * j + 1][...].astype(f32)).astype(bf16)
            if outputs == 1:
                made[at][...] = total
            else:
                for side in range(2):

                    @pl.when(step == side)
                    def _():
                        made[at + side][...] = total

            at += outputs

    results = when.call(
        kernel, [jnp.stack(scalars).astype(jnp.int32)], operands, specs, outs, shapes, grid=(2,), name="join_halves"
    )
    grouped, at = [], 0
    for outputs in count:
        grouped.append(results[at : at + outputs])
        at += outputs
    return grouped


def assemble(when, pieces, own):
    rows, cols = pieces[0].shape
    count = len(pieces)

    def kernel(own_ref, *refs):
        ins, out = refs[:count], refs[count]
        key = jnp.bitwise_xor(pl.program_id(0), own_ref[0])
        for m in range(count):

            @pl.when(key == m)
            def _():
                out[...] = ins[m][...]

    return when.call(
        kernel,
        [jnp.reshape(own, (1,)).astype(jnp.int32)],
        list(pieces),
        [whole_spec(p) for p in pieces],
        [pl.BlockSpec((rows, cols), lambda i, *_: (i, 0))],
        [jax.ShapeDtypeStruct((rows * count, cols), bf16)],
        grid=(count,),
        name="assemble",
    )[0]


def finish_sums(when, held, constants, emit, shapes, name):
    layers = len(held)
    owns, operands, places = [], [], []
    for l, arrays in enumerate(held):
        first = 0
        for pieces, own in arrays:
            for m, piece in enumerate(pieces):
                operands.append(piece)
                places.append((l, len(owns), m, first))
            owns.append(own)
            first += piece.shape[0] * len(pieces)
    cols = operands[0].shape[1]

    def kernel(own_ref, *refs):
        ins = refs[: len(operands)]
        fixed = refs[len(operands) : len(operands) + len(constants)]
        outs, rows_ref = refs[len(operands) + len(constants) : -1], refs[-1]
        step = pl.program_id(0)
        for ref, (l, j, m, start) in zip(ins, places):
            count = ref.shape[0]

            @pl.when(step == l)
            def _():
                place = start + jnp.bitwise_xor(own_ref[j], m) * count
                rows_ref[pl.ds(pl.multiple_of(place, 16), count), :] = ref[...]

        emit(rows_ref, fixed, outs)

    return when.call(
        kernel,
        [jnp.stack([jnp.asarray(o, jnp.int32) for o in owns])],
        operands + list(constants),
        [whole_spec(a) for a in operands + list(constants)],
        [pl.BlockSpec((1,) + shape, lambda i, *_: (i, 0, 0)) for shape in shapes],
        [jax.ShapeDtypeStruct((layers,) + shape, f32) for shape in shapes],
        grid=(layers,),
        scratch_shapes=[pltpu.VMEM((first, cols), bf16)],
        name=name,
    )


def swapped(array, axis, distance):
    size = lax.axis_size(axis)
    return lax.ppermute(array, axis, [(i, i ^ distance) for i in range(size)])


def distances(size):
    return [1 << b for b in range(size.bit_length() - 1)]


def bit_of(axis, distance):
    return (lax.axis_index(axis) // distance) % 2


def joined(array, axis, distance):
    partner = swapped(array, axis, distance)
    upper = bit_of(axis, distance) == 1
    return jnp.concatenate(
        [jnp.where(upper, partner, array), jnp.where(upper, array, partner)], axis=0
    )


def gather_inner(rows, inner):
    for distance in distances(inner):
        rows = joined(rows, "tensor", distance)
    return rows


def inner_source(rows, inner):
    if inner == 2:
        return (rows, swapped(rows, "tensor", 1))
    return (gather_inner(rows, inner), 0)


def reduce_start(partial_sums, inner, when):
    if len(partial_sums) == 4:
        keep0, send0, keep1, send1 = partial_sums
        when.before += [send0, send1]
        return [keep0, keep1], [swapped(send0, "tensor", 1), swapped(send1, "tensor", 1)]
    now = jnp.split(partial_sums[0], 2)
    for distance in reversed(distances(inner)):
        half = now[0].shape[0] // 2
        bit = bit_of("tensor", distance)
        keep = [lax.dynamic_slice_in_dim(one, bit * half, half, 0) for one in now]
        send = [lax.dynamic_slice_in_dim(one, (1 - bit) * half, half, 0) for one in now]
        got = [swapped(one, "tensor", distance) for one in send]
        if distance > 1:
            (now,) = reduce_join([(keep, got)], when)
    return keep, got


def reduce_join(pending, when):
    return by_blocks(
        when,
        join_pair_kernel,
        [[keep[0], got[0], keep[1], got[1]] for keep, got in pending],
        [],
        [bf16, bf16],
        "join_pair",
    )


def sum_over_dp(arrays, orders, when, whole=False):
    nows, gots, wholes = list(arrays), [], []
    for array, order in zip(arrays, orders):
        half = array.shape[0] // 2
        bit = bit_of("dp", order[0])
        send = lax.dynamic_slice_in_dim(array, (1 - bit) * half, half, 0)
        when.before.append(send)
        gots.append(swapped(send, "dp", order[0]))
        wholes.append(bit)
    yield
    for stage in range(1, len(orders[0])):
        halving = stage < len(orders[0]) - 1
        items = [
            (now, whole, got, bit_of("dp", order[stage]) if halving else None)
            for now, whole, got, order in zip(nows, wholes, gots, orders)
        ]
        made = join_halves(when, items)
        nows = [one[0] for one in made]
        gots = [swapped(one[-1], "dp", order[stage]) for one, order in zip(made, orders)]
        wholes = [None] * len(nows)
        yield
    items = [(now, None, got, None) for now, got in zip(nows, gots)]
    nows = [one[0] for one in join_halves(when, items)]
    held = []
    for now, order in zip(nows, orders):
        pieces = {0: now}
        kept = order[:-1]
        for j in reversed(range(len(kept))):
            key = 1 << (len(kept) - 1 - j)
            pieces.update(
                {m | key: swapped(p, "dp", kept[j]) for m, p in list(pieces.items())}
            )
        held.append(pieces)
    yield
    results = []
    for pieces, order in zip(held, orders):
        kept = order[:-1]
        own = sum(bit_of("dp", d) * (1 << (len(kept) - 1 - j)) for j, d in enumerate(kept))
        pieces = [pieces[m] for m in range(len(pieces))]
        if whole:
            pieces, own = [assemble(when, pieces, own)], 0
        results.append((pieces, own))
    return results


class Sum:
    def __init__(self, arrays, orders, when, whole=False):
        self.run = sum_over_dp(arrays, orders, when, whole)
        self.value = None
        self.step()

    def step(self):
        if self.value is None:
            try:
                next(self.run)
            except StopIteration as stop:
                self.value = stop.value

    def finish(self):
        while self.value is None:
            self.step()
        return self.value


def small_sum(array, axes):
    for axis in axes:
        for distance in distances(lax.axis_size(axis)):
            array = array + swapped(array, axis, distance)
    return array


def to_shares(rows, inner, parts):
    half = rows.shape[0] // 2
    if inner == 2 and parts == 2:
        upper = bit_of("tensor", 1)
        send = lax.dynamic_slice_in_dim(rows, (1 - upper) * half, half, 0)
        got = swapped(send, "tensor", 1)
        return [jnp.where(upper == 1, got, rows[:half]), jnp.where(upper == 1, rows[half:], got)]
    whole = gather_inner(rows, inner)
    part_rows = whole.shape[0] // parts
    share = part_rows // inner
    first = lax.rem(lax.axis_index("tensor"), inner) * share
    return [
        lax.dynamic_slice_in_dim(whole, part * part_rows + first, share, 0)
        for part in range(parts)
    ]


def to_placement(shares, inner):
    parts = len(shares)
    if inner == 2 and parts == 2:
        upper = bit_of("tensor", 1) == 1
        mine = jnp.where(upper, shares[1], shares[0])
        theirs = jnp.where(upper, shares[0], shares[1])
        got = swapped(theirs, "tensor", 1)
        return jnp.concatenate([jnp.where(upper, got, mine), jnp.where(upper, mine, got)], axis=0)
    whole = jnp.concatenate([gather_inner(rows, inner) for rows in shares], axis=0)
    rows = whole.shape[0] // inner
    index = lax.rem(lax.axis_index("tensor"), inner)
    return lax.dynamic_slice_in_dim(whole, index * rows, rows, 0)


def on_device(
    tokens,
    doc_starts,
    norm_gains,
    norm_shifts,
    qkv_weight,
    qkv_bias,
    dense_weight,
    dense_bias,
    up_weight,
    up_bias,
    down_weight,
    down_bias,
    out_grad,
):
    layers = qkv_weight.shape[0]
    seqs = doc_starts.shape[0]
    model = tokens.shape[1]
    size = lax.axis_size("tensor")
    inner = size // seqs
    index = lax.axis_index("tensor")
    inner_index = lax.rem(index, inner)
    length = tokens.shape[0] * inner
    heads = qkv_weight.shape[2] // (3 * HS)
    padded = heads + heads % 2
    width = padded * HS
    group = 2 * PAIR if padded % 4 == 0 else PAIR
    parts = PARTS
    part_rows = length // parts
    share = part_rows // inner
    block = share if inner == 2 else min(512, part_rows)
    per_part = part_rows // block
    dp_size = lax.axis_size("dp")
    early_x = distances(dp_size)
    late_x = early_x[1:] + early_x[:1]

    when = Order()
    order = jnp.asarray(column_order(heads), bf16)
    feature = feature_matrix(group)
    dct = jnp.asarray(feature, bf16)
    dctt = jnp.asarray(feature.T, bf16)
    starts = jnp.where(index < inner, doc_starts, doc_starts[::-1])
    cosine, sine = rotary_tables(starts, length)
    zero_state = jnp.zeros((seqs, padded // 2 * PAIR, 2 * PAIR), f32)
    gains = norm_gains.astype(f32)
    shifts = norm_shifts.astype(f32)

    last = layers - 1
    place = jnp.full((1,), inner_index, jnp.int32)

    xs = to_shares(tokens, inner, parts)
    columns = [
        jnp.stack([gains[l, 0], gains[l, 1], shifts[l, 0], shifts[l, 1]], axis=1)
        for l in range(layers)
    ]

    def fold(l):
        qkv, up, dense, down = qkv_weight[l], up_weight[l], dense_weight[l], down_weight[l]
        ordered, wq, wu = fold_gains(when, qkv, up, order, columns[l])
        bias_one = dot(norm_shifts[l, 0:1], qkv) + qkv_bias[l].astype(f32)[None]
        bq = jnp.dot(bias_one, order.astype(f32), precision=lax.Precision.HIGHEST)
        bu = dot(norm_shifts[l, 1:2], up) + up_bias[l].astype(f32)[None]
        if padded != heads:
            dense = jnp.concatenate([dense, jnp.zeros((width - heads * HS, model), bf16)], axis=0)
        wo = jnp.concatenate([dense, down], axis=0)
        return (wq, bq, wu, bu, wo), ordered

    folded = [None] * layers
    when.before += [cosine, sine, *xs]
    folded[0] = fold(0)
    crossing_x = [swapped(xs[0], "tensor", inner), None]
    x_parts = [None] * parts
    x_parts[0] = (
        inner_source(xs[0], inner),
        inner_source(when.after(crossing_x[0]), inner),
    )
    when.mark(crossing_x[0])
    sent = when.after(xs[1])
    crossing_x[1] = swapped(sent, "tensor", inner)
    when.before.append(sent)

    inputs = [None] * layers
    saved = [[None] * parts for _ in range(layers)]
    sums = [[None] * parts for _ in range(layers)]

    def run_forward(l, part, state):
        own, other = x_parts[part]
        xh, qkv, ca, rden, gp, states, state, *out = forward_layer(
            when, own, other, starts, place, folded[l][0], dct, cosine, sine, state, part, parts, block
        )
        saved[l][part] = (xh, qkv, ca, rden, gp, states)
        sums[l][part] = out
        return state

    def begin_reduce(partial_sum):
        return reduce_start(partial_sum, inner, when)

    def cross_reduce(*pending):
        crossings = [
            (mine, swapped(theirs, "tensor", inner)) for mine, theirs in reduce_join(pending, when)
        ]
        return crossings if len(crossings) > 1 else crossings[0]

    def end_forward(l, ends):
        made = by_blocks(
            when,
            end_forward_kernel,
            [[*crossing, inputs[l][part]] for part, crossing in ends],
            [dense_bias[l : l + 1], down_bias[l : l + 1]],
            [bf16],
            "end_forward",
        )
        return [one[0] for one in made]

    def end_backward(l, ends):
        return by_blocks(
            when,
            end_backward_kernel,
            [[*crossing, inputs[l][part], incoming[part]] for part, crossing in ends],
            [],
            [f32, bf16],
            "end_backward",
        )

    def whole_part(share_rows, crossing):
        return inner_source(share_rows, inner), inner_source(when.after(crossing), inner)

    def send_across(rows):
        when.before.append(rows)
        return swapped(rows, "tensor", inner)

    out_grad_shares = to_shares(out_grad, inner, parts)
    incoming = out_grad_shares
    grads = [None] * parts
    crossing_grad = [None] * parts

    def send_out_grad(part):
        crossing_grad[part] = send_across(when.after(out_grad_shares[part]))

    for l in range(layers):
        inputs[l] = xs
        state = run_forward(l, 0, zero_state)
        if l < last:
            pending = begin_reduce(sums[l][0])
            if l == 0:
                x_parts[1] = whole_part(xs[1], crossing_x[1])
            crossing0 = cross_reduce(pending)
            state = run_forward(l, 1, state)
            pending = begin_reduce(sums[l][1])
            (x0,) = end_forward(l, [(0, crossing0)])
            far0 = send_across(x0)
            crossing1 = cross_reduce(pending)
            folded[l + 1] = fold(l + 1)
            x_parts = [whole_part(x0, far0), None]
            (x1,) = end_forward(l, [(1, crossing1)])
            far1 = send_across(x1)
            xs = [x0, x1]
        else:
            x_parts[1] = whole_part(xs[1], far1)
            send_out_grad(1)
            state = run_forward(l, 1, state)
            grads[1] = whole_part(out_grad_shares[1], crossing_grad[1])
            send_out_grad(0)

    small = [None] * layers
    weight_sums = [None] * layers

    def run_backward(l, part, state):
        own, other = grads[part]
        xh, qkv, ca, rden, gp, states = saved[l][part]
        kept = (qkv, ca, rden, gp, states)
        dz, db, state, *dx = backward_layer(
            when,
            own,
            other,
            starts,
            place,
            folded[l][0],
            dctt,
            cosine,
            sine,
            state,
            kept,
            part,
            parts,
            block,
        )
        return dz, dx, db, state

    def out_weights(l):
        return out_weight_grad(
            when, [kept[2] for kept in saved[l]], grads, place, part_rows, block
        )[0]

    def in_weights(l, dzs, dbs, bias_grad, pieces):
        db = sum(dbs)
        *made, norm_sums = in_weight_grad(
            when,
            [kept[0] for kept in saved[l]],
            dzs,
            db,
            columns[l],
            folded[l][1],
            up_weight[l],
            block,
            pieces,
        )
        small[l] = (jnp.concatenate([norm_sums[:, :4].T, bias_grad], axis=0), db)
        return made

    running = []

    def advance():
        for one in running:
            one.step()

    def bias_sum():
        return sum(
            jnp.sum(rows.astype(bf16).astype(f32), axis=0, keepdims=True) for rows in incoming
        )

    for l in reversed(range(layers)):
        bias_grad = bias_sum()
        dz1, dx1, db1, state = run_backward(l, 1, zero_state)
        if l == last:
            grads[0] = whole_part(out_grad_shares[0], crossing_grad[0])
        else:
            grads[0] = whole_part(far0[0], far0[1])
        if l > 0:
            pending1 = begin_reduce(dx1)
            out_sum = Sum([out_weights(l)], [early_x], when, True)
            running.append(out_sum)
            crossing1 = cross_reduce(pending1)
            dz0, dx0, db0, state = run_backward(l, 0, state)
            ((g1, low1),) = end_backward(l, [(1, crossing1)])
            far1 = send_across(low1)
            pending0 = begin_reduce(dx0)
            advance()
            crossing0 = cross_reduce(pending0)
            made = in_weights(l, [dz0, dz1], [db0, db1], bias_grad, 1)
            advance()
            grads = [None, whole_part(low1, far1)]
            in_sum = Sum(made, [early_x], when, True)
            running.append(in_sum)
            weight_sums[l] = (out_sum, in_sum)
            ((g0, low0),) = end_backward(l, [(0, crossing0)])
            far0 = (low0, send_across(low0))
            incoming = [g0, g1]
        else:
            advance()
            out_sum = Sum([out_weights(l)], [early_x], when)
            advance()
            running.append(out_sum)
            dz0, dx0, db0, state = run_backward(l, 0, state)
            advance()
            made = in_weights(l, [dz0, dz1], [db0, db1], bias_grad, 2)
            final = Sum(made, [early_x, late_x], when)
            weight_sums[l] = (out_sum, final)

    norm_rows = jnp.concatenate([one[0] for one in small], axis=0)
    span = small[0][1].shape[1]
    norm_rows = jnp.pad(norm_rows, ((0, 0), (0, max(span - model, 0))))
    bias_rows = jnp.concatenate([one[1] for one in small], axis=0)
    bias_rows = jnp.pad(bias_rows, ((0, 0), (0, max(model - span, 0))))
    small_rows = jnp.concatenate([norm_rows, bias_rows], axis=0)
    small_exchanges = [("dp", d) for d in distances(dp_size)]
    small_exchanges += [("tensor", d) for d in distances(size)]

    def small_steps(rows):
        for axis, distance in small_exchanges:
            sent = when.after(rows)
            when.before.append(sent)
            got = swapped(sent, axis, distance)
            yield
            summed = when.after(rows + got)
            if axis == "tensor":
                summed = jnp.concatenate([summed[: 5 * layers], rows[5 * layers :]], axis=0)
            rows = summed
        yield rows

    small_run = small_steps(small_rows)

    pending = [begin_reduce(one) for one in (dx0, dx1)]
    advance()
    crossing = cross_reduce(*pending)
    next(small_run)
    final.step()
    next(small_run)
    pending = [begin_reduce(one) for one in sums[last]]
    out_crossing = cross_reduce(*pending)
    advance()
    final.step()
    next(small_run)
    incoming = [one[0] for one in end_backward(0, list(enumerate(crossing)))]
    tokens_grad = to_placement(incoming, inner)
    advance()
    final.step()
    next(small_run)
    results = end_forward(last, list(enumerate(out_crossing)))
    result = to_placement(results, inner)
    while any(one.value is None for one in running):
        advance()
    for small_rows in small_run:
        pass
    def emit_out(rows_ref, fixed, outs):
        outs[0][0] = rows_ref[: heads * HS, :].astype(f32)
        outs[1][0] = rows_ref[width:, :].astype(f32)

    def emit_in(rows_ref, fixed, outs):
        outs[0][0] = dot_nt(rows_ref[:, : 3 * width], fixed[0][...])
        outs[1][0] = rows_ref[:, 3 * width :].astype(f32)

    hidden_size = up_weight.shape[2]
    when.before.append(tokens_grad)
    dense_total, down_total = finish_sums(
        when,
        [sums_of[0].finish() for sums_of in weight_sums],
        [],
        emit_out,
        [(heads * HS, model), (hidden_size, model)],
        "finish_out",
    )
    when.before.append(result)
    qkv_total, up_total = finish_sums(
        when,
        [sums_of[1].finish() for sums_of in weight_sums],
        [order],
        emit_in,
        [(model, heads * 3 * HS), (model, hidden_size)],
        "finish_in",
    )
    bias_rows = small_rows[5 * layers :, :span]
    norm_rows = small_rows[: 5 * layers, :model].reshape(layers, 5, model)

    bias_total = norm_rows[:, 4]
    bias_one = bias_rows[:, : 3 * width]
    return (
        result,
        tokens_grad,
        norm_rows[:, 0:2],
        norm_rows[:, 2:4],
        qkv_total,
        jnp.dot(bias_one, order.astype(f32).T, precision=lax.Precision.HIGHEST),
        dense_total,
        bias_total,
        up_total,
        bias_rows[:, 3 * width :],
        down_total,
        bias_total,
    )


def solution(mesh):
    return jax.shard_map(
        on_device,
        mesh=mesh,
        in_specs=(
            P(("dp", "tensor"), None),
            P("dp", None),
            P(),
            P(),
            P(None, None, "tensor"),
            P(None, "tensor"),
            P(None, "tensor", None),
            P(),
            P(None, None, "tensor"),
            P(None, "tensor"),
            P(None, "tensor", None),
            P(),
            P(("dp", "tensor"), None),
        ),
        out_specs=(
            P(("dp", "tensor"), None),
            P(("dp", "tensor"), None),
            P(),
            P(),
            P(None, None, "tensor"),
            P(None, "tensor"),
            P(None, "tensor", None),
            P(),
            P(None, None, "tensor"),
            P(None, "tensor"),
            P(None, "tensor", None),
            P(),
        ),
        check_vma=False,
    )
```

```python
from functools import partial
import math

import numpy as np
import jax
import jax.numpy as jnp
from jax import lax
from jax.experimental import pallas as pl
from jax.experimental.pallas import tpu as pltpu
from jax.sharding import PartitionSpec as P

HS = 64
FEATS = 64
ROT = 16
PAIR = 2 * HS
SUB = 128
HIDDEN_CHUNK = 256
PARTS = 2

norm_eps = 1e-05
feature_scale = 0.75
rotary_base = 10000.0

f32 = jnp.float32
bf16 = jnp.bfloat16
NT = (((1,), (1,)), ((), ()))
TN = (((0,), (0,)), ((), ()))


def pair_order():
    half = ROT // 2
    rest = (HS - ROT) // 2
    order = []
    for side in range(2):
        for head in range(2):
            order += [(head, side * half + i) for i in range(half)]
        for head in range(2):
            order += [(head, ROT + side * rest + i) for i in range(rest)]
    return order


def column_order(heads):
    padded = heads + heads % 2
    width = padded * HS
    matrix = np.zeros((heads * 3 * HS, 3 * width), np.float32)
    order = pair_order()
    for pair in range(padded // 2):
        for lane, (side, entry) in enumerate(order):
            head = 2 * pair + side
            if head < heads:
                for part in range(2):
                    matrix[head * 3 * HS + part * HS + entry, part * width + pair * PAIR + lane] = 1
    for head in range(heads):
        for entry in range(HS):
            matrix[head * 3 * HS + 2 * HS + entry, 2 * width + head * HS + entry] = 1
    return matrix


def feature_matrix(group):
    rows = np.arange(FEATS)[:, None]
    cols = np.arange(HS)[None, :]
    table = np.cos(np.pi * (cols + 0.5) * rows / HS) * np.sqrt(2.0 / HS)
    table = table * np.where(rows == 0, np.sqrt(0.5), 1.0) * feature_scale
    matrix = np.zeros((group, group), np.float32)
    for pair in range(group // PAIR):
        for lane, (side, entry) in enumerate(pair_order()):
            start = pair * PAIR + side * FEATS
            matrix[pair * PAIR + lane, start : start + FEATS] = table[:, entry]
    return matrix


def rotary_tables(starts, length):
    places = jnp.arange(length, dtype=jnp.int32)
    started = starts[:, :, None] <= places[None, None, :]
    latest = jnp.max(jnp.where(started, starts[:, :, None], 0), axis=1)
    offsets = (places[None, :] - latest).reshape(1, -1).astype(f32)
    half = ROT // 2
    inverse = rotary_base ** (-(jnp.arange(half, dtype=f32) * 2.0 / ROT))
    angles = inverse[:, None] * offsets
    cos_lanes = np.zeros((half, PAIR), np.float32)
    sin_lanes = np.zeros((half, PAIR), np.float32)
    plain = np.zeros((1, PAIR), np.float32)
    for lane, (_, entry) in enumerate(pair_order()):
        if entry < ROT:
            cos_lanes[entry % half, lane] = 1.0
            sin_lanes[entry % half, lane] = -1.0 if entry < half else 1.0
        else:
            plain[0, lane] = 1.0

    def spread(table, lanes):
        return lax.dot_general(
            table, jnp.asarray(lanes), TN, precision=lax.Precision.HIGHEST
        )

    cosine = spread(jnp.cos(angles), cos_lanes) + jnp.asarray(plain)
    return cosine, spread(jnp.sin(angles), sin_lanes)


def dot(a, b):
    return jnp.dot(a, b, preferred_element_type=f32)


def dot_nt(a, b):
    return lax.dot_general(a, b, NT, preferred_element_type=f32)


def latest_start(starts_ref, seq, count, places):
    latest = jnp.zeros_like(places)
    for j in range(count):
        start = starts_ref[seq, j]
        latest = jnp.maximum(latest, jnp.where(start <= places, start, 0))
    return latest


def latest_scalar(starts_ref, seq, count, place):
    latest = jnp.int32(0)
    for j in range(count):
        start = starts_ref[seq, j]
        latest = jnp.maximum(latest, jnp.where(start <= place, start, 0))
    return latest


def block_masks(starts_ref, seq, count, place):
    rows = place + lax.broadcasted_iota(jnp.int32, (SUB, SUB), 0)
    cols = place + lax.broadcasted_iota(jnp.int32, (SUB, SUB), 1)
    latest_rows = latest_start(starts_ref, seq, count, rows)
    allowed = (cols <= rows) & (cols >= latest_rows)
    carried = (latest_rows <= place).astype(f32)
    following = latest_scalar(starts_ref, seq, count, place + SUB)
    feeding = (rows >= following).astype(f32)
    keeping = jnp.where(following <= place, 1.0, 0.0).astype(f32)
    return rows, cols, allowed, carried, feeding, keeping


def gelu_parts(hidden):
    share = 0.5 + 0.5 * lax.erf(hidden * math.sqrt(0.5))
    bell = jnp.exp(hidden * hidden * -0.5)
    return hidden * share, share + hidden * (bell * (1.0 / math.sqrt(2.0 * math.pi)))


def lane_halves():
    lane = lax.broadcasted_iota(jnp.int32, (SUB, PAIR), 1)
    low = (lane < HS).astype(f32).astype(bf16)
    return low, 1 - low


def pick_rows(seq, within, index, refs):
    values = []
    for one in refs:
        if len(one) == 1:
            values.append(one[0][...])
        else:
            values.append(jnp.where(within == index, one[0][...], one[1][...]))
    return jnp.where(seq == 0, values[0], values[1])


def place_rows(seq, within, index, rows, refs):
    if len(refs) == 1:
        refs[0][...] = rows
        return
    for side in range(2):
        for sent in range(2):

            @pl.when((seq == side) & ((within == index) == (sent == 0)))
            def _():
                refs[2 * side + sent][...] = rows


def forward_kernel(
    count,
    blocks_per_seq,
    first_place,
    shapes,
    starts_ref,
    index_ref,
    *refs,
):
    ways, rest = shapes
    sources = (refs[: ways[0]], refs[ways[0] : sum(ways)])
    outs = refs[sum(ways) + 16 : sum(ways) + 16 + rest]
    forward_body(
        count,
        blocks_per_seq,
        first_place,
        starts_ref,
        index_ref[0],
        sources,
        outs,
        *refs[sum(ways) : sum(ways) + 16],
        *refs[sum(ways) + 16 + rest :],
    )


def forward_body(
    count,
    blocks_per_seq,
    first_place,
    starts_ref,
    index,
    sources,
    outs,
    wq_ref,
    bq_ref,
    wu_ref,
    bu_ref,
    wo_ref,
    dct_ref,
    cos_ref,
    sin_ref,
    state_in_ref,
    xh_ref,
    qkv_ref,
    ca_ref,
    rden_ref,
    gp_ref,
    states_ref,
    state_out_ref,
    state_ref,
):
    step = pl.program_id(0)
    seq = step // blocks_per_seq
    within = lax.rem(step, blocks_per_seq)
    rows = sources[0][0].shape[0]
    inner = wu_ref.shape[1]
    width = wo_ref.shape[0] - inner
    pairs = width // PAIR
    group = dct_ref.shape[0]

    @pl.when(within == 0)
    def _():
        state_ref[...] = state_in_ref[0]

    x = pick_rows(seq, within, index, sources).astype(f32)
    center = jnp.mean(x, axis=-1, keepdims=True)
    shifted = x - center
    spread = jnp.mean(shifted * shifted, axis=-1, keepdims=True)
    xh = (shifted * lax.rsqrt(spread + norm_eps)).astype(bf16)
    xh_ref[...] = xh

    cosine = cos_ref[...]
    sine = sin_ref[...]
    dct = dct_ref[...]
    mixed = dot(xh, wq_ref[...]) + bq_ref[...]
    for start in range(0, 2 * width, group):
        turned = []
        for lane in range(start, start + group, PAIR):
            tile = mixed[:, lane : lane + PAIR]
            turned.append((tile * cosine + pltpu.roll(tile, HS, 1) * sine).astype(bf16))
        turned = turned[0] if len(turned) == 1 else jnp.concatenate(turned, axis=1)
        qkv_ref[:, start : start + group] = jnp.exp(dot(turned, dct)).astype(bf16)
    qkv_ref[:, 2 * width :] = mixed[:, 2 * width :].astype(bf16)

    low_lanes = lax.broadcasted_iota(jnp.int32, (SUB, PAIR), 1) < HS
    low, high = lane_halves()
    ones = jnp.ones((SUB, PAIR), bf16)
    active, slope = gelu_parts(dot(xh, wu_ref[...]) + bu_ref[...])
    ca_ref[:, width:] = active.astype(bf16)
    gp_ref[...] = slope.astype(bf16)

    for sub in range(rows // SUB):
        place = first_place + within * rows + sub * SUB
        _, _, allowed, carried, feeding, keeping = block_masks(starts_ref, seq, count, place)
        carried = carried.astype(bf16)
        feeding = feeding.astype(bf16)
        at = slice(sub * SUB, (sub + 1) * SUB)
        for pair in range(pairs):
            lanes = slice(pair * PAIR, (pair + 1) * PAIR)
            q = qkv_ref[at, pair * PAIR : (pair + 1) * PAIR]
            k = qkv_ref[at, width + pair * PAIR : width + (pair + 1) * PAIR]
            v = qkv_ref[at, 2 * width + pair * PAIR : 2 * width + (pair + 1) * PAIR]
            q0, q1 = q * low, q * high
            qs = jnp.concatenate([q0, q1], axis=0)
            scores = dot_nt(qs, k)
            weights = [
                jnp.where(allowed, scores[:SUB], 0.0).astype(bf16),
                jnp.where(allowed, scores[SUB:], 0.0).astype(bf16),
            ]
            state = state_ref[pair * PAIR : (pair + 1) * PAIR, :]
            state_low = state.astype(bf16)
            first = (sub * pairs + pair) * PAIR
            states_ref[first : first + PAIR, :] = state_low
            left = jnp.concatenate(
                [
                    jnp.concatenate([weights[0], q0 * carried], axis=1),
                    jnp.concatenate([weights[1], q1 * carried], axis=1),
                ],
                axis=0,
            )
            valued = jnp.concatenate([v, ones], axis=1)
            both = dot(left, jnp.concatenate([valued, state_low], axis=0))
            numerator = jnp.where(low_lanes, both[:SUB, :PAIR], both[SUB:, :PAIR])
            denominator = jnp.where(low_lanes, both[:SUB, PAIR:], both[SUB:, PAIR:])
            inverse = 1.0 / denominator
            ca_ref[at, lanes] = (numerator * inverse).astype(bf16)
            rden_ref[at, lanes] = inverse.astype(bf16)
            added = lax.dot_general(k * feeding, valued, TN, preferred_element_type=f32)
            state_ref[pair * PAIR : (pair + 1) * PAIR, :] = keeping * state + added

    out = dot(ca_ref[...], wo_ref[...]).astype(bf16)
    place_rows(seq, within, index, out, outs)

    @pl.when(within == blocks_per_seq - 1)
    def _():
        state_out_ref[0] = state_ref[...]


def backward_kernel(
    count,
    blocks_per_seq,
    first_place,
    shapes,
    starts_ref,
    index_ref,
    *refs,
):
    ways, rest = shapes
    sources = (refs[: ways[0]], refs[ways[0] : sum(ways)])
    outs = refs[sum(ways) + 15 : sum(ways) + 15 + rest]
    backward_body(
        count,
        blocks_per_seq,
        first_place,
        starts_ref,
        index_ref[0],
        sources,
        outs,
        *refs[sum(ways) : sum(ways) + 15],
        *refs[sum(ways) + 15 + rest :],
    )


def backward_body(
    count,
    blocks_per_seq,
    first_place,
    starts_ref,
    index,
    sources,
    outs,
    wq_ref,
    wu_ref,
    wo_ref,
    dctt_ref,
    cos_ref,
    sin_ref,
    state_in_ref,
    qkv_ref,
    ca_ref,
    rden_ref,
    gp_ref,
    states_ref,
    dz_ref,
    db_ref,
    state_out_ref,
    state_ref,
    dqk_ref,
    split_ref,
    dnum_ref,
):
    step = pl.program_id(0)
    blocks = pl.num_programs(0)
    seq = (blocks - 1 - step) // blocks_per_seq
    within = lax.rem(blocks - 1 - step, blocks_per_seq)
    rows = sources[0][0].shape[0]
    inner = wu_ref.shape[1]
    width = wo_ref.shape[0] - inner
    pairs = width // PAIR
    group = dctt_ref.shape[0]

    @pl.when(within == blocks_per_seq - 1)
    def _():
        state_ref[...] = state_in_ref[0]

    @pl.when(step == 0)
    def _():
        db_ref[...] = jnp.zeros_like(db_ref)

    bg = pick_rows(seq, within, index, sources)
    context_grad = dot_nt(bg, wo_ref[:width, :])

    low_rows = lax.broadcasted_iota(jnp.int32, (rows, PAIR), 1) < HS
    low_lanes = lax.broadcasted_iota(jnp.int32, (SUB, PAIR), 1) < HS
    low, high = lane_halves()
    ones = jnp.ones((SUB, PAIR), bf16)
    zeros = jnp.zeros((SUB, PAIR), bf16)
    sum_rows = lax.broadcasted_iota(jnp.int32, (2 * PAIR, 2 * PAIR), 0)
    sum_cols = lax.broadcasted_iota(jnp.int32, (2 * PAIR, 2 * PAIR), 1)
    same_head = (lax.rem(sum_rows, PAIR) // HS) == (sum_cols // PAIR)
    summing = jnp.where(same_head, -1.0 / HS, 0.0).astype(bf16)

    for pair in range(pairs):
        lanes = slice(pair * PAIR, (pair + 1) * PAIR)
        scaled = context_grad[:, lanes] * rden_ref[:, lanes].astype(f32)
        dnum_ref[:, lanes] = scaled.astype(bf16)
        product = scaled * ca_ref[:, lanes].astype(f32)
        product_high = product.astype(bf16)
        product_low = (product - product_high.astype(f32)).astype(bf16)
        dden = dot(jnp.concatenate([product_high, product_low], axis=1), summing)
        for side in range(2):
            part = dden[:, side * PAIR : (side + 1) * PAIR]
            top = part.astype(bf16).astype(f32)
            split = jnp.where(low_rows, part, part - top).astype(bf16)
            split_ref[:, (2 * pair + side) * PAIR : (2 * pair + side + 1) * PAIR] = split

    subs = rows // SUB
    chunk = min(inner, HIDDEN_CHUNK)
    chunks = inner // chunk
    done = 0

    def hidden_chunk(j):
        at = slice(j * chunk, (j + 1) * chunk)
        active_grad = dot_nt(bg, wo_ref[width + j * chunk : width + (j + 1) * chunk, :])
        grad = (active_grad * gp_ref[:, at].astype(f32)).astype(bf16)
        dz_ref[:, 3 * width + j * chunk : 3 * width + (j + 1) * chunk] = grad

    for sub in reversed(range(subs)):
        while done < (subs - sub) * chunks // subs:
            hidden_chunk(done)
            done += 1
        place = first_place + within * rows + sub * SUB
        rows_at, cols_at, allowed, carried, feeding, keeping = block_masks(
            starts_ref, seq, count, place
        )
        latest_cols = latest_start(starts_ref, seq, count, cols_at)
        flipped = (rows_at <= cols_at) & (rows_at >= latest_cols)
        carried_low = carried.astype(bf16)
        at = slice(sub * SUB, (sub + 1) * SUB)
        items = [dict(pair=pair) for pair in range(pairs)]
        for it in items:
            pair = it["pair"]
            it["q"] = qkv_ref[at, pair * PAIR : (pair + 1) * PAIR]
            it["k"] = qkv_ref[at, width + pair * PAIR : width + (pair + 1) * PAIR]
            it["v"] = qkv_ref[at, 2 * width + pair * PAIR : 2 * width + (pair + 1) * PAIR]
            it["dnum"] = dnum_ref[at, pair * PAIR : (pair + 1) * PAIR]
            it["split"] = [
                split_ref[at, (2 * pair + side) * PAIR : (2 * pair + side + 1) * PAIR]
                for side in range(2)
            ]
            first = (sub * pairs + pair) * PAIR
            it["state"] = states_ref[first : first + PAIR, :]
            it["later"] = state_ref[pair * PAIR : (pair + 1) * PAIR, :]
            it["later_low"] = it["later"].astype(bf16)
        for it in items:
            it["xs"] = jnp.concatenate(
                [
                    jnp.concatenate([it["dnum"] * low, it["split"][0]], axis=1),
                    jnp.concatenate([it["dnum"] * high, it["split"][1]], axis=1),
                ],
                axis=0,
            )
            valued = jnp.concatenate([it["v"], ones], axis=1)
            it["ahead"] = dot_nt(it["xs"], jnp.concatenate([valued, it["state"]], axis=0))
        for it in items:
            back = []
            for side, mask in enumerate((low, high)):
                back.append(
                    dot_nt(
                        jnp.concatenate([it["v"] * mask, ones], axis=1),
                        jnp.concatenate(
                            [
                                jnp.concatenate([it["dnum"], it["split"][side]], axis=1),
                                it["later_low"],
                            ],
                            axis=0,
                        ),
                    )
                )
            it["back"] = back
        for it in items:
            ks = jnp.concatenate([it["k"] * low, it["k"] * high], axis=0)
            it["q_turned"] = jnp.transpose(it["q"])
            it["over"] = dot(
                ks, jnp.concatenate([it["q_turned"], it["later_low"][:, :PAIR]], axis=1)
            )
        for it in items:
            qc = it["q"] * carried_low
            qs = jnp.concatenate([qc * low, qc * high], axis=0)
            added = lax.dot_general(qs, it["xs"], TN, preferred_element_type=f32)
            pair = it["pair"]
            state_ref[pair * PAIR : (pair + 1) * PAIR, :] = keeping * it["later"] + added
        for it in items:
            dscores = jnp.concatenate(
                [
                    jnp.where(allowed, it["ahead"][:SUB, :SUB], 0.0).astype(bf16),
                    jnp.where(allowed, it["ahead"][SUB:, :SUB], 0.0).astype(bf16),
                ],
                axis=0,
            )
            it["dq"] = dot(dscores, it["k"])
        for it in items:
            left = jnp.concatenate(
                [
                    jnp.concatenate(
                        [
                            jnp.where(flipped, it["back"][side][:, :SUB], 0.0).astype(bf16),
                            jnp.where(
                                flipped, it["over"][side * SUB : (side + 1) * SUB, :SUB], 0.0
                            ).astype(bf16),
                        ],
                        axis=1,
                    )
                    for side in range(2)
                ],
                axis=0,
            )
            right = jnp.concatenate(
                [
                    jnp.concatenate([it["q"], zeros], axis=1),
                    jnp.concatenate([zeros, it["dnum"]], axis=1),
                ],
                axis=0,
            )
            it["both"] = dot(left, right)
        for it in items:
            pair = it["pair"]
            dq, ahead, both, back, over = (
                it["dq"],
                it["ahead"],
                it["both"],
                it["back"],
                it["over"],
            )
            dq = (
                jnp.where(low_lanes, dq[:SUB], dq[SUB:])
                + jnp.where(low_lanes, ahead[:SUB, SUB:], ahead[SUB:, SUB:]) * carried
            )
            dk = (
                jnp.where(low_lanes, both[:SUB, :PAIR], both[SUB:, :PAIR])
                + jnp.where(low_lanes, back[0][:, SUB:], back[1][:, SUB:]) * feeding
            )
            dv = (
                jnp.where(low_lanes, both[:SUB, PAIR:], both[SUB:, PAIR:])
                + jnp.where(low_lanes, over[:SUB, SUB:], over[SUB:, SUB:]) * feeding
            )
            dqk_ref[at, pair * PAIR : (pair + 1) * PAIR] = (dq * it["q"].astype(f32)).astype(bf16)
            dqk_ref[at, width + pair * PAIR : width + (pair + 1) * PAIR] = (
                dk * it["k"].astype(f32)
            ).astype(bf16)
            dz_ref[at, 2 * width + pair * PAIR : 2 * width + (pair + 1) * PAIR] = dv.astype(bf16)

    cosine = cos_ref[...]
    sine = sin_ref[...]
    dctt = dctt_ref[...]
    for start in range(0, 2 * width, group):
        turned = dot(dqk_ref[:, start : start + group], dctt)
        for lane in range(0, group, PAIR):
            tile = turned[:, lane : lane + PAIR]
            back = tile * cosine - pltpu.roll(tile, HS, 1) * sine
            dz_ref[:, start + lane : start + lane + PAIR] = back.astype(bf16)

    dx = dot_nt(dz_ref[:, 3 * width :], wu_ref[...]) + dot_nt(dz_ref[:, : 3 * width], wq_ref[...])
    place_rows(seq, within, index, dx.astype(bf16), outs)
    db_ref[...] += jnp.sum(dz_ref[...].astype(f32), axis=0, keepdims=True)

    @pl.when(within == 0)
    def _():
        state_out_ref[0] = state_ref[...]


def out_weight_kernel(parts, steps, ways, index_ref, *refs):
    lefts = refs[:parts]
    rights, at = [], parts
    for count in ways:
        rights.append(refs[at : at + count])
        at += count
    grad_ref, total_ref = refs[at:]
    step = pl.program_id(0)
    per_part = steps // parts
    per_side = per_part // 2
    index = index_ref[0]

    @pl.when(step == 0)
    def _():
        total_ref[...] = jnp.zeros_like(total_ref)

    for part in range(parts):
        for side in range(2):
            first = part * per_part + side * per_side
            blocks = rights[2 * part + side]

            @pl.when((step >= first) & (step < first + per_side))
            def _():
                right = blocks[0][...]
                if len(blocks) == 2:
                    right = jnp.where(step - first == index, right, blocks[1][...])
                total_ref[...] += lax.dot_general(
                    lefts[part][...], right, TN, preferred_element_type=f32
                )

    @pl.when(step == steps - 1)
    def _():
        grad_ref[...] = total_ref[...].astype(bf16)


def in_weight_kernel(parts, steps, pieces, *refs):
    lefts, rights = refs[:parts], refs[parts : 2 * parts]
    db_ref, gains_ref, wq_ref, wu_ref = refs[2 * parts : 2 * parts + 4]
    grad_refs = refs[2 * parts + 4 : 2 * parts + 4 + pieces]
    sums_ref, total_ref = refs[2 * parts + 4 + pieces :]
    step = pl.program_id(0)
    per_part = steps // parts

    @pl.when(step == 0)
    def _():
        total_ref[...] = jnp.zeros_like(total_ref)

    for part in range(parts):

        @pl.when((step >= part * per_part) & (step < (part + 1) * per_part))
        def _():
            total_ref[...] += lax.dot_general(
                lefts[part][...], rights[part][...], TN, preferred_element_type=f32
            )

    @pl.when(step == steps - 1)
    def _():
        split = wq_ref.shape[1]
        rows = 128
        lane = lax.broadcasted_iota(jnp.int32, (rows, 128), 1)
        per_piece = total_ref.shape[0] // pieces
        for piece, grad_ref in enumerate(grad_refs):

            @pl.loop(0, per_piece // rows)
            def _(block):
                inside = pl.ds(pl.multiple_of(block * rows, rows), rows)
                at = pl.ds(pl.multiple_of(piece * per_piece + block * rows, rows), rows)
                columns = gains_ref[at, :]
                sums = jnp.zeros((rows, 128), f32)
                for j, (weight_ref, cols) in enumerate(
                    ((wq_ref, slice(0, split)), (wu_ref, slice(split, None)))
                ):
                    gain, shift = columns[:, j : j + 1], columns[:, 2 + j : 3 + j]
                    total = total_ref[at, cols]
                    bias = db_ref[:, cols]
                    weight = weight_ref[at, :].astype(f32)
                    grad_ref[inside, cols] = (gain * total + shift * bias).astype(bf16)
                    sums = sums + jnp.where(
                        lane == j, jnp.sum(weight * total, axis=1, keepdims=True), 0.0
                    )
                    sums = sums + jnp.where(
                        lane == 2 + j, jnp.sum(weight * bias, axis=1, keepdims=True), 0.0
                    )
                sums_ref[at, :] = sums


def with_token(kernel, inputs, waits):
    def body(*refs):
        outputs = refs[inputs + waits :]
        token_at = kernel.token
        outputs[token_at][...] = jnp.zeros_like(outputs[token_at])
        kernel.run(*refs[:inputs], *outputs[:token_at], *outputs[token_at + 1 :])

    return body


class Timed:
    def __init__(self, run, token):
        self.run = run
        self.token = token


class Order:
    def __init__(self):
        self.before = []
        self.token = None

    def after(self, array):
        if self.token is None:
            return array
        return array + self.token.astype(array.dtype).reshape((1,) * array.ndim)

    def call(self, run, scalars, operands, specs, out_specs, out_shape, **options):
        waits, self.before = self.before, []
        if self.token is not None:
            waits = waits + [self.token]
        token_spec = pl.BlockSpec((1, 1), lambda i, *_: (0, 0))
        body = with_token(Timed(run, len(out_shape)), len(scalars) + len(operands), len(waits))
        *results, token = pl.pallas_call(
            body,
            grid_spec=pltpu.PrefetchScalarGridSpec(
                num_scalar_prefetch=len(scalars),
                grid=options.pop("grid"),
                in_specs=list(specs) + [pl.BlockSpec(memory_space=pl.ANY)] * len(waits),
                out_specs=list(out_specs) + [token_spec],
                scratch_shapes=options.pop("scratch_shapes", []),
            ),
            out_shape=list(out_shape) + [jax.ShapeDtypeStruct((1, 1), f32)],
            compiler_params=pltpu.CompilerParams(vmem_limit_bytes=56 * 1024 * 1024),
            cost_estimate=pl.CostEstimate(flops=0, bytes_accessed=0, transcendentals=0),
            **options,
        )(*scalars, *operands, *waits)
        self.token = token
        return results

    def mark(self, *arrays):
        self.before += arrays
        self.call(lambda *refs: None, [], [], [], [], [], grid=(1,), name="mark")


def whole_spec(array):
    return pl.BlockSpec(array.shape, lambda i, *_: (0,) * array.ndim)


def row_spec(block, cols, first, last, offset=0):
    return pl.BlockSpec((block, cols), lambda i, *_: (jnp.clip(i, first, last) - first + offset, 0))


def split_rows(source):
    return not isinstance(source[1], int)


def row_sources(sources, block, per_seq, step_of):
    arrays, specs, ways = [], [], []
    for side, source in enumerate(sources):
        first = side * per_seq
        model = source[0].shape[1]
        if split_rows(source):
            arrays += source
            specs += [pl.BlockSpec((block, model), lambda i, *_: (0, 0))] * 2
            ways.append(2)
        else:
            arrays.append(source[0])
            specs.append(
                pl.BlockSpec(
                    (block, model),
                    lambda i, *_, first=first, offset=source[1]: (
                        jnp.clip(step_of(i), first, first + per_seq - 1) - first + offset,
                        0,
                    ),
                )
            )
            ways.append(1)
    return arrays, specs, tuple(ways)


def row_outs(block, model, blocks, split, step_of):
    if split == 1:
        return [pl.BlockSpec((block, model), lambda i, *_: (step_of(i), 0))]
    return [pl.BlockSpec((block, model), lambda i, *_: (0, 0))] * 4


def forward_layer(when, own, other, starts, index, weights, dct, cosine, sine, state_in, part, parts, block):
    wq, bq, wu, bu, wo = weights
    model = wq.shape[0]
    seqs, count = starts.shape
    length = cosine.shape[0] // seqs // parts
    rows = length * seqs
    hidden = wu.shape[1]
    width = wo.shape[0] - hidden
    pairs = width // PAIR
    per_seq = length // block
    blocks = per_seq * seqs
    by_rows = lambda cols: pl.BlockSpec((block, cols), lambda i, *_: (i, 0))
    table = pl.BlockSpec(
        (block, PAIR),
        lambda i, *_: ((i // per_seq) * per_seq * parts + part * per_seq + lax.rem(i, per_seq), 0),
    )
    state_spec = pl.BlockSpec((1, pairs * PAIR, 2 * PAIR), lambda i, *_: (i // per_seq, 0, 0))
    state_rows = block // SUB * pairs * PAIR
    sources, source_specs, ways = row_sources((own, other), block, per_seq, lambda i: i)
    outs = row_outs(block, model, blocks, len(own) if split_rows(own) else 1, lambda i: i)
    return when.call(
        partial(forward_kernel, count, per_seq, part * length, (ways, len(outs))),
        [starts, index],
        [*sources, *weights, dct, cosine, sine, state_in],
        source_specs
            + [whole_spec(w) for w in (*weights, dct)]
            + [table, table, state_spec],
        [
                by_rows(model),
                by_rows(3 * width),
                by_rows(width + hidden),
                by_rows(width),
                by_rows(hidden),
                pl.BlockSpec((state_rows, 2 * PAIR), lambda i, *_: (i, 0)),
                state_spec,
                *outs,
            ],
        [
            jax.ShapeDtypeStruct((rows, model), bf16),
            jax.ShapeDtypeStruct((rows, 3 * width), bf16),
            jax.ShapeDtypeStruct((rows, width + hidden), bf16),
            jax.ShapeDtypeStruct((rows, width), bf16),
            jax.ShapeDtypeStruct((rows, hidden), bf16),
            jax.ShapeDtypeStruct((blocks * state_rows, 2 * PAIR), bf16),
            jax.ShapeDtypeStruct((seqs, pairs * PAIR, 2 * PAIR), f32),
            *[jax.ShapeDtypeStruct((rows // len(outs), model), bf16) for _ in outs],
        ],
        grid=(blocks,),
        scratch_shapes=[pltpu.VMEM((pairs * PAIR, 2 * PAIR), f32)],
        name="forward_layer",
    )


def backward_layer(
    when, own, other, starts, index, weights, dctt, cosine, sine, state_in, saved, part, parts, block
):
    wq, _, wu, _, wo = weights
    weights = (wq, wu, wo)
    model = wq.shape[0]
    seqs, count = starts.shape
    length = cosine.shape[0] // seqs // parts
    rows = length * seqs
    hidden = wu.shape[1]
    width = wo.shape[0] - hidden
    span = 3 * width + hidden
    pairs = width // PAIR
    per_seq = length // block
    blocks = per_seq * seqs
    by_rows = lambda cols: pl.BlockSpec((block, cols), lambda i, *_: (blocks - 1 - i, 0))

    def table_index(i, *_):
        at = blocks - 1 - i
        return (at // per_seq) * per_seq * parts + part * per_seq + lax.rem(at, per_seq), 0

    table = pl.BlockSpec((block, PAIR), table_index)
    state_spec = pl.BlockSpec(
        (1, pairs * PAIR, 2 * PAIR), lambda i, *_: ((blocks - 1 - i) // per_seq, 0, 0)
    )
    state_rows = block // SUB * pairs * PAIR
    back = lambda i: blocks - 1 - i
    sources, source_specs, ways = row_sources((own, other), block, per_seq, back)
    outs = row_outs(block, model, blocks, len(own) if split_rows(own) else 1, back)
    return when.call(
        partial(backward_kernel, count, per_seq, part * length, (ways, len(outs))),
        [starts, index],
        [*sources, *weights, dctt, cosine, sine, state_in, *saved],
        source_specs
            + [whole_spec(w) for w in (*weights, dctt)]
            + [
                table,
                table,
                state_spec,
                by_rows(3 * width),
                by_rows(width + hidden),
                by_rows(width),
                by_rows(hidden),
                pl.BlockSpec((state_rows, 2 * PAIR), lambda i, *_: (blocks - 1 - i, 0)),
            ],
        [
                by_rows(span),
                pl.BlockSpec((1, span), lambda i, *_: (0, 0)),
                state_spec,
                *outs,
            ],
        [
            jax.ShapeDtypeStruct((rows, span), bf16),
            jax.ShapeDtypeStruct((1, span), f32),
            jax.ShapeDtypeStruct((seqs, pairs * PAIR, 2 * PAIR), f32),
            *[jax.ShapeDtypeStruct((rows // len(outs), model), bf16) for _ in outs],
        ],
        grid=(blocks,),
        scratch_shapes=[
                pltpu.VMEM((pairs * PAIR, 2 * PAIR), f32),
                pltpu.VMEM((block, 2 * width), bf16),
                pltpu.VMEM((block, 2 * width), bf16),
                pltpu.VMEM((block, width), bf16),
            ],
        name="backward_layer",
    )


def out_weight_grad(when, cas, grads, index, length, block):
    parts = len(cas)
    per_side = length // block
    per_part = 2 * per_side
    steps = per_part * parts
    inner, model = cas[0].shape[1], grads[0][0][0].shape[1]
    rights, right_specs, ways = [], [], ()
    for p, pair in enumerate(grads):
        arrays, specs, count = row_sources(
            pair, block, per_side, lambda i, p=p: jnp.clip(i - p * per_part, 0, per_part - 1)
        )
        rights += arrays
        right_specs += specs
        ways += count
    return when.call(
        partial(out_weight_kernel, parts, steps, ways),
        [index],
        [*cas, *rights],
        [row_spec(block, inner, p * per_part, (p + 1) * per_part - 1) for p in range(parts)]
        + right_specs,
        [pl.BlockSpec((inner, model), lambda i, *_: (0, 0))],
        [jax.ShapeDtypeStruct((inner, model), bf16)],
        grid=(steps,),
        scratch_shapes=[pltpu.VMEM((inner, model), f32)],
        name="out_weight_grad",
    )


def in_weight_grad(when, xhs, dzs, db, columns, wq, wu, block, pieces):
    parts = len(xhs)
    per_part = xhs[0].shape[0] // block
    steps = per_part * parts
    model, span = xhs[0].shape[1], dzs[0].shape[1]
    rows_of = lambda cols: [
        row_spec(block, cols, p * per_part, (p + 1) * per_part - 1) for p in range(parts)
    ]
    per_piece = model // pieces
    return when.call(
        partial(in_weight_kernel, parts, steps, pieces),
        [],
        [*xhs, *dzs, db, columns, wq, wu],
        rows_of(model) + rows_of(span) + [whole_spec(a) for a in (db, columns, wq, wu)],
        [pl.BlockSpec((per_piece, span), lambda i, *_: (0, 0))] * pieces
        + [pl.BlockSpec((model, 128), lambda i, *_: (0, 0))],
        [jax.ShapeDtypeStruct((per_piece, span), bf16)] * pieces
        + [jax.ShapeDtypeStruct((model, 128), f32)],
        grid=(steps,),
        scratch_shapes=[pltpu.VMEM((model, span), f32)],
        name="in_weight_grad",
    )


def join_pair_kernel(keep0, got0, keep1, got1, mine, theirs):
    mine[...] = (keep0[...].astype(f32) + got0[...].astype(f32)).astype(bf16)
    theirs[...] = (keep1[...].astype(f32) + got1[...].astype(f32)).astype(bf16)


def end_forward_kernel(mine, got, base, dense_bias, down_bias, rows):
    biases = dense_bias[...].astype(f32) + down_bias[...].astype(f32)
    summed = mine[...].astype(f32) + got[...].astype(f32)
    rows[...] = (base[...].astype(f32) + (summed + biases)).astype(bf16)


def end_backward_kernel(mine, got, base, before, rows, low):
    normed_grad = mine[...].astype(f32) + got[...].astype(f32)
    rows_in = base[...].astype(f32)
    center = jnp.mean(rows_in, axis=-1, keepdims=True)
    shifted = rows_in - center
    spread = jnp.mean(shifted * shifted, axis=-1, keepdims=True)
    inverse = lax.rsqrt(spread + norm_eps)
    normal = shifted * inverse
    along = jnp.mean(normed_grad * normal, axis=-1, keepdims=True)
    level = jnp.mean(normed_grad, axis=-1, keepdims=True)
    total = before[...].astype(f32) + inverse * (normed_grad - level - normal * along)
    rows[...] = total
    low[...] = total.astype(bf16)


def fold_kernel(qkv_ref, up_ref, order_ref, columns_ref, ordered_ref, wq_ref, wu_ref):
    columns = columns_ref[...]
    ordered = dot(qkv_ref[...], order_ref[...])
    ordered_ref[...] = ordered.astype(bf16)
    wq_ref[...] = (columns[:, 0:1] * ordered).astype(bf16)
    wu_ref[...] = (columns[:, 1:2] * up_ref[...].astype(f32)).astype(bf16)


def fold_gains(when, qkv, up, order, columns):
    model, hidden = up.shape
    span = order.shape[1]
    rows = min(256, model)
    by_rows = lambda cols: pl.BlockSpec((rows, cols), lambda i, *_: (i, 0))
    return when.call(
        fold_kernel,
        [],
        [qkv, up, order, columns],
        [by_rows(qkv.shape[1]), by_rows(hidden), whole_spec(order), by_rows(columns.shape[1])],
        [by_rows(span), by_rows(span), by_rows(hidden)],
        [
            jax.ShapeDtypeStruct((model, span), bf16),
            jax.ShapeDtypeStruct((model, span), bf16),
            jax.ShapeDtypeStruct((model, hidden), bf16),
        ],
        grid=(model // rows,),
        name="fold_gains",
    )


def by_blocks(when, kernel, sets, small, types, name):
    rows, cols = sets[0][0].shape
    block = min(256, rows)
    spec = pl.BlockSpec((block, cols), lambda i, *_: (i, 0))
    each, made = len(sets[0]), len(types)

    def body(*refs):
        ins, outs = refs[: len(sets) * each + len(small)], refs[len(sets) * each + len(small) :]
        for j in range(len(sets)):
            kernel(
                *ins[j * each : (j + 1) * each],
                *ins[len(sets) * each :],
                *outs[j * made : (j + 1) * made],
            )

    results = when.call(
        body,
        [],
        [a for one in sets for a in one] + list(small),
        [spec] * (len(sets) * each) + [whole_spec(a) for a in small],
        [spec] * (len(sets) * made),
        [jax.ShapeDtypeStruct((rows, cols), t) for _ in sets for t in types],
        grid=(rows // block,),
        name=name,
    )
    return [results[j * made : (j + 1) * made] for j in range(len(sets))]


def join_halves(when, items):
    scalars, operands, specs, outs, shapes, count = [], [], [], [], [], []
    for j, (now, bit, got, after_bit) in enumerate(items):
        half, cols = got.shape
        block = half // 2
        scalars += [jnp.int32(0) if bit is None else bit, jnp.int32(0) if after_bit is None else after_bit]

        def chosen(g, table, j=j, split=after_bit is not None):
            return jnp.where(g == 0, table[2 * j + 1], 1 - table[2 * j + 1]) if split else g

        def now_index(g, table, j=j, chosen=chosen, whole=bit is not None):
            at = chosen(g, table)
            return (table[2 * j] * 2 + at if whole else at), 0

        def got_index(g, table, chosen=chosen):
            return chosen(g, table), 0

        operands += [now, got]
        specs += [pl.BlockSpec((block, cols), now_index), pl.BlockSpec((block, cols), got_index)]
        if after_bit is None:
            outs.append(pl.BlockSpec((block, cols), lambda g, table: (g, 0)))
            shapes.append(jax.ShapeDtypeStruct((half, cols), bf16))
            count.append(1)
        else:
            outs += [pl.BlockSpec((block, cols), lambda g, table: (0, 0))] * 2
            shapes += [jax.ShapeDtypeStruct((block, cols), bf16)] * 2
            count.append(2)

    def kernel(table_ref, *refs):
        ins, made = refs[: 2 * len(items)], refs[2 * len(items) :]
        step = pl.program_id(0)
        at = 0
        for j, outputs in enumerate(count):
            total = (ins[2 * j][...].astype(f32) + ins[2 * j + 1][...].astype(f32)).astype(bf16)
            if outputs == 1:
                made[at][...] = total
            else:
                for side in range(2):

                    @pl.when(step == side)
                    def _():
                        made[at + side][...] = total

            at += outputs

    results = when.call(
        kernel, [jnp.stack(scalars).astype(jnp.int32)], operands, specs, outs, shapes, grid=(2,), name="join_halves"
    )
    grouped, at = [], 0
    for outputs in count:
        grouped.append(results[at : at + outputs])
        at += outputs
    return grouped


def assemble(when, pieces, own):
    rows, cols = pieces[0].shape
    count = len(pieces)

    def kernel(own_ref, *refs):
        ins, out = refs[:count], refs[count]
        key = jnp.bitwise_xor(pl.program_id(0), own_ref[0])
        for m in range(count):

            @pl.when(key == m)
            def _():
                out[...] = ins[m][...]

    return when.call(
        kernel,
        [jnp.reshape(own, (1,)).astype(jnp.int32)],
        list(pieces),
        [whole_spec(p) for p in pieces],
        [pl.BlockSpec((rows, cols), lambda i, *_: (i, 0))],
        [jax.ShapeDtypeStruct((rows * count, cols), bf16)],
        grid=(count,),
        name="assemble",
    )[0]


def finish_sums(when, held, constants, emit, shapes, name):
    layers = len(held)
    owns, operands, places = [], [], []
    for l, arrays in enumerate(held):
        first = 0
        for pieces, own in arrays:
            for m, piece in enumerate(pieces):
                operands.append(piece)
                places.append((l, len(owns), m, first))
            owns.append(own)
            first += piece.shape[0] * len(pieces)
    cols = operands[0].shape[1]

    def kernel(own_ref, *refs):
        ins = refs[: len(operands)]
        fixed = refs[len(operands) : len(operands) + len(constants)]
        outs, rows_ref = refs[len(operands) + len(constants) : -1], refs[-1]
        step = pl.program_id(0)
        for ref, (l, j, m, start) in zip(ins, places):
            count = ref.shape[0]

            @pl.when(step == l)
            def _():
                place = start + jnp.bitwise_xor(own_ref[j], m) * count
                rows_ref[pl.ds(pl.multiple_of(place, 16), count), :] = ref[...]

        emit(rows_ref, fixed, outs)

    return when.call(
        kernel,
        [jnp.stack([jnp.asarray(o, jnp.int32) for o in owns])],
        operands + list(constants),
        [whole_spec(a) for a in operands + list(constants)],
        [pl.BlockSpec((1,) + shape, lambda i, *_: (i, 0, 0)) for shape in shapes],
        [jax.ShapeDtypeStruct((layers,) + shape, f32) for shape in shapes],
        grid=(layers,),
        scratch_shapes=[pltpu.VMEM((first, cols), bf16)],
        name=name,
    )


def swapped(array, axis, distance):
    size = lax.axis_size(axis)
    return lax.ppermute(array, axis, [(i, i ^ distance) for i in range(size)])


def distances(size):
    return [1 << b for b in range(size.bit_length() - 1)]


def bit_of(axis, distance):
    return (lax.axis_index(axis) // distance) % 2


def joined(array, axis, distance):
    partner = swapped(array, axis, distance)
    upper = bit_of(axis, distance) == 1
    return jnp.concatenate(
        [jnp.where(upper, partner, array), jnp.where(upper, array, partner)], axis=0
    )


def gather_inner(rows, inner):
    for distance in distances(inner):
        rows = joined(rows, "tensor", distance)
    return rows


def inner_source(rows, inner):
    if inner == 2:
        return (rows, swapped(rows, "tensor", 1))
    return (gather_inner(rows, inner), 0)


def reduce_start(partial_sums, inner, when):
    if len(partial_sums) == 4:
        keep0, send0, keep1, send1 = partial_sums
        when.before += [send0, send1]
        return [keep0, keep1], [swapped(send0, "tensor", 1), swapped(send1, "tensor", 1)]
    now = jnp.split(partial_sums[0], 2)
    for distance in reversed(distances(inner)):
        half = now[0].shape[0] // 2
        bit = bit_of("tensor", distance)
        keep = [lax.dynamic_slice_in_dim(one, bit * half, half, 0) for one in now]
        send = [lax.dynamic_slice_in_dim(one, (1 - bit) * half, half, 0) for one in now]
        got = [swapped(one, "tensor", distance) for one in send]
        if distance > 1:
            (now,) = reduce_join([(keep, got)], when)
    return keep, got


def reduce_join(pending, when):
    return by_blocks(
        when,
        join_pair_kernel,
        [[keep[0], got[0], keep[1], got[1]] for keep, got in pending],
        [],
        [bf16, bf16],
        "join_pair",
    )


def sum_over_dp(arrays, orders, when, whole=False):
    nows, gots, wholes = list(arrays), [], []
    for array, order in zip(arrays, orders):
        half = array.shape[0] // 2
        bit = bit_of("dp", order[0])
        send = lax.dynamic_slice_in_dim(array, (1 - bit) * half, half, 0)
        when.before.append(send)
        gots.append(swapped(send, "dp", order[0]))
        wholes.append(bit)
    yield
    for stage in range(1, len(orders[0])):
        halving = stage < len(orders[0]) - 1
        items = [
            (now, whole, got, bit_of("dp", order[stage]) if halving else None)
            for now, whole, got, order in zip(nows, wholes, gots, orders)
        ]
        made = join_halves(when, items)
        nows = [one[0] for one in made]
        gots = [swapped(one[-1], "dp", order[stage]) for one, order in zip(made, orders)]
        wholes = [None] * len(nows)
        yield
    items = [(now, None, got, None) for now, got in zip(nows, gots)]
    nows = [one[0] for one in join_halves(when, items)]
    held = []
    for now, order in zip(nows, orders):
        pieces = {0: now}
        kept = order[:-1]
        for j in reversed(range(len(kept))):
            key = 1 << (len(kept) - 1 - j)
            pieces.update(
                {m | key: swapped(p, "dp", kept[j]) for m, p in list(pieces.items())}
            )
        held.append(pieces)
    yield
    results = []
    for pieces, order in zip(held, orders):
        kept = order[:-1]
        own = sum(bit_of("dp", d) * (1 << (len(kept) - 1 - j)) for j, d in enumerate(kept))
        pieces = [pieces[m] for m in range(len(pieces))]
        if whole:
            pieces, own = [assemble(when, pieces, own)], 0
        results.append((pieces, own))
    return results


class Sum:
    def __init__(self, arrays, orders, when, whole=False):
        self.run = sum_over_dp(arrays, orders, when, whole)
        self.value = None
        self.step()

    def step(self):
        if self.value is None:
            try:
                next(self.run)
            except StopIteration as stop:
                self.value = stop.value

    def finish(self):
        while self.value is None:
            self.step()
        return self.value


def small_sum(array, axes):
    for axis in axes:
        for distance in distances(lax.axis_size(axis)):
            array = array + swapped(array, axis, distance)
    return array


def to_shares(rows, inner, parts):
    half = rows.shape[0] // 2
    if inner == 2 and parts == 2:
        upper = bit_of("tensor", 1)
        send = lax.dynamic_slice_in_dim(rows, (1 - upper) * half, half, 0)
        got = swapped(send, "tensor", 1)
        return [jnp.where(upper == 1, got, rows[:half]), jnp.where(upper == 1, rows[half:], got)]
    whole = gather_inner(rows, inner)
    part_rows = whole.shape[0] // parts
    share = part_rows // inner
    first = lax.rem(lax.axis_index("tensor"), inner) * share
    return [
        lax.dynamic_slice_in_dim(whole, part * part_rows + first, share, 0)
        for part in range(parts)
    ]


def to_placement(shares, inner):
    parts = len(shares)
    if inner == 2 and parts == 2:
        upper = bit_of("tensor", 1) == 1
        mine = jnp.where(upper, shares[1], shares[0])
        theirs = jnp.where(upper, shares[0], shares[1])
        got = swapped(theirs, "tensor", 1)
        return jnp.concatenate([jnp.where(upper, got, mine), jnp.where(upper, mine, got)], axis=0)
    whole = jnp.concatenate([gather_inner(rows, inner) for rows in shares], axis=0)
    rows = whole.shape[0] // inner
    index = lax.rem(lax.axis_index("tensor"), inner)
    return lax.dynamic_slice_in_dim(whole, index * rows, rows, 0)


def on_device(
    tokens,
    doc_starts,
    norm_gains,
    norm_shifts,
    qkv_weight,
    qkv_bias,
    dense_weight,
    dense_bias,
    up_weight,
    up_bias,
    down_weight,
    down_bias,
    out_grad,
):
    layers = qkv_weight.shape[0]
    seqs = doc_starts.shape[0]
    model = tokens.shape[1]
    size = lax.axis_size("tensor")
    inner = size // seqs
    index = lax.axis_index("tensor")
    inner_index = lax.rem(index, inner)
    length = tokens.shape[0] * inner
    heads = qkv_weight.shape[2] // (3 * HS)
    padded = heads + heads % 2
    width = padded * HS
    group = 2 * PAIR if padded % 4 == 0 else PAIR
    parts = PARTS
    part_rows = length // parts
    share = part_rows // inner
    block = share if inner == 2 else min(512, part_rows)
    per_part = part_rows // block
    dp_size = lax.axis_size("dp")
    early_x = distances(dp_size)
    late_x = early_x[1:] + early_x[:1]

    when = Order()
    order = jnp.asarray(column_order(heads), bf16)
    feature = feature_matrix(group)
    dct = jnp.asarray(feature, bf16)
    dctt = jnp.asarray(feature.T, bf16)
    starts = jnp.where(index < inner, doc_starts, doc_starts[::-1])
    cosine, sine = rotary_tables(starts, length)
    zero_state = jnp.zeros((seqs, padded // 2 * PAIR, 2 * PAIR), f32)
    gains = norm_gains.astype(f32)
    shifts = norm_shifts.astype(f32)

    last = layers - 1
    place = jnp.full((1,), inner_index, jnp.int32)

    xs = to_shares(tokens, inner, parts)
    columns = [
        jnp.stack([gains[l, 0], gains[l, 1], shifts[l, 0], shifts[l, 1]], axis=1)
        for l in range(layers)
    ]

    def fold(l):
        qkv, up, dense, down = qkv_weight[l], up_weight[l], dense_weight[l], down_weight[l]
        ordered, wq, wu = fold_gains(when, qkv, up, order, columns[l])
        bias_one = dot(norm_shifts[l, 0:1], qkv) + qkv_bias[l].astype(f32)[None]
        bq = jnp.dot(bias_one, order.astype(f32), precision=lax.Precision.HIGHEST)
        bu = dot(norm_shifts[l, 1:2], up) + up_bias[l].astype(f32)[None]
        if padded != heads:
            dense = jnp.concatenate([dense, jnp.zeros((width - heads * HS, model), bf16)], axis=0)
        wo = jnp.concatenate([dense, down], axis=0)
        return (wq, bq, wu, bu, wo), ordered

    folded = [None] * layers
    when.before += [cosine, sine, *xs]
    folded[0] = fold(0)
    crossing_x = [swapped(xs[0], "tensor", inner), None]
    x_parts = [None] * parts
    x_parts[0] = (
        inner_source(xs[0], inner),
        inner_source(when.after(crossing_x[0]), inner),
    )
    when.mark(crossing_x[0])
    sent = when.after(xs[1])
    crossing_x[1] = swapped(sent, "tensor", inner)
    when.before.append(sent)

    inputs = [None] * layers
    saved = [[None] * parts for _ in range(layers)]
    sums = [[None] * parts for _ in range(layers)]

    def run_forward(l, part, state):
        own, other = x_parts[part]
        xh, qkv, ca, rden, gp, states, state, *out = forward_layer(
            when, own, other, starts, place, folded[l][0], dct, cosine, sine, state, part, parts, block
        )
        saved[l][part] = (xh, qkv, ca, rden, gp, states)
        sums[l][part] = out
        return state

    def begin_reduce(partial_sum):
        return reduce_start(partial_sum, inner, when)

    def cross_reduce(*pending):
        crossings = [
            (mine, swapped(theirs, "tensor", inner)) for mine, theirs in reduce_join(pending, when)
        ]
        return crossings if len(crossings) > 1 else crossings[0]

    def end_forward(l, ends):
        made = by_blocks(
            when,
            end_forward_kernel,
            [[*crossing, inputs[l][part]] for part, crossing in ends],
            [dense_bias[l : l + 1], down_bias[l : l + 1]],
            [bf16],
            "end_forward",
        )
        return [one[0] for one in made]

    def end_backward(l, ends):
        return by_blocks(
            when,
            end_backward_kernel,
            [[*crossing, inputs[l][part], incoming[part]] for part, crossing in ends],
            [],
            [f32, bf16],
            "end_backward",
        )

    def whole_part(share_rows, crossing):
        return inner_source(share_rows, inner), inner_source(when.after(crossing), inner)

    def send_across(rows):
        when.before.append(rows)
        return swapped(rows, "tensor", inner)

    out_grad_shares = to_shares(out_grad, inner, parts)
    incoming = out_grad_shares
    grads = [None] * parts
    crossing_grad = [None] * parts

    def send_out_grad(part):
        crossing_grad[part] = send_across(when.after(out_grad_shares[part]))

    for l in range(layers):
        inputs[l] = xs
        state = run_forward(l, 0, zero_state)
        if l < last:
            pending = begin_reduce(sums[l][0])
            if l == 0:
                x_parts[1] = whole_part(xs[1], crossing_x[1])
            crossing0 = cross_reduce(pending)
            state = run_forward(l, 1, state)
            pending = begin_reduce(sums[l][1])
            (x0,) = end_forward(l, [(0, crossing0)])
            far0 = send_across(x0)
            crossing1 = cross_reduce(pending)
            folded[l + 1] = fold(l + 1)
            x_parts = [whole_part(x0, far0), None]
            (x1,) = end_forward(l, [(1, crossing1)])
            far1 = send_across(x1)
            xs = [x0, x1]
        else:
            x_parts[1] = whole_part(xs[1], far1)
            send_out_grad(1)
            state = run_forward(l, 1, state)
            grads[1] = whole_part(out_grad_shares[1], crossing_grad[1])
            send_out_grad(0)

    small = [None] * layers
    weight_sums = [None] * layers

    def run_backward(l, part, state):
        own, other = grads[part]
        xh, qkv, ca, rden, gp, states = saved[l][part]
        kept = (qkv, ca, rden, gp, states)
        dz, db, state, *dx = backward_layer(
            when,
            own,
            other,
            starts,
            place,
            folded[l][0],
            dctt,
            cosine,
            sine,
            state,
            kept,
            part,
            parts,
            block,
        )
        return dz, dx, db, state

    def out_weights(l):
        return out_weight_grad(
            when, [kept[2] for kept in saved[l]], grads, place, part_rows, block
        )[0]

    def in_weights(l, dzs, dbs, bias_grad, pieces):
        db = sum(dbs)
        *made, norm_sums = in_weight_grad(
            when,
            [kept[0] for kept in saved[l]],
            dzs,
            db,
            columns[l],
            folded[l][1],
            up_weight[l],
            block,
            pieces,
        )
        small[l] = (jnp.concatenate([norm_sums[:, :4].T, bias_grad], axis=0), db)
        return made

    running = []

    def advance():
        for one in running:
            one.step()

    def bias_sum():
        return sum(
            jnp.sum(rows.astype(bf16).astype(f32), axis=0, keepdims=True) for rows in incoming
        )

    for l in reversed(range(layers)):
        bias_grad = bias_sum()
        dz1, dx1, db1, state = run_backward(l, 1, zero_state)
        if l == last:
            grads[0] = whole_part(out_grad_shares[0], crossing_grad[0])
        else:
            grads[0] = whole_part(far0[0], far0[1])
        if l > 0:
            pending1 = begin_reduce(dx1)
            out_sum = Sum([out_weights(l)], [early_x], when, True)
            running.append(out_sum)
            crossing1 = cross_reduce(pending1)
            dz0, dx0, db0, state = run_backward(l, 0, state)
            ((g1, low1),) = end_backward(l, [(1, crossing1)])
            far1 = send_across(low1)
            pending0 = begin_reduce(dx0)
            advance()
            crossing0 = cross_reduce(pending0)
            made = in_weights(l, [dz0, dz1], [db0, db1], bias_grad, 1)
            advance()
            grads = [None, whole_part(low1, far1)]
            in_sum = Sum(made, [early_x], when, True)
            running.append(in_sum)
            weight_sums[l] = (out_sum, in_sum)
            ((g0, low0),) = end_backward(l, [(0, crossing0)])
            far0 = (low0, send_across(low0))
            incoming = [g0, g1]
        else:
            advance()
            out_sum = Sum([out_weights(l)], [early_x], when)
            advance()
            running.append(out_sum)
            dz0, dx0, db0, state = run_backward(l, 0, state)
            advance()
            made = in_weights(l, [dz0, dz1], [db0, db1], bias_grad, 2)
            final = Sum(made, [early_x, late_x], when)
            weight_sums[l] = (out_sum, final)

    norm_rows = jnp.concatenate([one[0] for one in small], axis=0)
    span = small[0][1].shape[1]
    norm_rows = jnp.pad(norm_rows, ((0, 0), (0, max(span - model, 0))))
    bias_rows = jnp.concatenate([one[1] for one in small], axis=0)
    bias_rows = jnp.pad(bias_rows, ((0, 0), (0, max(model - span, 0))))
    small_rows = jnp.concatenate([norm_rows, bias_rows], axis=0)
    small_exchanges = [("dp", d) for d in distances(dp_size)]
    small_exchanges += [("tensor", d) for d in distances(size)]

    def small_steps(rows):
        for axis, distance in small_exchanges:
            sent = when.after(rows)
            when.before.append(sent)
            got = swapped(sent, axis, distance)
            yield
            summed = when.after(rows + got)
            if axis == "tensor":
                summed = jnp.concatenate([summed[: 5 * layers], rows[5 * layers :]], axis=0)
            rows = summed
        yield rows

    small_run = small_steps(small_rows)

    pending = [begin_reduce(one) for one in (dx0, dx1)]
    advance()
    crossing = cross_reduce(*pending)
    next(small_run)
    final.step()
    next(small_run)
    pending = [begin_reduce(one) for one in sums[last]]
    out_crossing = cross_reduce(*pending)
    final.step()
    advance()
    next(small_run)
    incoming = [one[0] for one in end_backward(0, list(enumerate(crossing)))]
    tokens_grad = to_placement(incoming, inner)
    advance()
    final.step()
    next(small_run)
    results = end_forward(last, list(enumerate(out_crossing)))
    result = to_placement(results, inner)
    while any(one.value is None for one in running):
        advance()
    for small_rows in small_run:
        pass
    def emit_out(rows_ref, fixed, outs):
        outs[0][0] = rows_ref[: heads * HS, :].astype(f32)
        outs[1][0] = rows_ref[width:, :].astype(f32)

    def emit_in(rows_ref, fixed, outs):
        outs[0][0] = dot_nt(rows_ref[:, : 3 * width], fixed[0][...])
        outs[1][0] = rows_ref[:, 3 * width :].astype(f32)

    hidden_size = up_weight.shape[2]
    when.before.append(tokens_grad)
    dense_total, down_total = finish_sums(
        when,
        [sums_of[0].finish() for sums_of in weight_sums],
        [],
        emit_out,
        [(heads * HS, model), (hidden_size, model)],
        "finish_out",
    )
    when.before.append(result)
    qkv_total, up_total = finish_sums(
        when,
        [sums_of[1].finish() for sums_of in weight_sums],
        [order],
        emit_in,
        [(model, heads * 3 * HS), (model, hidden_size)],
        "finish_in",
    )
    bias_rows = small_rows[5 * layers :, :span]
    norm_rows = small_rows[: 5 * layers, :model].reshape(layers, 5, model)

    bias_total = norm_rows[:, 4]
    bias_one = bias_rows[:, : 3 * width]
    return (
        result,
        tokens_grad,
        norm_rows[:, 0:2],
        norm_rows[:, 2:4],
        qkv_total,
        jnp.dot(bias_one, order.astype(f32).T, precision=lax.Precision.HIGHEST),
        dense_total,
        bias_total,
        up_total,
        bias_rows[:, 3 * width :],
        down_total,
        bias_total,
    )


def solution(mesh):
    return jax.shard_map(
        on_device,
        mesh=mesh,
        in_specs=(
            P(("dp", "tensor"), None),
            P("dp", None),
            P(),
            P(),
            P(None, None, "tensor"),
            P(None, "tensor"),
            P(None, "tensor", None),
            P(),
            P(None, None, "tensor"),
            P(None, "tensor"),
            P(None, "tensor", None),
            P(),
            P(("dp", "tensor"), None),
        ),
        out_specs=(
            P(("dp", "tensor"), None),
            P(("dp", "tensor"), None),
            P(),
            P(),
            P(None, None, "tensor"),
            P(None, "tensor"),
            P(None, "tensor", None),
            P(),
            P(None, None, "tensor"),
            P(None, "tensor"),
            P(None, "tensor", None),
            P(),
        ),
        check_vma=False,
    )
```
